32 devices in a mesh: elev: 8 (over z, core), valley: 2 (over y), down: 2 (over x).
Axes of the slice: x: 2, y: 2, z: 4, core: 2. Of those that a mesh axis runs over, the one named last changes fastest.
Arguments:
- resid: bfloat16 [8, 8, 4, 128, 256], P('elev', 'valley', 'down'), may hold values from -6 to 6
- direction: bfloat16 [8, 8, 4, 128, 256], P('elev', 'valley', 'down'), may hold values from -6 to 6
- diag_blocks: bfloat16 [8, 8, 4, 256, 256], P('elev', 'valley', 'down'), may hold values from -0.375 to 0.375
- lower_blocks: bfloat16 [8, 8, 4, 256, 256], P('elev', 'valley', 'down')
- upper_blocks: bfloat16 [8, 8, 4, 256, 256], P('elev', 'valley', 'down')
- inv_pivots: bfloat16 [8, 8, 4, 256, 256], P('elev', 'valley', 'down')
- down_coupling: bfloat16 [8, 8, 4, 256, 256], P('elev', 'valley', 'down'), may hold values from -0.375 to 0.375
- valley_coupling: bfloat16 [8, 8, 4, 256, 256], P('elev', 'valley', 'down'), may hold values from -0.375 to 0.375
- coupled_column: int32 [8, 8, 4], P('elev', 'valley', 'down'), may hold values from 0 to 7
Outputs:
- preconditioned: bfloat16 [8, 8, 4, 128, 256], P('elev', 'valley', 'down')
- image: float32 [8, 8, 4, 128, 256], P('elev', 'valley', 'down')
The draws below stay inside these ranges and needn't reach their ends.
All inputs are finite; a program needn't handle non-finite values.
Results may differ from the reference program's by a relative error of at most 0.015.
Values may be sent and summed in bfloat16 or wider, within the bound.
No kernel may reach another device: no remote copies, remote signals or barrier semaphores. Data moves between devices by JAX's collectives and lax.ppermute only.
A program may use at most 64 MiB of HBM per device.

```python
import math
import jax
import jax.numpy as jnp

BS = 256
NR = 128
NLAY = 8
VBLK = 8
DBLK = 4


def decay_blocks(key):
    pick_key, slow_key, fast_key, noise_key = jax.random.split(key, 4)
    shape = (NLAY, VBLK, DBLK, BS)
    share = 0.5
    picked = jax.random.uniform(pick_key, shape, jnp.float32)
    slow = jax.random.uniform(slow_key, shape, jnp.float32, 0.86, 0.93)
    fast = jax.random.uniform(fast_key, shape, jnp.float32, 0.15, 0.6)
    rates = jnp.where(picked < share, slow, fast)
    noise = jax.random.normal(noise_key, shape + (BS,), jnp.float32) * (0.2 / math.sqrt(BS))
    return (-(rates[..., None] * jnp.eye(BS, dtype=jnp.float32) + noise)).astype(jnp.bfloat16)


def draw_lower_blocks(key, part):
    return decay_blocks(jax.random.fold_in(key, 11))


def draw_upper_blocks(key, part):
    return decay_blocks(jax.random.fold_in(key, 12))


def draw_inv_pivots(key, part):
    noise_key = jax.random.fold_in(key, 13)
    noise = jax.random.normal(noise_key, (NLAY, VBLK, DBLK, BS, BS), jnp.float32) * (0.2 / math.sqrt(BS))
    return (noise + jnp.eye(BS, dtype=jnp.float32)).astype(jnp.bfloat16)


def plant(array, key, smallest, high):
    longest = array.shape.index(max(array.shape))
    spots = []
    for shift in (0, 1):
        where = [jax.random.randint(jax.random.fold_in(key, axis), (), 0, length) for axis, length in enumerate(array.shape)]
        where[longest] = (where[longest] + shift) % array.shape[longest]
        spots.append(tuple(where))
    return array.at[spots[0]].set(smallest).at[spots[1]].set(high)


def shard_levels(stream_key, shape, cuts, low, high):
    def one(dim, shards_of):
        heights = jax.random.uniform(jax.random.fold_in(jax.random.fold_in(stream_key, 6), dim), (shards_of,), jnp.float32, low / len(cuts), high / len(cuts))
        return jnp.repeat(jnp.exp(heights), shape[dim] // shards_of).reshape((-1,) + (1,) * (len(shape) - dim - 1))

    level = one(*cuts[0])
    for cut in cuts[1:]:
        level = level * one(*cut)
    return level


def gaussian(rng, dims, width, most, pieces=(), held_as=jnp.bfloat16):
    values = width * jax.random.normal(rng, dims, jnp.float32)
    if pieces:
        values = values * shard_levels(rng, dims, pieces, -0.22, 0.18)
    return jnp.clip(values, -most, most).astype(held_as)


def setup_inputs(seed: int = 0) -> dict:
    streams_of = jax.random.split(jax.random.key(seed), 10)
    return {
        "resid": gaussian(streams_of[0], (NLAY, VBLK, DBLK, NR, BS), 1.0, 6.0, ((0, 8), (1, 2), (2, 2))),
        "direction": gaussian(streams_of[1], (NLAY, VBLK, DBLK, NR, BS), 1.0, 6.0, ((0, 8), (1, 2), (2, 2))),
        "diag_blocks": gaussian(streams_of[2], (NLAY, VBLK, DBLK, BS, BS), BS ** -0.5, 0.375, ((0, 8), (1, 2), (2, 2))),
        "lower_blocks": draw_lower_blocks(jax.random.fold_in(streams_of[9], 71), 0),
        "upper_blocks": draw_upper_blocks(jax.random.fold_in(streams_of[9], 71), 0),
        "inv_pivots": draw_inv_pivots(jax.random.fold_in(streams_of[9], 71), 0),
        "down_coupling": gaussian(streams_of[6], (NLAY, VBLK, DBLK, BS, BS), BS ** -0.5, 0.375, ((0, 8), (1, 2), (2, 2))),
        "valley_coupling": gaussian(streams_of[7], (NLAY, VBLK, DBLK, BS, BS), BS ** -0.5, 0.375, ((0, 8), (1, 2), (2, 2))),
        "coupled_column": plant(jax.random.randint(streams_of[8], (NLAY, VBLK, DBLK), 0, VBLK), jax.random.fold_in(streams_of[8], 1), 0, VBLK - 1).astype(jnp.int32),
    }


def product(vectors, blocks):
    return jnp.einsum('...rs,...st->...rt', vectors.astype(jnp.float32), blocks.astype(jnp.float32))


def reference(resid, direction, diag_blocks, lower_blocks, upper_blocks, inv_pivots, down_coupling, valley_coupling, coupled_column):
    layer_count = resid.shape[0]
    empty_front = jnp.zeros(resid.shape[1:], jnp.bfloat16)
    front = empty_front
    fronts = []
    for height in range(layer_count):
        inner = (resid[height].astype(jnp.float32) - product(front, lower_blocks[height])).astype(jnp.bfloat16)
        front = product(inner, inv_pivots[height]).astype(jnp.bfloat16)
        fronts.append(front)
    solved = [None] * layer_count
    above = empty_front
    for height in range(layer_count - 1, -1, -1):
        carried = product(above, upper_blocks[height]).astype(jnp.bfloat16)
        above = (fronts[height].astype(jnp.float32) - product(carried, inv_pivots[height])).astype(jnp.bfloat16)
        solved[height] = above
    preconditioned = jnp.stack(solved)
    down_index = jnp.arange(resid.shape[2], dtype=jnp.int32)[None, :]
    images = []
    for height in range(layer_count):
        current = direction[height]
        below_dir = direction[height - 1] if height > 0 else empty_front
        above_dir = direction[height + 1] if height + 1 < layer_count else empty_front
        upstream = jnp.concatenate([empty_front[:, :1], current[:, :-1]], axis=1)
        partner = current[coupled_column[height], down_index]
        total = product(current, diag_blocks[height])
        total = total + product(below_dir, lower_blocks[height])
        total = total + product(above_dir, upper_blocks[height])
        total = total + product(upstream, down_coupling[height])
        total = total + product(partner, valley_coupling[height])
        images.append(total)
    return preconditioned, jnp.stack(images)
```

```python
import functools

import jax
import jax.numpy as jnp
from jax import lax
from jax.experimental import pallas as pl
from jax.experimental.pallas import tpu as pltpu
from jax.sharding import PartitionSpec as P

BF16 = jnp.bfloat16
F32 = jnp.float32
VMEM = pltpu.MemorySpace.VMEM
GROUPS = 2


def dot(x, y):
    return jnp.dot(x, y, preferred_element_type=F32)


def call(kernel, outs, *operands, products=1):
    spec = pl.BlockSpec(memory_space=pltpu.VMEM)
    held = [pltpu.with_memory_space_constraint(x, VMEM) for x in operands]
    result = pl.pallas_call(
        kernel,
        out_shape=[VMEM(shape, dtype) for shape, dtype in outs],
        in_specs=[spec] * len(held),
        out_specs=[spec] * len(outs),
        compiler_params=pltpu.CompilerParams(vmem_limit_bytes=8 << 20),
        cost_estimate=pl.CostEstimate(
            flops=products * 2 * 128 * 256 * 256, bytes_accessed=1 << 18, transcendentals=0
        ),
    )(*held)
    return result


def place():
    height = lax.axis_index("elev")
    return height // 2, lax.rem(height, 2)


def swap_cores(value):
    count = lax.axis_size("elev")
    return lax.ppermute(value, "elev", [(i, i ^ 1) for i in range(count)])


def swap_chips(value, low):
    pairs = []
    for i in range(lax.axis_size("elev")):
        chip = i // 2
        pairs.append((i, i + 2 if chip == low else i - 2 if chip == low + 1 else i ^ 1))
    return lax.ppermute(value, "elev", pairs)


def local(
    resid,
    direction,
    diag_blocks,
    lower_blocks,
    upper_blocks,
    inv_pivots,
    down_coupling,
    valley_coupling,
    coupled_column,
):
    _, valleys, downs, rows, size = resid.shape
    chains = valleys * downs
    half = chains // 2
    groups = GROUPS
    width = half // groups
    chips = lax.axis_size("elev") // 2
    vectors = lambda x: x.reshape(chains, rows, size)
    blocks = lambda x: x.reshape(chains, size, size)
    rhs, current = vectors(resid), vectors(direction)
    lower, upper, pivot = blocks(lower_blocks), blocks(upper_blocks), blocks(inv_pivots)

    elev = lax.axis_size("elev")
    beside = swap_cores(current)
    across = lax.ppermute(
        current,
        "elev",
        [(i, i + 1) for i in range(1, elev - 1, 2)] + [(i + 1, i) for i in range(1, elev - 1, 2)],
    )

    def first(l_ref, p_ref, r_ref, keep_ref, send_ref):
        _, core = place()
        for i in range(half):
            for ref, base in ((send_ref, (1 - core) * half), (keep_ref, core * half)):
                block = p_ref[base + i]
                ref[i, :size] = (-dot(l_ref[base + i], block)).astype(BF16)
                ref[i, size:] = dot(r_ref[base + i], block).astype(BF16)

    packed = ((half, size + rows, size), BF16)
    keep1, send1 = call(first, [packed, packed], lower, pivot, rhs, products=3 * chains)
    recv1 = swap_cores(send1)

    def second(u_ref, p_ref, keep_ref, send_ref):
        _, core = place()
        for i in range(half):
            for ref, base in ((send_ref, (1 - core) * half), (keep_ref, core * half)):
                ref[i] = (-dot(u_ref[base + i], p_ref[base + i])).astype(BF16)

    square = ((half, size, size), BF16)
    keep2, send2 = call(second, [square, square], upper, pivot, products=2 * chains)

    def begin(keep_ref, recv_ref, start_ref):
        _, core = place()

        def write(bottom, top):
            for i in range(half):
                start_ref[i] = (
                    top[i, size:].astype(F32) + dot(bottom[i, size:], top[i, :size])
                ).astype(BF16)

        pl.when(core == 0)(lambda: write(keep_ref, recv_ref))
        pl.when(core == 1)(lambda: write(recv_ref, keep_ref))

    (start,) = call(begin, [((half, rows, size), BF16)], keep1, recv1, products=half)

    def join(keep_ref, recv_ref, through_ref):
        _, core = place()

        def write(bottom, top):
            for i in range(half):
                through_ref[i] = dot(bottom[i, :size], top[i, :size]).astype(BF16)

        pl.when(core == 0)(lambda: write(keep_ref, recv_ref))
        pl.when(core == 1)(lambda: write(recv_ref, keep_ref))

    (through,) = call(join, [square], keep1, recv1, products=2 * half)
    recv2 = swap_cores(send2)

    def back(keep_ref, recv_ref, back_ref):
        _, core = place()

        def write(bottom, top):
            for i in range(half):
                back_ref[i] = dot(top[i], bottom[i]).astype(BF16)

        pl.when(core == 0)(lambda: write(keep_ref, recv_ref))
        pl.when(core == 1)(lambda: write(recv_ref, keep_ref))

    (backward,) = call(back, [square], keep2, recv2, products=2 * half)

    message = ((width, rows, size), BF16)
    spans = [slice(g * width, (g + 1) * width) for g in range(groups)]

    def advance(span, low, in_ref, start_ref, through_ref, out_ref):
        chip, _ = place()
        at = span.start

        def step():
            for i in range(width):
                out_ref[i] = (
                    start_ref[at + i].astype(F32) + dot(in_ref[i], through_ref[at + i])
                ).astype(BF16)

        def idle():
            out_ref[...] = in_ref[...]

        pl.when(chip == low)(step)
        pl.when(chip != low)(idle)

    fronts = [start[span] for span in spans]
    heard = [[] for _ in spans]
    for low in range(chips - 1):
        for g, span in enumerate(spans):
            arrived = swap_chips(fronts[g], low)
            heard[g].append(arrived)
            if low < chips - 2:
                (fronts[g],) = call(
                    functools.partial(advance, span, low + 1),
                    [message],
                    arrived,
                    start,
                    through,
                    products=width,
                )

    def turn(span, *refs):
        heard_refs = refs[: chips - 1]
        start_ref, through_ref, keep1_ref, recv1_ref, keep2_ref, recv2_ref = refs[chips - 1 : -3]
        top_ref, base_ref, in_ref = refs[-3:]
        chip, core = place()
        at = span.start

        @pl.when(chip == 0)
        def _():
            in_ref[...] = jnp.zeros_like(in_ref)

        for low in range(chips - 1):

            @pl.when(chip == low + 1)
            def _():
                in_ref[...] = heard_refs[low][...]

        def write(first_ref, second_ref):
            for i in range(width):
                arrived = in_ref[i]
                top = (
                    start_ref[at + i].astype(F32) + dot(arrived, through_ref[at + i])
                ).astype(BF16)
                low = first_ref[at + i, size:].astype(F32) + dot(arrived, first_ref[at + i, :size])
                top_ref[i] = top
                base_ref[i] = (
                    low.astype(BF16).astype(F32) + dot(top, second_ref[at + i])
                ).astype(BF16)

        pl.when(core == 0)(lambda: write(keep1_ref, keep2_ref))
        pl.when(core == 1)(lambda: write(recv1_ref, recv2_ref))

    tops, bases = [], []
    for g, span in enumerate(spans):
        top, base, _ = call(
            functools.partial(turn, span),
            [message] * 3,
            *heard[g],
            start,
            through,
            keep1,
            recv1,
            keep2,
            recv2,
            products=3 * width,
        )
        tops.append(top)
        bases.append(base)

    def retreat(span, low, in_ref, base_ref, back_ref, out_ref):
        chip, _ = place()
        at = span.start

        def step():
            for i in range(width):
                out_ref[i] = (
                    base_ref[i].astype(F32) + dot(in_ref[i], back_ref[at + i])
                ).astype(BF16)

        def idle():
            out_ref[...] = in_ref[...]

        pl.when(chip == low)(step)
        pl.when(chip != low)(idle)

    solved = list(bases)
    heard = [[] for _ in spans]
    for low in range(chips - 2, -1, -1):
        for g, span in enumerate(spans):
            arrived = swap_chips(solved[g], low)
            heard[g].insert(0, arrived)
            if low > 0:
                (solved[g],) = call(
                    functools.partial(retreat, span, low),
                    [message],
                    arrived,
                    bases[g],
                    backward,
                    products=width,
                )

    def finish(span, *refs):
        heard_refs = refs[: chips - 1]
        top_ref, base_ref, back_ref, keep2_ref, recv2_ref = refs[chips - 1 : -3]
        keep_ref, send_ref, in_ref = refs[-3:]
        chip, core = place()
        at = span.start

        @pl.when(chip == chips - 1)
        def _():
            in_ref[...] = jnp.zeros_like(in_ref)

        for low in range(chips - 1):

            @pl.when(chip == low)
            def _():
                in_ref[...] = heard_refs[low][...]

        def write(top_block, bottom_out, top_out):
            for i in range(width):
                arrived = in_ref[i]
                bottom_out[i] = (
                    base_ref[i].astype(F32) + dot(arrived, back_ref[at + i])
                ).astype(BF16)
                top_out[i] = (
                    top_ref[i].astype(F32) + dot(arrived, top_block[at + i])
                ).astype(BF16)

        pl.when(core == 0)(lambda: write(recv2_ref, keep_ref, send_ref))
        pl.when(core == 1)(lambda: write(keep2_ref, send_ref, keep_ref))

    kept, given = [], []
    for g, span in enumerate(spans):
        keep, send, _ = call(
            functools.partial(finish, span),
            [message] * 3,
            *heard[g],
            tops[g],
            bases[g],
            backward,
            keep2,
            recv2,
            products=2 * width,
        )
        kept.append(keep)
        given.append(swap_cores(send))

    def gather(*refs):
        kept_refs, given_refs, out_ref, sems = refs[:groups], refs[groups:-2], refs[-2], refs[-1]
        _, core = place()
        copies = []
        for g in range(groups):
            for which, (ref, side) in enumerate(((kept_refs[g], core), (given_refs[g], 1 - core))):
                copies.append(
                    pltpu.make_async_copy(
                        ref,
                        out_ref.at[pl.ds(side * half + g * width, width)],
                        sems.at[2 * g + which],
                    )
                )
        for copy in copies:
            copy.start()
        for copy in copies:
            copy.wait()

    spec = pl.BlockSpec(memory_space=pltpu.VMEM)
    parts = [pltpu.with_memory_space_constraint(x, VMEM) for x in kept + given]
    preconditioned = pl.pallas_call(
        gather,
        out_shape=jax.ShapeDtypeStruct((chains, rows, size), BF16),
        in_specs=[spec] * len(parts),
        out_specs=pl.BlockSpec(memory_space=pl.ANY),
        scratch_shapes=[pltpu.SemaphoreType.DMA((2 * groups,))],
        compiler_params=pltpu.CompilerParams(vmem_limit_bytes=8 << 20),
    )(*parts)

    downs_count, valley_count = lax.axis_size("down"), lax.axis_size("valley")
    rim = lax.ppermute(
        direction[0, :, -1],
        "down",
        [(i, (i + 1) % downs_count) for i in range(downs_count)],
    )
    others = [
        lax.ppermute(
            current, "valley", [(i, (i + by) % valley_count) for i in range(valley_count)]
        )
        for by in range(1, valley_count)
    ]

    def near(current_ref, beside_ref, diag_ref, lower_ref, upper_ref, out_ref):
        _, core = place()

        def write(block_ref):
            for i in range(chains):
                out_ref[i] = dot(current_ref[i], diag_ref[i]) + dot(beside_ref[i], block_ref[i])

        pl.when(core == 0)(lambda: write(upper_ref))
        pl.when(core == 1)(lambda: write(lower_ref))

    total_shape = ((chains, rows, size), F32)
    (partial_sum,) = call(
        near,
        [total_shape],
        current,
        beside,
        blocks(diag_blocks),
        lower,
        upper,
        products=2 * chains,
    )

    def far(column_ref, *refs):
        current_ref, across_ref, rim_ref = refs[:3]
        others_refs = refs[3 : 2 + valley_count]
        lower_ref, upper_ref, down_ref, valley_ref, sum_ref = refs[2 + valley_count : -3]
        out_ref, partner_ref, total_ref = refs[-3:]
        chip, core = place()
        mine = lax.axis_index("valley")
        edge = lax.axis_index("down")

        for i in range(chains):
            column = column_ref[i // downs, i % downs]
            owner = column // valleys
            spot = lax.rem(column, valleys) * downs + i % downs
            behind = lax.rem(mine - owner + valley_count, valley_count)

            @pl.when(behind == 0)
            def _():
                partner_ref[i] = current_ref[spot]

            for by in range(1, valley_count):

                @pl.when(behind == by)
                def _():
                    partner_ref[i] = others_refs[by - 1][spot]

        for i in range(chains):
            total = sum_ref[i] + dot(partner_ref[i], valley_ref[i])
            if i % downs:
                total = total + dot(current_ref[i - 1], down_ref[i])
            total_ref[i] = total

        @pl.when(edge > 0)
        def _():
            for i in range(0, chains, downs):
                total_ref[i] += dot(rim_ref[i // downs], down_ref[i])

        @pl.when(jnp.logical_and(core == 0, chip > 0))
        def _():
            for i in range(chains):
                total_ref[i] += dot(across_ref[i], lower_ref[i])

        @pl.when(jnp.logical_and(core == 1, chip < chips - 1))
        def _():
            for i in range(chains):
                total_ref[i] += dot(across_ref[i], upper_ref[i])

        pltpu.sync_copy(total_ref, out_ref)

    operands = [current, across, rim] + others
    operands += [lower, upper, blocks(down_coupling), blocks(valley_coupling), partial_sum]
    operands = [pltpu.with_memory_space_constraint(x, VMEM) for x in operands]
    image = pl.pallas_call(
        far,
        out_shape=jax.ShapeDtypeStruct((chains, rows, size), F32),
        in_specs=[pl.BlockSpec(memory_space=pltpu.SMEM)] + [spec] * len(operands),
        out_specs=pl.BlockSpec(memory_space=pl.ANY),
        scratch_shapes=[
            pltpu.VMEM((chains, rows, size), BF16),
            pltpu.VMEM((chains, rows, size), F32),
        ],
        compiler_params=pltpu.CompilerParams(vmem_limit_bytes=8 << 20),
        cost_estimate=pl.CostEstimate(
            flops=3 * chains * 2 * rows * size * size, bytes_accessed=4 << 20, transcendentals=0
        ),
    )(coupled_column[0], *operands)
    return (preconditioned.reshape(resid.shape), image.reshape(resid.shape))


def solution(mesh):
    spec = P("elev", "valley", "down", None, None)
    in_specs = (spec,) * 8 + (P("elev", "valley", "down"),)
    return jax.shard_map(
        local, mesh=mesh, in_specs=in_specs, out_specs=(spec, spec), check_vma=False
    )
```

```python
import functools

import jax
import jax.numpy as jnp
from jax import lax
from jax.experimental import pallas as pl
from jax.experimental.pallas import tpu as pltpu
from jax.sharding import PartitionSpec as P

BF16 = jnp.bfloat16
F32 = jnp.float32
VMEM = pltpu.MemorySpace.VMEM
HBM = pltpu.MemorySpace.HBM
GROUPS = 2


def dot(x, y):
    return jnp.dot(x, y, preferred_element_type=F32)


def call(kernel, outs, operands, hbm=(), after=(), scratch=(), products=1):
    spec = pl.BlockSpec(memory_space=pltpu.VMEM)
    anywhere = pl.BlockSpec(memory_space=pl.ANY)
    held = [pltpu.with_memory_space_constraint(x, VMEM) for x in operands]
    far = [pltpu.with_memory_space_constraint(x, HBM) for x in hbm]
    count = len(held) + len(far)

    def body(*refs):
        kernel(*refs[:count], *refs[count + len(after) :])

    return pl.pallas_call(
        body,
        out_shape=[VMEM(shape, dtype) for shape, dtype in outs],
        in_specs=[spec] * len(held) + [anywhere] * (len(far) + len(after)),
        out_specs=[spec] * len(outs),
        scratch_shapes=list(scratch),
        compiler_params=pltpu.CompilerParams(vmem_limit_bytes=8 << 20),
        cost_estimate=pl.CostEstimate(
            flops=products * 2 * 128 * 256 * 256, bytes_accessed=1 << 18, transcendentals=0
        ),
    )(*held, *far, *after)


def place():
    height = lax.axis_index("elev")
    return height // 2, lax.rem(height, 2)


def swap_cores(value):
    count = lax.axis_size("elev")
    return lax.ppermute(value, "elev", [(i, i ^ 1) for i in range(count)])


def swap_chips(value, low):
    pairs = []
    for i in range(lax.axis_size("elev")):
        chip = i // 2
        pairs.append((i, i + 2 if chip == low else i - 2 if chip == low + 1 else i ^ 1))
    return lax.ppermute(value, "elev", pairs)


def local(
    resid,
    direction,
    diag_blocks,
    lower_blocks,
    upper_blocks,
    inv_pivots,
    down_coupling,
    valley_coupling,
    coupled_column,
):
    _, valleys, downs, rows, size = resid.shape
    chains = valleys * downs
    half = chains // 2
    groups = GROUPS
    width = half // groups
    chips = lax.axis_size("elev") // 2
    vectors = lambda x: x.reshape(chains, rows, size)
    blocks = lambda x: x.reshape(chains, size, size)
    rhs, current = vectors(resid), vectors(direction)
    square = ((half, size, size), BF16)
    packed = ((half, size + rows, size), BF16)
    message = ((width, rows, size), BF16)
    every_block = ((chains, size, size), BF16)
    every_vector = ((chains, rows, size), BF16)
    every_sum = ((chains, rows, size), F32)
    spans = [slice(g * width, (g + 1) * width) for g in range(groups)]

    beside = swap_cores(current)

    def first(l_ref, p_ref, r_ref, d_ref, keep_ref, send_ref, lower_v, pivot_v, dir_v, rhs_v, sem):
        _, core = place()
        copies = []
        for side in (1 - core, core):
            part = pl.ds(side * half, half)
            for source, target in ((p_ref, pivot_v), (l_ref, lower_v), (r_ref, rhs_v)):
                copies.append(
                    pltpu.make_async_copy(
                        source.at[part], target.at[part], sem.at[len(copies)]
                    )
                )
        copies.append(pltpu.make_async_copy(d_ref, dir_v, sem.at[len(copies)]))
        for copy in copies:
            copy.start()
        for number, (ref, side) in enumerate(((send_ref, 1 - core), (keep_ref, core))):
            for copy in copies[3 * number : 3 * number + 3]:
                copy.wait()
            for i in range(half):
                block = pivot_v[side * half + i]
                ref[i, :size] = (-dot(lower_v[side * half + i], block)).astype(BF16)
                ref[i, size:] = dot(rhs_v[side * half + i], block).astype(BF16)
        copies[-1].wait()

    keep1, send1, lower_v, pivot_v, dir_v = call(
        first,
        [packed, packed, every_block, every_block, every_vector],
        [],
        hbm=[blocks(lower_blocks), blocks(inv_pivots), rhs, current],
        scratch=[pltpu.VMEM((chains, rows, size), BF16), pltpu.SemaphoreType.DMA((7,))],
        products=3 * chains,
    )
    recv1 = swap_cores(send1)

    def give(which, core, dir_ref, beside_ref, at, out_ref):
        @pl.when(core == which)
        def _():
            out_ref[...] = dir_ref[pl.ds(core * half + at, width)]

        @pl.when(core != which)
        def _():
            out_ref[...] = beside_ref[pl.ds(core * half + at, width)]

    def begin(keep_ref, recv_ref, dir_ref, beside_ref, start_ref, *out_refs):
        chip, core = place()

        def write(bottom, top):
            for i in range(half):
                start_ref[i] = (
                    top[i, size:].astype(F32) + dot(bottom[i, size:], top[i, :size])
                ).astype(BF16)

        pl.when(core == 0)(lambda: write(keep_ref, recv_ref))
        pl.when(core == 1)(lambda: write(recv_ref, keep_ref))
        for out_ref, span in zip(out_refs, spans):

            @pl.when(chip == 0)
            def _():
                out_ref[...] = start_ref[span]

            @pl.when(chip != 0)
            def _():
                give(0, core, dir_ref, beside_ref, span.start, out_ref)

    start, *fronts = call(
        begin,
        [((half, rows, size), BF16)] + [message] * groups,
        [keep1, recv1, dir_v, beside],
        products=half,
    )

    def second(p_ref, u_ref, keep_ref, send_ref, upper_v, sem):
        _, core = place()
        copies = []
        for side in (1 - core, core):
            part = pl.ds(side * half, half)
            copies.append(
                pltpu.make_async_copy(u_ref.at[part], upper_v.at[part], sem.at[len(copies)])
            )
        for copy in copies:
            copy.start()
        for copy, ref, side in zip(copies, (send_ref, keep_ref), (1 - core, core)):
            copy.wait()
            for i in range(half):
                at = side * half + i
                ref[i] = (-dot(upper_v[at], p_ref[at])).astype(BF16)

    keep2, send2, upper_v = call(
        second,
        [square, square, every_block],
        [pivot_v],
        hbm=[blocks(upper_blocks)],
        scratch=[pltpu.SemaphoreType.DMA((2,))],
        products=2 * chains,
    )

    def join(keep_ref, recv_ref, through_ref, bottom_ref):
        _, core = place()

        def write(bottom, top):
            bottom_ref[...] = bottom[...]
            for i in range(half):
                through_ref[i] = dot(bottom[i, :size], top[i, :size]).astype(BF16)

        pl.when(core == 0)(lambda: write(keep_ref, recv_ref))
        pl.when(core == 1)(lambda: write(recv_ref, keep_ref))

    through, bottom = call(join, [square, packed], [keep1, recv1], products=2 * half)
    recv2 = swap_cores(send2)

    def back(keep_ref, recv_ref, back_ref, low_ref, high_ref):
        _, core = place()

        def write(bottom, top):
            low_ref[...] = bottom[...]
            high_ref[...] = top[...]
            for i in range(half):
                back_ref[i] = dot(top[i], bottom[i]).astype(BF16)

        pl.when(core == 0)(lambda: write(keep_ref, recv_ref))
        pl.when(core == 1)(lambda: write(recv_ref, keep_ref))

    backward, back_low, back_high = call(
        back, [square] * 3, [keep2, recv2], products=2 * half
    )

    def near(dir_ref, beside_ref, lower_ref, upper_ref, diag_ref, out_ref, diag_v, sem):
        _, core = place()
        copy = pltpu.make_async_copy(diag_ref, diag_v, sem.at[0])
        copy.start()

        def write(block_ref):
            for i in range(chains):
                out_ref[i] = dot(beside_ref[i], block_ref[i])

        pl.when(core == 0)(lambda: write(upper_ref))
        pl.when(core == 1)(lambda: write(lower_ref))
        copy.wait()
        for i in range(chains):
            out_ref[i] += dot(dir_ref[i], diag_v[i])

    (near_sum,) = call(
        near,
        [every_sum],
        [dir_v, beside, lower_v, upper_v],
        hbm=[blocks(diag_blocks)],
        scratch=[pltpu.VMEM((chains, size, size), BF16), pltpu.SemaphoreType.DMA((1,))],
        products=2 * chains,
    )

    def advance(span, low, in_ref, start_ref, through_ref, dir_ref, beside_ref, out_ref):
        chip, core = place()
        at = span.start

        @pl.when(chip == low)
        def _():
            for i in range(width):
                out_ref[i] = (
                    start_ref[at + i].astype(F32) + dot(in_ref[i], through_ref[at + i])
                ).astype(BF16)

        @pl.when(chip != low)
        def _():
            give(0, core, dir_ref, beside_ref, at, out_ref)

    heard_up = [[] for _ in spans]
    for low in range(chips - 1):
        for g, span in enumerate(spans):
            arrived = swap_chips(fronts[g], low)
            heard_up[g].append(arrived)
            if low < chips - 2:
                (fronts[g],) = call(
                    functools.partial(advance, span, low + 1),
                    [message],
                    [arrived, start, through, dir_v, beside],
                    after=[near_sum] if low == 0 and g == 0 else [],
                    products=width,
                )

    downs_count, valley_count = lax.axis_size("down"), lax.axis_size("valley")
    rim = lax.ppermute(
        direction[0, :, -1],
        "down",
        [(i, (i + 1) % downs_count) for i in range(downs_count)],
    )
    others = [
        lax.ppermute(
            current, "valley", [(i, (i + by) % valley_count) for i in range(valley_count)]
        )
        for by in range(1, valley_count)
    ]

    def far(*refs):
        dir_ref, sum_ref, rim_ref = refs[:3]
        others_refs = refs[3 : 2 + valley_count]
        down_ref, valley_ref, column_ref, out_ref = refs[2 + valley_count : 6 + valley_count]
        partner_ref, down_v, valley_v, column_s, sem = refs[6 + valley_count :]
        mine = lax.axis_index("valley")
        edge = lax.axis_index("down")
        copies = [
            pltpu.make_async_copy(source, target, sem.at[i])
            for i, (source, target) in enumerate(
                ((column_ref, column_s), (down_ref, down_v), (valley_ref, valley_v))
            )
        ]
        for copy in copies:
            copy.start()
        copies[0].wait()
        for i in range(chains):
            column = column_s[i // downs, i % downs]
            owner = column // valleys
            spot = lax.rem(column, valleys) * downs + i % downs
            behind = lax.rem(mine - owner + valley_count, valley_count)

            @pl.when(behind == 0)
            def _():
                partner_ref[i] = dir_ref[spot]

            for by in range(1, valley_count):

                @pl.when(behind == by)
                def _():
                    partner_ref[i] = others_refs[by - 1][spot]

        copies[1].wait()
        for i in range(chains):
            if i % downs:
                out_ref[i] = sum_ref[i] + dot(dir_ref[i - 1], down_v[i])

        @pl.when(edge > 0)
        def _():
            for i in range(0, chains, downs):
                out_ref[i] = sum_ref[i] + dot(rim_ref[i // downs], down_v[i])

        @pl.when(edge == 0)
        def _():
            for i in range(0, chains, downs):
                out_ref[i] = sum_ref[i]

        copies[2].wait()
        for i in range(chains):
            out_ref[i] += dot(partner_ref[i], valley_v[i])

    (far_sum,) = call(
        far,
        [every_sum],
        [dir_v, near_sum, rim] + others,
        hbm=[blocks(down_coupling), blocks(valley_coupling), coupled_column[0]],
        scratch=[
            pltpu.VMEM((chains, rows, size), BF16),
            pltpu.VMEM((chains, size, size), BF16),
            pltpu.VMEM((chains, size, size), BF16),
            pltpu.SMEM((valleys, downs), jnp.int32),
            pltpu.SemaphoreType.DMA((3,)),
        ],
        products=2 * chains,
    )

    def turn(span, *refs):
        heard_refs = refs[: chips - 1]
        start_ref, through_ref, bottom_ref, low_ref, dir_ref, beside_ref = refs[chips - 1 : -4]
        top_ref, base_ref, out_ref, in_ref = refs[-4:]
        chip, core = place()
        at = span.start

        @pl.when(chip == 0)
        def _():
            in_ref[...] = jnp.zeros_like(in_ref)

        for low in range(chips - 1):

            @pl.when(chip == low + 1)
            def _():
                in_ref[...] = heard_refs[low][...]

        for i in range(width):
            arrived = in_ref[i]
            top = (start_ref[at + i].astype(F32) + dot(arrived, through_ref[at + i])).astype(BF16)
            base = bottom_ref[at + i, size:].astype(F32) + dot(arrived, bottom_ref[at + i, :size])
            top_ref[i] = top
            base_ref[i] = (base.astype(BF16).astype(F32) + dot(top, low_ref[at + i])).astype(BF16)

        @pl.when(chip == chips - 1)
        def _():
            out_ref[...] = base_ref[...]

        @pl.when(chip != chips - 1)
        def _():
            give(1, core, dir_ref, beside_ref, at, out_ref)

    tops, bases, solved = [], [], []
    for g, span in enumerate(spans):
        top, base, out = call(
            functools.partial(turn, span),
            [message] * 3,
            heard_up[g] + [start, through, bottom, back_low, dir_v, beside],
            scratch=[pltpu.VMEM(*message)],
            products=3 * width,
        )
        tops.append(top)
        bases.append(base)
        solved.append(out)

    def retreat(span, low, in_ref, base_ref, back_ref, dir_ref, beside_ref, out_ref):
        chip, core = place()
        at = span.start

        @pl.when(chip == low)
        def _():
            for i in range(width):
                out_ref[i] = (
                    base_ref[i].astype(F32) + dot(in_ref[i], back_ref[at + i])
                ).astype(BF16)

        @pl.when(chip != low)
        def _():
            give(1, core, dir_ref, beside_ref, at, out_ref)

    heard_down = [[] for _ in spans]
    for low in range(chips - 2, -1, -1):
        for g, span in enumerate(spans):
            arrived = swap_chips(solved[g], low)
            heard_down[g].insert(0, arrived)
            if low > 0:
                (solved[g],) = call(
                    functools.partial(retreat, span, low),
                    [message],
                    [arrived, bases[g], backward, dir_v, beside],
                    after=[far_sum] if low == chips - 2 and g == 0 else [],
                    products=width,
                )

    def finish(span, *refs):
        up_refs, down_refs = refs[: chips - 1], refs[chips - 1 : 2 * chips - 2]
        top_ref, base_ref, back_ref, high_ref = refs[2 * chips - 2 : -4]
        keep_ref, own_ref, send_ref, in_ref = refs[-4:]
        chip, core = place()
        at = span.start
        sent_halo = send_ref.at[pl.ds(width, width)]

        @pl.when(chip == chips - 1)
        def _():
            in_ref[...] = jnp.zeros_like(in_ref)

        for low in range(chips - 1):

            @pl.when(chip == low)
            def _():
                in_ref[...] = down_refs[low][...]

        for which, mine, other in ((0, own_ref, sent_halo), (1, sent_halo, own_ref)):

            @pl.when(core == which)
            def _():
                @pl.when(chip == 0)
                def _():
                    mine[...] = jnp.zeros_like(mine)

                @pl.when(chip == chips - 1)
                def _():
                    other[...] = jnp.zeros_like(other)

                for low in range(chips - 1):

                    @pl.when(chip == low + 1)
                    def _():
                        mine[...] = down_refs[low][...]

                    @pl.when(chip == low)
                    def _():
                        other[...] = up_refs[low][...]

        for i in range(width):
            arrived = in_ref[i]
            low = (base_ref[i].astype(F32) + dot(arrived, back_ref[at + i])).astype(BF16)
            high = (top_ref[i].astype(F32) + dot(arrived, high_ref[at + i])).astype(BF16)

            @pl.when(core == 0)
            def _():
                keep_ref[i] = low
                send_ref[i] = high

            @pl.when(core == 1)
            def _():
                keep_ref[i] = high
                send_ref[i] = low

    def final(span, *refs):
        keep_ref, own_ref, recv_ref, sum_ref, lower_ref, upper_ref = refs[:6]
        solved_ref, image_ref, total_ref, sem = refs[-4:]
        _, core = place()
        at = span.start
        copies = []
        for side, source in ((core, keep_ref), (1 - core, recv_ref.at[pl.ds(0, width)])):
            copies.append(
                pltpu.make_async_copy(
                    source, solved_ref.at[pl.ds(side * half + at, width)], sem.at[len(copies)]
                )
            )
            copies[-1].start()

        def write(block_ref):
            for number, side in enumerate((core, 1 - core)):
                base = side * half + at
                for i in range(width):
                    halo = own_ref[i] if number == 0 else recv_ref[width + i]
                    total_ref[number * width + i] = sum_ref[base + i] + dot(
                        halo, block_ref[base + i]
                    )

        pl.when(core == 0)(lambda: write(lower_ref))
        pl.when(core == 1)(lambda: write(upper_ref))
        for number, side in enumerate((core, 1 - core)):
            copies.append(
                pltpu.make_async_copy(
                    total_ref.at[pl.ds(number * width, width)],
                    image_ref.at[pl.ds(side * half + at, width)],
                    sem.at[len(copies)],
                )
            )
            copies[-1].start()
        for copy in copies:
            copy.wait()

    spec = pl.BlockSpec(memory_space=pltpu.VMEM)
    anywhere = pl.BlockSpec(memory_space=pl.ANY)
    outputs = []
    for g, span in enumerate(spans):
        keep, own, send = call(
            functools.partial(finish, span),
            [message, message, ((2 * width, rows, size), BF16)],
            heard_up[g] + heard_down[g] + [tops[g], bases[g], backward, back_high],
            scratch=[pltpu.VMEM(*message)],
            products=2 * width,
        )
        operands = [keep, own, swap_cores(send), far_sum, lower_v, upper_v]
        operands = [pltpu.with_memory_space_constraint(x, VMEM) for x in operands]
        outputs = pl.pallas_call(
            functools.partial(final, span),
            out_shape=[HBM(*every_vector), HBM(*every_sum)],
            in_specs=[spec] * len(operands) + [anywhere] * len(outputs),
            out_specs=[anywhere] * 2,
            input_output_aliases={len(operands) + i: i for i in range(len(outputs))},
            scratch_shapes=[
                pltpu.VMEM((2 * width, rows, size), F32),
                pltpu.SemaphoreType.DMA((4,)),
            ],
            compiler_params=pltpu.CompilerParams(vmem_limit_bytes=8 << 20),
            cost_estimate=pl.CostEstimate(
                flops=4 * width * rows * size * size, bytes_accessed=1 << 20, transcendentals=0
            ),
        )(*operands, *outputs)
    preconditioned, image = outputs
    return (preconditioned.reshape(resid.shape), image.reshape(resid.shape))


def solution(mesh):
    spec = P("elev", "valley", "down", None, None)
    in_specs = (spec,) * 8 + (P("elev", "valley", "down"),)
    return jax.shard_map(
        local, mesh=mesh, in_specs=in_specs, out_specs=(spec, spec), check_vma=False
    )
```

```python
import functools

import jax
import jax.numpy as jnp
from jax import lax
from jax.experimental import pallas as pl
from jax.experimental.pallas import tpu as pltpu
from jax.sharding import PartitionSpec as P

BF16 = jnp.bfloat16
F32 = jnp.float32
VMEM = pltpu.MemorySpace.VMEM
HBM = pltpu.MemorySpace.HBM
GROUPS = 2


def dot(x, y):
    return jnp.dot(x, y, preferred_element_type=F32)


def call(kernel, outs, operands, hbm=(), after=(), scratch=(), products=1, room=1):
    spec = pl.BlockSpec(memory_space=pltpu.VMEM)
    anywhere = pl.BlockSpec(memory_space=pl.ANY)
    held = [pltpu.with_memory_space_constraint(x, VMEM) for x in operands]
    far = [pltpu.with_memory_space_constraint(x, HBM) for x in hbm]
    count = len(held) + len(far)

    def body(*refs):
        kernel(*refs[:count], *refs[count + len(after) :])

    return pl.pallas_call(
        body,
        out_shape=[VMEM(shape, dtype) for shape, dtype in outs],
        in_specs=[spec] * len(held) + [anywhere] * (len(far) + len(after)),
        out_specs=[spec] * len(outs),
        scratch_shapes=list(scratch),
        compiler_params=pltpu.CompilerParams(vmem_limit_bytes=room << 20),
        cost_estimate=pl.CostEstimate(
            flops=products * 2 * 128 * 256 * 256, bytes_accessed=1 << 18, transcendentals=0
        ),
    )(*held, *far, *after)


def place():
    height = lax.axis_index("elev")
    return height // 2, lax.rem(height, 2)


def swap_cores(value):
    count = lax.axis_size("elev")
    return lax.ppermute(value, "elev", [(i, i ^ 1) for i in range(count)])


def swap_chips(value, low):
    pairs = []
    for i in range(lax.axis_size("elev")):
        chip = i // 2
        pairs.append((i, i + 2 if chip == low else i - 2 if chip == low + 1 else i ^ 1))
    return lax.ppermute(value, "elev", pairs)


def local(
    resid,
    direction,
    diag_blocks,
    lower_blocks,
    upper_blocks,
    inv_pivots,
    down_coupling,
    valley_coupling,
    coupled_column,
):
    _, valleys, downs, rows, size = resid.shape
    chains = valleys * downs
    half = chains // 2
    groups = GROUPS
    width = half // groups
    chips = lax.axis_size("elev") // 2
    vectors = lambda x: x.reshape(chains, rows, size)
    blocks = lambda x: x.reshape(chains, size, size)
    rhs, current = vectors(resid), vectors(direction)
    square = ((half, size, size), BF16)
    packed = ((half, size + rows, size), BF16)
    message = ((width, rows, size), BF16)
    every_block = ((chains, size, size), BF16)
    every_vector = ((chains, rows, size), BF16)
    every_sum = ((chains, rows, size), F32)
    spans = [slice(g * width, (g + 1) * width) for g in range(groups)]

    beside = swap_cores(current)

    def first(*refs):
        l_ref, p_ref, r_ref, d_ref, keep_ref, send_ref, lower_v, pivot_v, dir_v, rim_ref = refs[:-2]
        rhs_v, sem = refs[-2:]
        _, core = place()
        copies = []
        for side in (1 - core, core):
            part = pl.ds(side * half, half)
            for source, target in ((p_ref, pivot_v), (l_ref, lower_v), (r_ref, rhs_v)):
                copies.append(
                    pltpu.make_async_copy(
                        source.at[part], target.at[part], sem.at[len(copies)]
                    )
                )
        copies.append(pltpu.make_async_copy(d_ref, dir_v, sem.at[len(copies)]))
        for copy in copies:
            copy.start()
        for number, (ref, side) in enumerate(((send_ref, 1 - core), (keep_ref, core))):
            for copy in copies[3 * number : 3 * number + 3]:
                copy.wait()
            for i in range(half):
                block = pivot_v[side * half + i]
                ref[i, :size] = (-dot(lower_v[side * half + i], block)).astype(BF16)
                ref[i, size:] = dot(rhs_v[side * half + i], block).astype(BF16)
        copies[-1].wait()
        for i in range(valleys):
            rim_ref[i] = dir_v[i * downs + downs - 1]

    keep1, send1, lower_v, pivot_v, dir_v, rim_out = call(
        first,
        [packed, packed, every_block, every_block, every_vector, ((valleys, rows, size), BF16)],
        [],
        hbm=[blocks(lower_blocks), blocks(inv_pivots), rhs, current],
        scratch=[pltpu.VMEM((chains, rows, size), BF16), pltpu.SemaphoreType.DMA((7,))],
        products=3 * chains,
        room=2,
    )
    recv1 = swap_cores(send1)

    def give(which, core, dir_ref, beside_ref, at, out_ref):
        @pl.when(core == which)
        def _():
            out_ref[...] = dir_ref[pl.ds(core * half + at, width)]

        @pl.when(core != which)
        def _():
            out_ref[...] = beside_ref[pl.ds(core * half + at, width)]

    def begin(keep_ref, recv_ref, dir_ref, beside_ref, start_ref, *out_refs):
        chip, core = place()

        def write(bottom, top):
            for i in range(half):
                start_ref[i] = (
                    top[i, size:].astype(F32) + dot(bottom[i, size:], top[i, :size])
                ).astype(BF16)

        pl.when(core == 0)(lambda: write(keep_ref, recv_ref))
        pl.when(core == 1)(lambda: write(recv_ref, keep_ref))
        for out_ref, span in zip(out_refs, spans):

            @pl.when(chip == 0)
            def _():
                out_ref[...] = start_ref[span]

            @pl.when(chip != 0)
            def _():
                give(0, core, dir_ref, beside_ref, span.start, out_ref)

    start, *fronts = call(
        begin,
        [((half, rows, size), BF16)] + [message] * groups,
        [keep1, recv1, dir_v, beside],
        products=half,
    )

    def second(p_ref, u_ref, keep_ref, send_ref, upper_v, sem):
        _, core = place()
        copies = []
        for side in (1 - core, core):
            part = pl.ds(side * half, half)
            copies.append(
                pltpu.make_async_copy(u_ref.at[part], upper_v.at[part], sem.at[len(copies)])
            )
        for copy in copies:
            copy.start()
        for copy, ref, side in zip(copies, (send_ref, keep_ref), (1 - core, core)):
            copy.wait()
            for i in range(half):
                at = side * half + i
                ref[i] = (-dot(upper_v[at], p_ref[at])).astype(BF16)

    keep2, send2, upper_v = call(
        second,
        [square, square, every_block],
        [pivot_v],
        hbm=[blocks(upper_blocks)],
        scratch=[pltpu.SemaphoreType.DMA((2,))],
        products=2 * chains,
    )

    def join(keep_ref, recv_ref, through_ref, bottom_ref):
        _, core = place()

        def write(bottom, top):
            bottom_ref[...] = bottom[...]
            for i in range(half):
                through_ref[i] = dot(bottom[i, :size], top[i, :size]).astype(BF16)

        pl.when(core == 0)(lambda: write(keep_ref, recv_ref))
        pl.when(core == 1)(lambda: write(recv_ref, keep_ref))

    through, bottom = call(join, [square, packed], [keep1, recv1], products=2 * half)
    recv2 = swap_cores(send2)

    def back(keep_ref, recv_ref, back_ref, low_ref, high_ref):
        _, core = place()

        def write(bottom, top):
            low_ref[...] = bottom[...]
            high_ref[...] = top[...]
            for i in range(half):
                back_ref[i] = dot(top[i], bottom[i]).astype(BF16)

        pl.when(core == 0)(lambda: write(keep_ref, recv_ref))
        pl.when(core == 1)(lambda: write(recv_ref, keep_ref))

    backward, back_low, back_high = call(
        back, [square] * 3, [keep2, recv2], products=2 * half
    )

    def near(dir_ref, beside_ref, lower_ref, upper_ref, diag_ref, out_ref, diag_v, sem):
        _, core = place()
        copy = pltpu.make_async_copy(diag_ref, diag_v, sem.at[0])
        copy.start()

        def write(block_ref):
            for i in range(chains):
                out_ref[i] = dot(beside_ref[i], block_ref[i])

        pl.when(core == 0)(lambda: write(upper_ref))
        pl.when(core == 1)(lambda: write(lower_ref))
        copy.wait()
        for i in range(chains):
            out_ref[i] += dot(dir_ref[i], diag_v[i])

    (near_sum,) = call(
        near,
        [every_sum],
        [dir_v, beside, lower_v, upper_v],
        hbm=[blocks(diag_blocks)],
        scratch=[pltpu.VMEM((chains, size, size), BF16), pltpu.SemaphoreType.DMA((1,))],
        products=2 * chains,
        room=2,
    )

    def advance(span, low, in_ref, start_ref, through_ref, dir_ref, beside_ref, out_ref):
        chip, core = place()
        at = span.start

        @pl.when(chip == low)
        def _():
            for i in range(width):
                out_ref[i] = (
                    start_ref[at + i].astype(F32) + dot(in_ref[i], through_ref[at + i])
                ).astype(BF16)

        @pl.when(chip != low)
        def _():
            give(0, core, dir_ref, beside_ref, at, out_ref)

    heard_up = [[] for _ in spans]
    for low in range(chips - 1):
        for g, span in enumerate(spans):
            arrived = swap_chips(fronts[g], low)
            heard_up[g].append(arrived)
            if low < chips - 2:
                (fronts[g],) = call(
                    functools.partial(advance, span, low + 1),
                    [message],
                    [arrived, start, through, dir_v, beside],
                    after=[near_sum] if low == 0 and g == 0 else [],
                    products=width,
                )

    downs_count, valley_count = lax.axis_size("down"), lax.axis_size("valley")
    rim = lax.ppermute(
        rim_out,
        "down",
        [(i, (i + 1) % downs_count) for i in range(downs_count)],
    )
    others = [
        lax.ppermute(
            current, "valley", [(i, (i + by) % valley_count) for i in range(valley_count)]
        )
        for by in range(1, valley_count)
    ]

    def far(*refs):
        dir_ref, sum_ref, rim_ref = refs[:3]
        others_refs = refs[3 : 2 + valley_count]
        down_ref, valley_ref, column_ref, out_ref = refs[2 + valley_count : 6 + valley_count]
        partner_ref, down_v, valley_v, column_s, sem = refs[6 + valley_count :]
        mine = lax.axis_index("valley")
        edge = lax.axis_index("down")
        copies = [
            pltpu.make_async_copy(source, target, sem.at[i])
            for i, (source, target) in enumerate(
                ((column_ref, column_s), (down_ref, down_v), (valley_ref, valley_v))
            )
        ]
        for copy in copies:
            copy.start()
        copies[0].wait()
        for i in range(chains):
            column = column_s[0, i % downs, i // downs]
            owner = column // valleys
            spot = lax.rem(column, valleys) * downs + i % downs
            behind = lax.rem(mine - owner + valley_count, valley_count)

            @pl.when(behind == 0)
            def _():
                partner_ref[i] = dir_ref[spot]

            for by in range(1, valley_count):

                @pl.when(behind == by)
                def _():
                    partner_ref[i] = others_refs[by - 1][spot]

        copies[1].wait()
        for i in range(chains):
            if i % downs:
                out_ref[i] = sum_ref[i] + dot(dir_ref[i - 1], down_v[i])

        @pl.when(edge > 0)
        def _():
            for i in range(0, chains, downs):
                out_ref[i] = sum_ref[i] + dot(rim_ref[i // downs], down_v[i])

        @pl.when(edge == 0)
        def _():
            for i in range(0, chains, downs):
                out_ref[i] = sum_ref[i]

        copies[2].wait()
        for i in range(chains):
            out_ref[i] += dot(partner_ref[i], valley_v[i])

    (far_sum,) = call(
        far,
        [every_sum],
        [dir_v, near_sum, rim] + others,
        hbm=[blocks(down_coupling), blocks(valley_coupling), jnp.swapaxes(coupled_column, 1, 2)],
        scratch=[
            pltpu.VMEM((chains, rows, size), BF16),
            pltpu.VMEM((chains, size, size), BF16),
            pltpu.VMEM((chains, size, size), BF16),
            pltpu.SMEM((1, downs, valleys), jnp.int32),
            pltpu.SemaphoreType.DMA((3,)),
        ],
        products=2 * chains,
        room=4,
    )

    def turn(span, *refs):
        heard_refs = refs[: chips - 1]
        start_ref, through_ref, bottom_ref, low_ref, dir_ref, beside_ref = refs[chips - 1 : -4]
        top_ref, base_ref, out_ref, in_ref = refs[-4:]
        chip, core = place()
        at = span.start

        @pl.when(chip == 0)
        def _():
            in_ref[...] = jnp.zeros_like(in_ref)

        for low in range(chips - 1):

            @pl.when(chip == low + 1)
            def _():
                in_ref[...] = heard_refs[low][...]

        for i in range(width):
            arrived = in_ref[i]
            top = (start_ref[at + i].astype(F32) + dot(arrived, through_ref[at + i])).astype(BF16)
            base = bottom_ref[at + i, size:].astype(F32) + dot(arrived, bottom_ref[at + i, :size])
            top_ref[i] = top
            base_ref[i] = (base.astype(BF16).astype(F32) + dot(top, low_ref[at + i])).astype(BF16)

        @pl.when(chip == chips - 1)
        def _():
            out_ref[...] = base_ref[...]

        @pl.when(chip != chips - 1)
        def _():
            give(1, core, dir_ref, beside_ref, at, out_ref)

    tops, bases, solved = [], [], []
    for g, span in enumerate(spans):
        top, base, out = call(
            functools.partial(turn, span),
            [message] * 3,
            heard_up[g] + [start, through, bottom, back_low, dir_v, beside],
            scratch=[pltpu.VMEM(*message)],
            products=3 * width,
        )
        tops.append(top)
        bases.append(base)
        solved.append(out)

    def retreat(span, low, in_ref, base_ref, back_ref, dir_ref, beside_ref, out_ref):
        chip, core = place()
        at = span.start

        @pl.when(chip == low)
        def _():
            for i in range(width):
                out_ref[i] = (
                    base_ref[i].astype(F32) + dot(in_ref[i], back_ref[at + i])
                ).astype(BF16)

        @pl.when(chip != low)
        def _():
            give(1, core, dir_ref, beside_ref, at, out_ref)

    heard_down = [[] for _ in spans]
    for low in range(chips - 2, -1, -1):
        for g, span in enumerate(spans):
            arrived = swap_chips(solved[g], low)
            heard_down[g].insert(0, arrived)
            if low > 0:
                (solved[g],) = call(
                    functools.partial(retreat, span, low),
                    [message],
                    [arrived, bases[g], backward, dir_v, beside],
                    after=[far_sum] if low == chips - 2 and g == 0 else [],
                    products=width,
                )

    def finish(span, *refs):
        up_refs, down_refs = refs[: chips - 1], refs[chips - 1 : 2 * chips - 2]
        top_ref, base_ref, back_ref, high_ref = refs[2 * chips - 2 : -4]
        keep_ref, own_ref, send_ref, in_ref = refs[-4:]
        chip, core = place()
        at = span.start
        sent_halo = send_ref.at[pl.ds(width, width)]

        @pl.when(chip == chips - 1)
        def _():
            in_ref[...] = jnp.zeros_like(in_ref)

        for low in range(chips - 1):

            @pl.when(chip == low)
            def _():
                in_ref[...] = down_refs[low][...]

        for which, mine, other in ((0, own_ref, sent_halo), (1, sent_halo, own_ref)):

            @pl.when(core == which)
            def _():
                @pl.when(chip == 0)
                def _():
                    mine[...] = jnp.zeros_like(mine)

                @pl.when(chip == chips - 1)
                def _():
                    other[...] = jnp.zeros_like(other)

                for low in range(chips - 1):

                    @pl.when(chip == low + 1)
                    def _():
                        mine[...] = down_refs[low][...]

                    @pl.when(chip == low)
                    def _():
                        other[...] = up_refs[low][...]

        for i in range(width):
            arrived = in_ref[i]
            low = (base_ref[i].astype(F32) + dot(arrived, back_ref[at + i])).astype(BF16)
            high = (top_ref[i].astype(F32) + dot(arrived, high_ref[at + i])).astype(BF16)

            @pl.when(core == 0)
            def _():
                keep_ref[i] = low
                send_ref[i] = high

            @pl.when(core == 1)
            def _():
                keep_ref[i] = high
                send_ref[i] = low

    def final(span, *refs):
        keep_ref, own_ref, recv_ref, sum_ref, lower_ref, upper_ref = refs[:6]
        solved_ref, image_ref, total_ref, sem = refs[-4:]
        _, core = place()
        at = span.start
        copies = []
        for side, source in ((core, keep_ref), (1 - core, recv_ref.at[pl.ds(0, width)])):
            copies.append(
                pltpu.make_async_copy(
                    source, solved_ref.at[pl.ds(side * half + at, width)], sem.at[len(copies)]
                )
            )
            copies[-1].start()

        def write(block_ref):
            for number, side in enumerate((core, 1 - core)):
                base = side * half + at
                for i in range(width):
                    halo = own_ref[i] if number == 0 else recv_ref[width + i]
                    total_ref[number * width + i] = sum_ref[base + i] + dot(
                        halo, block_ref[base + i]
                    )

        pl.when(core == 0)(lambda: write(lower_ref))
        pl.when(core == 1)(lambda: write(upper_ref))
        for number, side in enumerate((core, 1 - core)):
            copies.append(
                pltpu.make_async_copy(
                    total_ref.at[pl.ds(number * width, width)],
                    image_ref.at[pl.ds(side * half + at, width)],
                    sem.at[len(copies)],
                )
            )
            copies[-1].start()
        for copy in copies:
            copy.wait()

    spec = pl.BlockSpec(memory_space=pltpu.VMEM)
    anywhere = pl.BlockSpec(memory_space=pl.ANY)
    outputs = []
    for g, span in enumerate(spans):
        keep, own, send = call(
            functools.partial(finish, span),
            [message, message, ((2 * width, rows, size), BF16)],
            heard_up[g] + heard_down[g] + [tops[g], bases[g], backward, back_high],
            scratch=[pltpu.VMEM(*message)],
            products=2 * width,
        )
        operands = [keep, own, swap_cores(send), far_sum, lower_v, upper_v]
        operands = [pltpu.with_memory_space_constraint(x, VMEM) for x in operands]
        outputs = pl.pallas_call(
            functools.partial(final, span),
            out_shape=[HBM(*every_vector), HBM(*every_sum)],
            in_specs=[spec] * len(operands) + [anywhere] * len(outputs),
            out_specs=[anywhere] * 2,
            input_output_aliases={len(operands) + i: i for i in range(len(outputs))},
            scratch_shapes=[
                pltpu.VMEM((2 * width, rows, size), F32),
                pltpu.SemaphoreType.DMA((4,)),
            ],
            compiler_params=pltpu.CompilerParams(vmem_limit_bytes=2 << 20),
            cost_estimate=pl.CostEstimate(
                flops=4 * width * rows * size * size, bytes_accessed=1 << 20, transcendentals=0
            ),
        )(*operands, *outputs)
    preconditioned, image = outputs
    return (preconditioned.reshape(resid.shape), image.reshape(resid.shape))


def solution(mesh):
    spec = P("elev", "valley", "down", None, None)
    in_specs = (spec,) * 8 + (P("elev", "valley", "down"),)
    return jax.shard_map(
        local, mesh=mesh, in_specs=in_specs, out_specs=(spec, spec), check_vma=False
    )
```

```python
import functools

import jax
import jax.numpy as jnp
from jax import lax
from jax.experimental import pallas as pl
from jax.experimental.pallas import tpu as pltpu
from jax.sharding import PartitionSpec as P

BF16 = jnp.bfloat16
F32 = jnp.float32
VMEM = pltpu.MemorySpace.VMEM
HBM = pltpu.MemorySpace.HBM
GROUPS = 2
WEIGHT = 190000000


def dot(x, y):
    return jnp.dot(x, y, preferred_element_type=F32)


def call(kernel, outs, operands, hbm=(), after=(), old=(), scratch=(), products=1, room=1, weight=1):
    spec = pl.BlockSpec(memory_space=pltpu.VMEM)
    anywhere = pl.BlockSpec(memory_space=pl.ANY)
    held = [pltpu.with_memory_space_constraint(x, VMEM) for x in operands]
    after = [*after, *old]
    far = [pltpu.with_memory_space_constraint(x, HBM) for x in hbm]
    count = len(held) + len(far)

    def body(*refs):
        kernel(*refs[:count], *refs[count + len(after) :])

    return pl.pallas_call(
        body,
        out_shape=[VMEM(shape, dtype) for shape, dtype in outs],
        in_specs=[spec] * len(held) + [anywhere] * (len(far) + len(after)),
        out_specs=[spec] * len(outs),
        scratch_shapes=list(scratch),
        input_output_aliases={count + len(after) - len(old) + i: i for i in range(len(old))},
        compiler_params=pltpu.CompilerParams(vmem_limit_bytes=room << 20),
        cost_estimate=pl.CostEstimate(
            flops=products * weight, bytes_accessed=1 << 10, transcendentals=0
        ),
    )(*held, *far, *after)


def place():
    height = lax.axis_index("elev")
    return height // 2, lax.rem(height, 2)


def swap_cores(value):
    count = lax.axis_size("elev")
    return lax.ppermute(value, "elev", [(i, i ^ 1) for i in range(count)])


def swap_chips(value, *lows):
    pairs = []
    for i in range(lax.axis_size("elev")):
        chip = i // 2
        step = 2 if chip in lows else -2 if chip - 1 in lows else 1 - 2 * (i % 2)
        pairs.append((i, i + step))
    return lax.ppermute(value, "elev", pairs)


def send_up(value, low):
    return lax.ppermute(value, "elev", [(2 * low, 2 * low + 2), (2 * low + 1, 2 * low + 3)])


def local(
    resid,
    direction,
    diag_blocks,
    lower_blocks,
    upper_blocks,
    inv_pivots,
    down_coupling,
    valley_coupling,
    coupled_column,
):
    _, valleys, downs, rows, size = resid.shape
    chains = valleys * downs
    half = chains // 2
    groups = GROUPS
    width = half // groups
    chips = lax.axis_size("elev") // 2
    vectors = lambda x: x.reshape(chains, rows, size)
    blocks = lambda x: x.reshape(chains, size, size)
    rhs, current = vectors(resid), vectors(direction)
    square = ((half, size, size), BF16)
    packed = ((half, size + rows, size), BF16)
    fuller = ((half, size + 2 * rows, size), BF16)
    message = ((width, rows, size), BF16)
    every_block = ((chains, size, size), BF16)
    every_vector = ((chains, rows, size), BF16)
    every_sum = ((chains, rows, size), F32)
    apart = chips > 3
    spans = [slice(g * width, (g + 1) * width) for g in range(groups)]

    half_blocks, half_vectors = ((half, size, size), BF16), ((half, rows, size), BF16)

    def send_products(l_ref, p_ref, r_ref, d_ref, out_ref, lower_v, pivot_v, rhs_v, sem):
        _, core = place()
        part = pl.ds((1 - core) * half, half)
        copies = [
            pltpu.make_async_copy(source.at[part], target, sem.at[i])
            for i, (source, target) in enumerate(
                (
                    (p_ref, pivot_v),
                    (r_ref, rhs_v),
                    (l_ref, lower_v),
                    (d_ref, out_ref.at[:, pl.ds(size + rows, rows)]),
                )
            )
        ]
        for copy in copies:
            copy.start()
        copies[0].wait()
        copies[1].wait()
        for i in range(half):
            out_ref[i, size : size + rows] = dot(rhs_v[i], pivot_v[i]).astype(BF16)
        copies[2].wait()
        for i in range(half):
            out_ref[i, :size] = (-dot(lower_v[i], pivot_v[i])).astype(BF16)
        copies[3].wait()

    send1, lower_other, pivot_other = call(
        send_products,
        [fuller, half_blocks, half_blocks],
        [],
        hbm=[blocks(lower_blocks), blocks(inv_pivots), rhs, current],
        scratch=[pltpu.VMEM(*half_vectors), pltpu.SemaphoreType.DMA((4,))],
        products=3 * half,
        room=2,
    )
    recv1 = swap_cores(send1)

    def keep_products(other_ref, l_ref, p_ref, u_ref, r_ref, d_ref, *refs):
        keep1_ref, keep2_ref, send2_ref, lower_v, own_v, other_v, dir_v = refs[:7]
        pivot_v, rhs_v, sem = refs[7:]
        _, core = place()
        own, other = pl.ds(core * half, half), pl.ds((1 - core) * half, half)
        copies = [
            pltpu.make_async_copy(source, target, sem.at[i])
            for i, (source, target) in enumerate(
                (
                    (p_ref.at[own], pivot_v),
                    (r_ref.at[own], rhs_v),
                    (l_ref.at[own], lower_v),
                    (d_ref, dir_v),
                    (u_ref.at[own], own_v),
                    (u_ref.at[other], other_v),
                    (d_ref.at[own], send2_ref.at[:, pl.ds(size, rows)]),
                )
            )
        ]
        for copy in copies:
            copy.start()
        copies[0].wait()
        copies[1].wait()
        for i in range(half):
            keep1_ref[i, size:] = dot(rhs_v[i], pivot_v[i]).astype(BF16)
        copies[2].wait()
        for i in range(half):
            keep1_ref[i, :size] = (-dot(lower_v[i], pivot_v[i])).astype(BF16)
        copies[3].wait()
        copies[4].wait()
        for i in range(half):
            keep2_ref[i] = (-dot(own_v[i], pivot_v[i])).astype(BF16)
        copies[5].wait()
        for i in range(half):
            send2_ref[i, :size] = (-dot(other_v[i], other_ref[i])).astype(BF16)
        copies[6].wait()

    keep1, keep2, send2, lower_own, upper_own, upper_other, dir_v = call(
        keep_products,
        [packed, square, packed, half_blocks, half_blocks, half_blocks, every_vector],
        [pivot_other],
        hbm=[blocks(lower_blocks), blocks(inv_pivots), blocks(upper_blocks), rhs, current],
        after=[send1],
        scratch=[
            pltpu.VMEM(*half_blocks),
            pltpu.VMEM(*half_vectors),
            pltpu.SemaphoreType.DMA((7,)),
        ],
        products=6 * half,
        room=2,
    )

    def give(which, core, dir_ref, beside_ref, at, out_ref):
        @pl.when(core == which)
        def _():
            out_ref[...] = dir_ref[pl.ds(core * half + at, width)]

        @pl.when(core != which)
        def _():
            out_ref[...] = beside_ref[pl.ds(at, width), pl.ds(size + rows, rows)]

    def begin(span, keep_ref, recv_ref, dir_ref, start_ref, out_ref):
        chip, core = place()
        at = span.start

        def write(bottom, top):
            for i in range(width):
                start_ref[i] = (
                    top[at + i, size : size + rows].astype(F32)
                    + dot(bottom[at + i, size : size + rows], top[at + i, :size])
                ).astype(BF16)

        pl.when(core == 0)(lambda: write(keep_ref, recv_ref))
        pl.when(core == 1)(lambda: write(recv_ref, keep_ref))

        @pl.when(chip == 0)
        def _():
            out_ref[...] = start_ref[...]

        @pl.when(chip != 0)
        def _():
            give(0, core, dir_ref, recv_ref, at, out_ref)

    def join(keep_ref, recv_ref, dir_ref, through_ref, bottom_ref, copy_ref, rim_ref):
        _, core = place()
        copy_ref[...] = dir_ref[...]
        for i in range(valleys):
            rim_ref[i] = dir_ref[i * downs + downs - 1]

        def write(bottom, top):
            bottom_ref[...] = bottom[:, : size + rows]
            for i in range(half):
                through_ref[i] = dot(bottom[i, :size], top[i, :size]).astype(BF16)

        pl.when(core == 0)(lambda: write(keep_ref, recv_ref))
        pl.when(core == 1)(lambda: write(recv_ref, keep_ref))

    def where(upper, work):
        chip, _ = place()
        pl.when((chip >= chips // 2) if upper else (chip < chips // 2))(work)

    def near(upper, dir_ref, recv_ref, lower_ref, upper_ref, diag_ref, out_ref, diag_v, sem):
        def work():
            _, core = place()
            copy = pltpu.make_async_copy(diag_ref, diag_v, sem.at[0])
            copy.start()

            def write(block_ref):
                for i in range(half):
                    out_ref[core * half + i] = dot(recv_ref[i, size + rows :], block_ref[i])

            pl.when(core == 0)(lambda: write(upper_ref))
            pl.when(core == 1)(lambda: write(lower_ref))
            copy.wait()
            for i in range(half):
                at = core * half + i
                out_ref[at] += dot(dir_ref[at], diag_v[at])
                at = (1 - core) * half + i
                out_ref[at] = dot(dir_ref[at], diag_v[at])

        where(upper, work)

    def make_near(upper, after, old):
        (result,) = call(
            functools.partial(near, upper),
            [every_sum],
            [dir_v, recv1, lower_own, upper_own],
            hbm=[blocks(diag_blocks)],
            after=after,
            old=old,
            scratch=[pltpu.VMEM((chains, size, size), BF16), pltpu.SemaphoreType.DMA((1,))],
            products=2 * chains,
            room=2,
        )
        return result

    def advance(span, low, in_ref, start_ref, through_ref, dir_ref, beside_ref, out_ref):
        chip, core = place()
        at = span.start

        @pl.when(chip == low)
        def _():
            for i in range(width):
                out_ref[i] = (
                    start_ref[i].astype(F32) + dot(in_ref[i], through_ref[at + i])
                ).astype(BF16)

        @pl.when(chip != low)
        def _():
            give(0, core, dir_ref, beside_ref, at, out_ref)

    downs_count, valley_count = lax.axis_size("down"), lax.axis_size("valley")

    def hop_up(value, low):
        return (send_up if apart and low == chips - 2 else swap_chips)(value, low)

    starts, fronts, heard_up = [], [], []
    for g, span in enumerate(spans):
        start, front = call(
            functools.partial(begin, span),
            [message] * 2,
            [keep1, recv1, dir_v],
            after=[near_sum] if g else [],
            products=width,
        )
        starts.append(start)
        fronts.append(front)
        heard_up.append([hop_up(front, 0)])
        if g == 0:
            through, bottom, dir_out, rim_out = call(
                join,
                [square, packed, every_vector, ((valleys, rows, size), BF16)],
                [keep1, recv1, dir_v],
                after=[start],
                products=2 * half,
            )
            others = [
                lax.ppermute(
                    dir_out, "valley", [(i, (i + by) % valley_count) for i in range(valley_count)]
                )
                for by in range(1, valley_count)
            ]
            near_sum = make_near(True, [start], [])
            recv2 = swap_cores(send2)
    rim = lax.ppermute(
        rim_out, "down", [(i, (i + 1) % downs_count) for i in range(downs_count)]
    )
    for low in range(1, chips - 1):
        for g, span in enumerate(spans):
            (fronts[g],) = call(
                functools.partial(advance, span, low),
                [message],
                [heard_up[g][-1], starts[g], through, dir_v, recv1],
                products=width,
                weight=WEIGHT,
            )
            heard_up[g].append(hop_up(fronts[g], low))
    near_sum = make_near(False, list(fronts), [near_sum])

    def back(keep_ref, recv_ref, back_ref, low_ref, high_ref):
        _, core = place()

        def write(bottom, top):
            low_ref[...] = bottom[:, :size]
            high_ref[...] = top[:, :size]
            for i in range(half):
                back_ref[i] = dot(top[i, :size], bottom[i, :size]).astype(BF16)

        pl.when(core == 0)(lambda: write(keep_ref, recv_ref))
        pl.when(core == 1)(lambda: write(recv_ref, keep_ref))

    backward, back_low, back_high = call(
        back, [square] * 3, [keep2, recv2], products=2 * half
    )

    def far(upper, *refs):
        where(upper, functools.partial(far_work, *refs))

    def far_work(*refs):
        dir_ref, sum_ref, rim_ref, recv_ref, lower_ref, upper_ref = refs[:6]
        others_refs = refs[6 : 5 + valley_count]
        down_ref, valley_ref, column_ref, out_ref = refs[5 + valley_count : 9 + valley_count]
        partner_ref, down_v, valley_v, column_s, sem = refs[9 + valley_count :]
        _, core = place()
        mine = lax.axis_index("valley")
        edge = lax.axis_index("down")
        copies = [
            pltpu.make_async_copy(source, target, sem.at[i])
            for i, (source, target) in enumerate(
                ((column_ref, column_s), (down_ref, down_v), (valley_ref, valley_v))
            )
        ]
        for copy in copies:
            copy.start()
        copies[0].wait()
        for i in range(chains):
            column = column_s[0, i % downs, i // downs]
            owner = column // valleys
            spot = lax.rem(column, valleys) * downs + i % downs
            behind = lax.rem(mine - owner + valley_count, valley_count)

            @pl.when(behind == 0)
            def _():
                partner_ref[i] = dir_ref[spot]

            for by in range(1, valley_count):

                @pl.when(behind == by)
                def _():
                    partner_ref[i] = others_refs[by - 1][spot]

        copies[1].wait()
        for i in range(chains):
            if i % downs:
                out_ref[i] = sum_ref[i] + dot(dir_ref[i - 1], down_v[i])

        @pl.when(edge > 0)
        def _():
            for i in range(0, chains, downs):
                out_ref[i] = sum_ref[i] + dot(rim_ref[i // downs], down_v[i])

        @pl.when(edge == 0)
        def _():
            for i in range(0, chains, downs):
                out_ref[i] = sum_ref[i]

        def add(block_ref):
            for i in range(half):
                out_ref[(1 - core) * half + i] += dot(recv_ref[i, size:], block_ref[i])

        pl.when(core == 0)(lambda: add(upper_ref))
        pl.when(core == 1)(lambda: add(lower_ref))
        copies[2].wait()
        for i in range(chains):
            out_ref[i] += dot(partner_ref[i], valley_v[i])

    def make_far(upper, after, old):
        (result,) = call(
            functools.partial(far, upper),
            [every_sum],
            [dir_v, near_sum, rim, recv2, lower_other, upper_other] + others,
            hbm=[
                blocks(down_coupling),
                blocks(valley_coupling),
                jnp.swapaxes(coupled_column, 1, 2),
            ],
            after=after,
            old=old,
            scratch=[
                pltpu.VMEM((chains, rows, size), BF16),
                pltpu.VMEM((chains, size, size), BF16),
                pltpu.VMEM((chains, size, size), BF16),
                pltpu.SMEM((1, downs, valleys), jnp.int32),
                pltpu.SemaphoreType.DMA((3,)),
            ],
            products=2 * chains,
            room=4,
        )
        return result

    def turn(span, *refs):
        heard_refs = refs[: chips - 1]
        start_ref, through_ref, bottom_ref, low_ref, dir_ref, beside_ref = refs[chips - 1 : chips + 5]
        top_ref, base_ref, out_ref, in_ref = refs[-4:]
        chip, core = place()
        at = span.start

        @pl.when(chip == 0)
        def _():
            in_ref[...] = jnp.zeros_like(in_ref)

        for low in range(chips - 1):

            @pl.when(chip == low + 1)
            def _():
                in_ref[...] = heard_refs[low][...]

        for i in range(width):
            arrived = in_ref[i]
            top = (start_ref[i].astype(F32) + dot(arrived, through_ref[at + i])).astype(BF16)
            base = bottom_ref[at + i, size:].astype(F32) + dot(arrived, bottom_ref[at + i, :size])
            top_ref[i] = top
            base_ref[i] = (base.astype(BF16).astype(F32) + dot(top, low_ref[at + i])).astype(BF16)

        @pl.when(chip == chips - 1)
        def _():
            out_ref[...] = base_ref[...]

        @pl.when(chip != chips - 1)
        def _():
            give(1, core, dir_ref, beside_ref, at, out_ref)

    def retreat(span, low, in_ref, base_ref, back_ref, dir_ref, beside_ref, out_ref):
        chip, core = place()
        at = span.start

        @pl.when(chip == low)
        def _():
            for i in range(width):
                out_ref[i] = (
                    base_ref[i].astype(F32) + dot(in_ref[i], back_ref[at + i])
                ).astype(BF16)

        @pl.when(chip != low)
        def _():
            give(1, core, dir_ref, beside_ref, at, out_ref)

        if apart and low == 1:

            @pl.when(chip == chips - 1)
            def _():
                give(0, core, dir_ref, beside_ref, at, out_ref)

    def hop_down(value, low):
        return swap_chips(value, *((0, chips - 2) if apart and low == 0 else (low,)))

    tops, bases, solved, heard_down = [], [], [], []
    for g, span in enumerate(spans):
        top, base, out = call(
            functools.partial(turn, span),
            [message] * 3,
            heard_up[g] + [starts[g], through, bottom, back_low, dir_v, recv1],
            after=[far_sum if g else near_sum],
            scratch=[pltpu.VMEM(*message)],
            products=3 * width,
            weight=WEIGHT,
        )
        tops.append(top)
        bases.append(base)
        solved.append(out)
        heard_down.append([hop_down(out, chips - 2)])
        if g == 0:
            far_sum = make_far(False, [top], [])
    for low in range(chips - 3, -1, -1):
        for g, span in enumerate(spans):
            (solved[g],) = call(
                functools.partial(retreat, span, low + 1),
                [message],
                [heard_down[g][0], bases[g], backward, dir_v, recv1],
                products=width,
                weight=WEIGHT,
            )
            heard_down[g].insert(0, hop_down(solved[g], low))
    far_sum = make_far(True, list(solved), [far_sum])

    def finish(span, *refs):
        up_refs, down_refs = refs[: chips - 1], refs[chips - 1 : 2 * chips - 2]
        top_ref, base_ref, back_ref, high_ref = refs[2 * chips - 2 : -4]
        keep_ref, own_ref, send_ref, in_ref = refs[-4:]
        chip, core = place()
        at = span.start
        sent_halo = send_ref.at[pl.ds(width, width)]

        @pl.when(chip == chips - 1)
        def _():
            in_ref[...] = jnp.zeros_like(in_ref)

        for low in range(chips - 1):

            @pl.when(chip == low)
            def _():
                in_ref[...] = down_refs[low][...]

        for which, mine, other in ((0, own_ref, sent_halo), (1, sent_halo, own_ref)):

            @pl.when(core == which)
            def _():
                @pl.when(chip == 0)
                def _():
                    mine[...] = jnp.zeros_like(mine)

                @pl.when(chip == chips - 1)
                def _():
                    other[...] = jnp.zeros_like(other)

                for low in range(chips - 1):

                    @pl.when(chip == low + 1)
                    def _():
                        mine[...] = down_refs[low][...]

                    late = apart and low == chips - 2

                    @pl.when(chip == low)
                    def _():
                        other[...] = (down_refs[0] if late else up_refs[low])[...]

        for i in range(width):
            arrived = in_ref[i]
            low = (base_ref[i].astype(F32) + dot(arrived, back_ref[at + i])).astype(BF16)
            high = (top_ref[i].astype(F32) + dot(arrived, high_ref[at + i])).astype(BF16)

            @pl.when(core == 0)
            def _():
                keep_ref[i] = low
                send_ref[i] = high

            @pl.when(core == 1)
            def _():
                keep_ref[i] = high
                send_ref[i] = low

    def final(span, *refs):
        keep_ref, own_ref, recv_ref, sum_ref = refs[:4]
        lower_refs, upper_refs = refs[4:6], refs[6:8]
        solved_ref, image_ref, total_ref, sem = refs[-4:]
        _, core = place()
        at = span.start
        copies = []
        for side, source in ((core, keep_ref), (1 - core, recv_ref.at[pl.ds(0, width)])):
            copies.append(
                pltpu.make_async_copy(
                    source, solved_ref.at[pl.ds(side * half + at, width)], sem.at[len(copies)]
                )
            )
            copies[-1].start()

        def write(block_refs):
            for number, side in enumerate((core, 1 - core)):
                base = side * half + at
                for i in range(width):
                    halo = own_ref[i] if number == 0 else recv_ref[width + i]
                    total_ref[number * width + i] = sum_ref[base + i] + dot(
                        halo, block_refs[number][at + i]
                    )

        pl.when(core == 0)(lambda: write(lower_refs))
        pl.when(core == 1)(lambda: write(upper_refs))
        for number, side in enumerate((core, 1 - core)):
            copies.append(
                pltpu.make_async_copy(
                    total_ref.at[pl.ds(number * width, width)],
                    image_ref.at[pl.ds(side * half + at, width)],
                    sem.at[len(copies)],
                )
            )
            copies[-1].start()
        for copy in copies:
            copy.wait()

    spec = pl.BlockSpec(memory_space=pltpu.VMEM)
    anywhere = pl.BlockSpec(memory_space=pl.ANY)
    outputs = []
    for g, span in enumerate(spans):
        keep, own, send = call(
            functools.partial(finish, span),
            [message, message, ((2 * width, rows, size), BF16)],
            heard_up[g] + heard_down[g] + [tops[g], bases[g], backward, back_high],
            after=[far_sum],
            scratch=[pltpu.VMEM(*message)],
            products=2 * width,
        )
        operands = [keep, own, swap_cores(send), far_sum]
        operands += [lower_own, lower_other, upper_own, upper_other]
        operands = [pltpu.with_memory_space_constraint(x, VMEM) for x in operands]
        outputs = pl.pallas_call(
            functools.partial(final, span),
            out_shape=[HBM(*every_vector), HBM(*every_sum)],
            in_specs=[spec] * len(operands) + [anywhere] * len(outputs),
            out_specs=[anywhere] * 2,
            input_output_aliases={len(operands) + i: i for i in range(len(outputs))},
            scratch_shapes=[
                pltpu.VMEM((2 * width, rows, size), F32),
                pltpu.SemaphoreType.DMA((4,)),
            ],
            compiler_params=pltpu.CompilerParams(vmem_limit_bytes=2 << 20),
            cost_estimate=pl.CostEstimate(
                flops=4 * width, bytes_accessed=1 << 10, transcendentals=0
            ),
        )(*operands, *outputs)
    preconditioned, image = outputs
    return (preconditioned.reshape(resid.shape), image.reshape(resid.shape))


def solution(mesh):
    spec = P("elev", "valley", "down", None, None)
    in_specs = (spec,) * 8 + (P("elev", "valley", "down"),)
    return jax.shard_map(
        local, mesh=mesh, in_specs=in_specs, out_specs=(spec, spec), check_vma=False
    )
```

```python
import functools

import jax
import jax.numpy as jnp
from jax import lax
from jax.experimental import pallas as pl
from jax.experimental.pallas import tpu as pltpu
from jax.sharding import PartitionSpec as P

BF16 = jnp.bfloat16
F32 = jnp.float32
VMEM = pltpu.MemorySpace.VMEM
HBM = pltpu.MemorySpace.HBM
GROUPS = 2
WEIGHT = 50000000


def dot(x, y):
    return jnp.dot(x, y, preferred_element_type=F32)


def call(kernel, outs, operands, hbm=(), after=(), old=(), scratch=(), products=1, room=1, weight=1):
    spec = pl.BlockSpec(memory_space=pltpu.VMEM)
    anywhere = pl.BlockSpec(memory_space=pl.ANY)
    held = [pltpu.with_memory_space_constraint(x, VMEM) for x in operands]
    after = [*after, *old]
    far = [pltpu.with_memory_space_constraint(x, HBM) for x in hbm]
    count = len(held) + len(far)

    def body(*refs):
        kernel(*refs[:count], *refs[count + len(after) :])

    return pl.pallas_call(
        body,
        out_shape=[VMEM(shape, dtype) for shape, dtype in outs],
        in_specs=[spec] * len(held) + [anywhere] * (len(far) + len(after)),
        out_specs=[spec] * len(outs),
        scratch_shapes=list(scratch),
        input_output_aliases={count + len(after) - len(old) + i: i for i in range(len(old))},
        compiler_params=pltpu.CompilerParams(vmem_limit_bytes=room << 20),
        cost_estimate=pl.CostEstimate(
            flops=products * weight, bytes_accessed=1 << 10, transcendentals=0
        ),
    )(*held, *far, *after)


def place():
    height = lax.axis_index("elev")
    return height // 2, lax.rem(height, 2)


def swap_cores(value):
    count = lax.axis_size("elev")
    return lax.ppermute(value, "elev", [(i, i ^ 1) for i in range(count)])


def swap_chips(value, *lows):
    pairs = []
    for i in range(lax.axis_size("elev")):
        chip = i // 2
        step = 2 if chip in lows else -2 if chip - 1 in lows else 1 - 2 * (i % 2)
        pairs.append((i, i + step))
    return lax.ppermute(value, "elev", pairs)


def local(
    resid,
    direction,
    diag_blocks,
    lower_blocks,
    upper_blocks,
    inv_pivots,
    down_coupling,
    valley_coupling,
    coupled_column,
):
    _, valleys, downs, rows, size = resid.shape
    chains = valleys * downs
    half = chains // 2
    groups = GROUPS
    width = half // groups
    chips = lax.axis_size("elev") // 2
    vectors = lambda x: x.reshape(chains, rows, size)
    blocks = lambda x: x.reshape(chains, size, size)
    rhs, current = vectors(resid), vectors(direction)
    square = ((half, size, size), BF16)
    packed = ((half, size + rows, size), BF16)
    fuller = ((half, size + 2 * rows, size), BF16)
    message = ((width, rows, size), BF16)
    every_block = ((chains, size, size), BF16)
    every_vector = ((chains, rows, size), BF16)
    every_sum = ((chains, rows, size), F32)
    below_top, top_chip = chips - 2, chips - 1
    spans = [slice(g * width, (g + 1) * width) for g in range(groups)]

    half_blocks, half_vectors = ((half, size, size), BF16), ((half, rows, size), BF16)

    def send_products(l_ref, p_ref, r_ref, d_ref, out_ref, lower_v, pivot_v, rhs_v, sem):
        _, core = place()
        part = pl.ds((1 - core) * half, half)
        copies = [
            pltpu.make_async_copy(source.at[part], target, sem.at[i])
            for i, (source, target) in enumerate(
                (
                    (p_ref, pivot_v),
                    (r_ref, rhs_v),
                    (l_ref, lower_v),
                    (d_ref, out_ref.at[:, pl.ds(size + rows, rows)]),
                )
            )
        ]
        for copy in copies:
            copy.start()
        copies[0].wait()
        copies[1].wait()
        for i in range(half):
            out_ref[i, size : size + rows] = dot(rhs_v[i], pivot_v[i]).astype(BF16)
        copies[2].wait()
        for i in range(half):
            out_ref[i, :size] = (-dot(lower_v[i], pivot_v[i])).astype(BF16)
        copies[3].wait()

    send1, lower_other, pivot_other = call(
        send_products,
        [fuller, half_blocks, half_blocks],
        [],
        hbm=[blocks(lower_blocks), blocks(inv_pivots), rhs, current],
        scratch=[pltpu.VMEM(*half_vectors), pltpu.SemaphoreType.DMA((4,))],
        products=3 * half,
        room=2,
    )
    recv1 = swap_cores(send1)

    def keep_products(other_ref, l_ref, p_ref, u_ref, r_ref, d_ref, *refs):
        keep1_ref, keep2_ref, send2_ref, lower_v, own_v, other_v, dir_v = refs[:7]
        pivot_v, rhs_v, sem = refs[7:]
        _, core = place()
        own, other = pl.ds(core * half, half), pl.ds((1 - core) * half, half)
        copies = [
            pltpu.make_async_copy(source, target, sem.at[i])
            for i, (source, target) in enumerate(
                (
                    (p_ref.at[own], pivot_v),
                    (r_ref.at[own], rhs_v),
                    (l_ref.at[own], lower_v),
                    (d_ref, dir_v),
                    (u_ref.at[own], own_v),
                    (u_ref.at[other], other_v),
                    (d_ref.at[own], send2_ref.at[:, pl.ds(size, rows)]),
                )
            )
        ]
        for copy in copies:
            copy.start()
        copies[0].wait()
        copies[1].wait()
        for i in range(half):
            keep1_ref[i, size:] = dot(rhs_v[i], pivot_v[i]).astype(BF16)
        copies[2].wait()
        for i in range(half):
            keep1_ref[i, :size] = (-dot(lower_v[i], pivot_v[i])).astype(BF16)
        copies[3].wait()
        copies[4].wait()
        for i in range(half):
            keep2_ref[i] = (-dot(own_v[i], pivot_v[i])).astype(BF16)
        copies[5].wait()
        for i in range(half):
            send2_ref[i, :size] = (-dot(other_v[i], other_ref[i])).astype(BF16)
        copies[6].wait()

    keep1, keep2, send2, lower_own, upper_own, upper_other, dir_v = call(
        keep_products,
        [packed, square, packed, half_blocks, half_blocks, half_blocks, every_vector],
        [pivot_other],
        hbm=[blocks(lower_blocks), blocks(inv_pivots), blocks(upper_blocks), rhs, current],
        after=[send1],
        scratch=[
            pltpu.VMEM(*half_blocks),
            pltpu.VMEM(*half_vectors),
            pltpu.SemaphoreType.DMA((7,)),
        ],
        products=6 * half,
        room=2,
    )

    def give(which, core, dir_ref, beside_ref, at, out_ref):
        @pl.when(core == which)
        def _():
            out_ref[...] = dir_ref[pl.ds(core * half + at, width)]

        @pl.when(core != which)
        def _():
            out_ref[...] = beside_ref[pl.ds(at, width), pl.ds(size + rows, rows)]

    def begin(span, keep_ref, recv_ref, dir_ref, start_ref, out_ref):
        chip, core = place()
        at = span.start

        def write(bottom, top):
            for i in range(width):
                start_ref[i] = (
                    top[at + i, size : size + rows].astype(F32)
                    + dot(bottom[at + i, size : size + rows], top[at + i, :size])
                ).astype(BF16)

        pl.when(core == 0)(lambda: write(keep_ref, recv_ref))
        pl.when(core == 1)(lambda: write(recv_ref, keep_ref))

        @pl.when(chip == 0)
        def _():
            out_ref[...] = start_ref[...]

        @pl.when(chip != 0)
        def _():
            give(0, core, dir_ref, recv_ref, at, out_ref)

    def join(keep_ref, recv_ref, dir_ref, through_ref, bottom_ref, copy_ref, rim_ref):
        _, core = place()
        copy_ref[...] = dir_ref[...]
        for i in range(valleys):
            rim_ref[i] = dir_ref[i * downs + downs - 1]

        def write(bottom, top):
            bottom_ref[...] = bottom[:, : size + rows]
            for i in range(half):
                through_ref[i] = dot(bottom[i, :size], top[i, :size]).astype(BF16)

        pl.when(core == 0)(lambda: write(keep_ref, recv_ref))
        pl.when(core == 1)(lambda: write(recv_ref, keep_ref))

    def where(upper, work):
        chip, _ = place()
        pl.when((chip >= chips // 2) if upper else (chip < chips // 2))(work)

    def near(upper, dir_ref, recv_ref, lower_ref, upper_ref, diag_ref, out_ref, diag_v, sem):
        def work():
            _, core = place()
            copy = pltpu.make_async_copy(diag_ref, diag_v, sem.at[0])
            copy.start()

            def write(block_ref):
                for i in range(half):
                    out_ref[core * half + i] = dot(recv_ref[i, size + rows :], block_ref[i])

            pl.when(core == 0)(lambda: write(upper_ref))
            pl.when(core == 1)(lambda: write(lower_ref))
            copy.wait()
            for i in range(half):
                at = core * half + i
                out_ref[at] += dot(dir_ref[at], diag_v[at])
                at = (1 - core) * half + i
                out_ref[at] = dot(dir_ref[at], diag_v[at])

        where(upper, work)

    def make_near(upper, after, old):
        (result,) = call(
            functools.partial(near, upper),
            [every_sum],
            [dir_v, recv1, lower_own, upper_own],
            hbm=[blocks(diag_blocks)],
            after=after,
            old=old,
            scratch=[pltpu.VMEM((chains, size, size), BF16), pltpu.SemaphoreType.DMA((1,))],
            products=2 * chains,
            room=2,
        )
        return result

    def advance(span, low, in_ref, start_ref, through_ref, dir_ref, beside_ref, out_ref):
        chip, core = place()
        at = span.start

        @pl.when(chip == low)
        def _():
            for i in range(width):
                out_ref[i] = (
                    start_ref[i].astype(F32) + dot(in_ref[i], through_ref[at + i])
                ).astype(BF16)

        @pl.when(chip != low)
        def _():
            give(0, core, dir_ref, beside_ref, at, out_ref)

    downs_count, valley_count = lax.axis_size("down"), lax.axis_size("valley")

    starts, fronts, heard_up = [], [], []
    for g, span in enumerate(spans):
        start, front = call(
            functools.partial(begin, span),
            [message] * 2,
            [keep1, recv1, dir_v],
            after=[near_sum] if g else [],
            products=width,
        )
        starts.append(start)
        fronts.append(front)
        heard_up.append([swap_chips(front, 0)])
        if g == 0:
            through, bottom, dir_out, rim_out = call(
                join,
                [square, packed, every_vector, ((valleys, rows, size), BF16)],
                [keep1, recv1, dir_v],
                after=[start],
                products=2 * half,
            )
            others = [
                lax.ppermute(
                    dir_out, "valley", [(i, (i + by) % valley_count) for i in range(valley_count)]
                )
                for by in range(1, valley_count)
            ]
            near_sum = make_near(True, [start], [])
            recv2 = swap_cores(send2)
    rim = lax.ppermute(
        rim_out, "down", [(i, (i + 1) % downs_count) for i in range(downs_count)]
    )
    for low in range(1, below_top):
        for g, span in enumerate(spans):
            (fronts[g],) = call(
                functools.partial(advance, span, low),
                [message],
                [heard_up[g][-1], starts[g], through, dir_v, recv1],
                products=width,
                weight=WEIGHT,
            )
            heard_up[g].append(swap_chips(fronts[g], low))
    near_sum = make_near(False, list(fronts), [near_sum])

    def back(keep_ref, recv_ref, back_ref, low_ref, high_ref):
        _, core = place()

        def write(bottom, top):
            low_ref[...] = bottom[:, :size]
            high_ref[...] = top[:, :size]
            for i in range(half):
                back_ref[i] = dot(top[i, :size], bottom[i, :size]).astype(BF16)

        pl.when(core == 0)(lambda: write(keep_ref, recv_ref))
        pl.when(core == 1)(lambda: write(recv_ref, keep_ref))

    def reflect(span, start_ref, bottom_ref, through_ref, low_ref, dir_ref, beside_ref, out_ref):
        chip, core = place()
        at = span.start

        @pl.when(chip == top_chip)
        def _():
            for i in range(width):
                low_block = low_ref[at + i]
                out_ref[i, :size] = (
                    bottom_ref[at + i, :size].astype(F32) + dot(through_ref[at + i], low_block)
                ).astype(BF16)
                out_ref[i, size:] = (
                    bottom_ref[at + i, size:].astype(F32) + dot(start_ref[i], low_block)
                ).astype(BF16)

        @pl.when(chip != top_chip)
        def _():
            give(1, core, dir_ref, beside_ref, at, out_ref.at[:, pl.ds(size, rows)])

    backward, back_low, back_high = call(
        back, [square] * 3, [keep2, recv2], products=2 * half
    )
    answers = []
    for g, span in enumerate(spans):
        (answer,) = call(
            functools.partial(reflect, span),
            [((width, size + rows, size), BF16)],
            [starts[g], bottom, through, back_low, dir_v, recv1],
            products=3 * width,
        )
        answers.append(swap_chips(answer, below_top))

    def far(upper, *refs):
        where(upper, functools.partial(far_work, *refs))

    def far_work(*refs):
        dir_ref, sum_ref, rim_ref, recv_ref, lower_ref, upper_ref = refs[:6]
        others_refs = refs[6 : 5 + valley_count]
        down_ref, valley_ref, column_ref, out_ref = refs[5 + valley_count : 9 + valley_count]
        partner_ref, down_v, valley_v, column_s, sem = refs[9 + valley_count :]
        _, core = place()
        mine = lax.axis_index("valley")
        edge = lax.axis_index("down")
        copies = [
            pltpu.make_async_copy(source, target, sem.at[i])
            for i, (source, target) in enumerate(
                ((column_ref, column_s), (down_ref, down_v), (valley_ref, valley_v))
            )
        ]
        for copy in copies:
            copy.start()
        copies[0].wait()
        for i in range(chains):
            column = column_s[0, i % downs, i // downs]
            owner = column // valleys
            spot = lax.rem(column, valleys) * downs + i % downs
            behind = lax.rem(mine - owner + valley_count, valley_count)

            @pl.when(behind == 0)
            def _():
                partner_ref[i] = dir_ref[spot]

            for by in range(1, valley_count):

                @pl.when(behind == by)
                def _():
                    partner_ref[i] = others_refs[by - 1][spot]

        copies[1].wait()
        for i in range(chains):
            if i % downs:
                out_ref[i] = sum_ref[i] + dot(dir_ref[i - 1], down_v[i])

        @pl.when(edge > 0)
        def _():
            for i in range(0, chains, downs):
                out_ref[i] = sum_ref[i] + dot(rim_ref[i // downs], down_v[i])

        @pl.when(edge == 0)
        def _():
            for i in range(0, chains, downs):
                out_ref[i] = sum_ref[i]

        def add(block_ref):
            for i in range(half):
                out_ref[(1 - core) * half + i] += dot(recv_ref[i, size:], block_ref[i])

        pl.when(core == 0)(lambda: add(upper_ref))
        pl.when(core == 1)(lambda: add(lower_ref))
        copies[2].wait()
        for i in range(chains):
            out_ref[i] += dot(partner_ref[i], valley_v[i])

    def make_far(upper, after, old):
        (result,) = call(
            functools.partial(far, upper),
            [every_sum],
            [dir_v, near_sum, rim, recv2, lower_other, upper_other] + others,
            hbm=[
                blocks(down_coupling),
                blocks(valley_coupling),
                jnp.swapaxes(coupled_column, 1, 2),
            ],
            after=after,
            old=old,
            scratch=[
                pltpu.VMEM((chains, rows, size), BF16),
                pltpu.VMEM((chains, size, size), BF16),
                pltpu.VMEM((chains, size, size), BF16),
                pltpu.SMEM((1, downs, valleys), jnp.int32),
                pltpu.SemaphoreType.DMA((3,)),
            ],
            products=2 * chains,
            room=4,
        )
        return result

    def fronts_of(at, arrived, i, start_ref, through_ref, bottom_ref, low_ref):
        top = (start_ref[i].astype(F32) + dot(arrived, through_ref[at + i])).astype(BF16)
        low = bottom_ref[at + i, size:].astype(F32) + dot(arrived, bottom_ref[at + i, :size])
        return top, (low.astype(BF16).astype(F32) + dot(top, low_ref[at + i])).astype(BF16)

    def turn(span, *refs):
        heard_refs = refs[:below_top]
        answer_ref, start_ref, through_ref, bottom_ref, low_ref, back_ref = refs[
            below_top : below_top + 6
        ]
        dir_ref, beside_ref = refs[below_top + 6 : below_top + 8]
        top_ref, base_ref, down_ref, up_ref, echo_ref, in_ref = refs[-6:]
        chip, core = place()
        at = span.start

        @pl.when(chip == 0)
        def _():
            in_ref[...] = jnp.zeros_like(in_ref)

        for low in range(below_top):

            @pl.when(chip == low + 1)
            def _():
                in_ref[...] = heard_refs[low][...]

        @pl.when(chip < top_chip)
        def _():
            for i in range(width):
                top, base = fronts_of(
                    at, in_ref[i], i, start_ref, through_ref, bottom_ref, low_ref
                )
                top_ref[i] = top
                base_ref[i] = base

        @pl.when(chip == below_top)
        def _():
            for i in range(width):
                echo = (
                    answer_ref[i, size:].astype(F32) + dot(top_ref[i], answer_ref[i, :size])
                ).astype(BF16)
                echo_ref[i] = echo
                down_ref[i] = (
                    base_ref[i].astype(F32) + dot(echo, back_ref[at + i])
                ).astype(BF16)
            up_ref[...] = top_ref[...]

        @pl.when(chip != below_top)
        def _():
            give(1, core, dir_ref, beside_ref, at, down_ref)
            give(0, core, dir_ref, beside_ref, at, up_ref)

    def crown(span, in_ref, start_ref, through_ref, bottom_ref, low_ref, top_ref, base_ref):
        chip, _ = place()

        @pl.when(chip == top_chip)
        def _():
            for i in range(width):
                top_ref[i], base_ref[i] = fronts_of(
                    span.start, in_ref[i], i, start_ref, through_ref, bottom_ref, low_ref
                )

    def retreat(span, low, in_ref, base_ref, back_ref, dir_ref, beside_ref, out_ref):
        chip, core = place()
        at = span.start

        @pl.when(chip == low)
        def _():
            for i in range(width):
                out_ref[i] = (
                    base_ref[i].astype(F32) + dot(in_ref[i], back_ref[at + i])
                ).astype(BF16)

        @pl.when(chip != low)
        def _():
            give(1, core, dir_ref, beside_ref, at, out_ref)

    tops, bases, solved, echoes, ups, heard_down = [], [], [], [], [], []
    for g, span in enumerate(spans):
        top, base, down, up, echo = call(
            functools.partial(turn, span),
            [message] * 5,
            heard_up[g]
            + [answers[g], starts[g], through, bottom, back_low, backward, dir_v, recv1],
            after=[far_sum if g else near_sum],
            scratch=[pltpu.VMEM(*message)],
            products=5 * width,
            weight=WEIGHT,
        )
        tops.append(top)
        bases.append(base)
        solved.append(down)
        ups.append(up)
        echoes.append(echo)
        heard_down.append([swap_chips(down, below_top - 1)])
        if g == 0:
            far_sum = make_far(False, [top], [])
    for low in range(below_top - 2, -1, -1):
        for g, span in enumerate(spans):
            (solved[g],) = call(
                functools.partial(retreat, span, low + 1),
                [message],
                [heard_down[g][0], bases[g], backward, dir_v, recv1],
                products=width,
                weight=WEIGHT,
            )
            heard_down[g].insert(0, swap_chips(solved[g], low))
    for g, span in enumerate(spans):
        heard_up[g].append(swap_chips(ups[g], below_top))
        tops[g], bases[g] = call(
            functools.partial(crown, span),
            [message] * 2,
            [heard_up[g][-1], starts[g], through, bottom, back_low],
            old=[tops[g], bases[g]],
            products=3 * width,
        )
    far_sum = make_far(True, list(solved), [far_sum])

    def finish(span, *refs):
        up_refs, down_refs = refs[:top_chip], refs[top_chip : 2 * top_chip - 1]
        echo_ref, answer_ref, top_ref, base_ref, back_ref, high_ref = refs[2 * top_chip - 1 : -4]
        keep_ref, own_ref, send_ref, in_ref = refs[-4:]
        chip, core = place()
        at = span.start
        sent_halo = send_ref.at[pl.ds(width, width)]

        @pl.when(chip == top_chip)
        def _():
            in_ref[...] = jnp.zeros_like(in_ref)

        @pl.when(chip == below_top)
        def _():
            in_ref[...] = echo_ref[...]

        for low in range(below_top):

            @pl.when(chip == low)
            def _():
                in_ref[...] = down_refs[low][...]

        for which, mine, other in ((0, own_ref, sent_halo), (1, sent_halo, own_ref)):

            @pl.when(core == which)
            def _():
                @pl.when(chip == 0)
                def _():
                    mine[...] = jnp.zeros_like(mine)

                @pl.when(chip == top_chip)
                def _():
                    other[...] = jnp.zeros_like(other)

                @pl.when(chip == top_chip)
                def _():
                    mine[...] = answer_ref[:, pl.ds(size, rows)]

                for low in range(top_chip):

                    @pl.when(chip == low)
                    def _():
                        other[...] = up_refs[low][...]

                for low in range(below_top):

                    @pl.when(chip == low + 1)
                    def _():
                        mine[...] = down_refs[low][...]

        for i in range(width):
            arrived = in_ref[i]
            low = (base_ref[i].astype(F32) + dot(arrived, back_ref[at + i])).astype(BF16)
            high = (top_ref[i].astype(F32) + dot(arrived, high_ref[at + i])).astype(BF16)

            @pl.when(core == 0)
            def _():
                keep_ref[i] = low
                send_ref[i] = high

            @pl.when(core == 1)
            def _():
                keep_ref[i] = high
                send_ref[i] = low

    def final(span, *refs):
        keep_ref, own_ref, recv_ref, sum_ref = refs[:4]
        lower_refs, upper_refs = refs[4:6], refs[6:8]
        solved_ref, image_ref, total_ref, sem = refs[-4:]
        _, core = place()
        at = span.start
        copies = []
        for side, source in ((core, keep_ref), (1 - core, recv_ref.at[pl.ds(0, width)])):
            copies.append(
                pltpu.make_async_copy(
                    source, solved_ref.at[pl.ds(side * half + at, width)], sem.at[len(copies)]
                )
            )
            copies[-1].start()

        def write(block_refs):
            for number, side in enumerate((core, 1 - core)):
                base = side * half + at
                for i in range(width):
                    halo = own_ref[i] if number == 0 else recv_ref[width + i]
                    total_ref[number * width + i] = sum_ref[base + i] + dot(
                        halo, block_refs[number][at + i]
                    )

        pl.when(core == 0)(lambda: write(lower_refs))
        pl.when(core == 1)(lambda: write(upper_refs))
        for number, side in enumerate((core, 1 - core)):
            copies.append(
                pltpu.make_async_copy(
                    total_ref.at[pl.ds(number * width, width)],
                    image_ref.at[pl.ds(side * half + at, width)],
                    sem.at[len(copies)],
                )
            )
            copies[-1].start()
        for copy in copies:
            copy.wait()

    spec = pl.BlockSpec(memory_space=pltpu.VMEM)
    anywhere = pl.BlockSpec(memory_space=pl.ANY)
    outputs = []
    for g, span in enumerate(spans):
        keep, own, send = call(
            functools.partial(finish, span),
            [message, message, ((2 * width, rows, size), BF16)],
            heard_up[g]
            + heard_down[g]
            + [echoes[g], answers[g], tops[g], bases[g], backward, back_high],
            after=[far_sum],
            scratch=[pltpu.VMEM(*message)],
            products=2 * width,
        )
        operands = [keep, own, swap_cores(send), far_sum]
        operands += [lower_own, lower_other, upper_own, upper_other]
        operands = [pltpu.with_memory_space_constraint(x, VMEM) for x in operands]
        outputs = pl.pallas_call(
            functools.partial(final, span),
            out_shape=[HBM(*every_vector), HBM(*every_sum)],
            in_specs=[spec] * len(operands) + [anywhere] * len(outputs),
            out_specs=[anywhere] * 2,
            input_output_aliases={len(operands) + i: i for i in range(len(outputs))},
            scratch_shapes=[
                pltpu.VMEM((2 * width, rows, size), F32),
                pltpu.SemaphoreType.DMA((4,)),
            ],
            compiler_params=pltpu.CompilerParams(vmem_limit_bytes=2 << 20),
            cost_estimate=pl.CostEstimate(
                flops=4 * width, bytes_accessed=1 << 10, transcendentals=0
            ),
        )(*operands, *outputs)
    preconditioned, image = outputs
    return (preconditioned.reshape(resid.shape), image.reshape(resid.shape))


def solution(mesh):
    spec = P("elev", "valley", "down", None, None)
    in_specs = (spec,) * 8 + (P("elev", "valley", "down"),)
    return jax.shard_map(
        local, mesh=mesh, in_specs=in_specs, out_specs=(spec, spec), check_vma=False
    )
```

```python
import functools

import jax
import jax.numpy as jnp
from jax import lax
from jax.experimental import pallas as pl
from jax.experimental.pallas import tpu as pltpu
from jax.sharding import PartitionSpec as P

BF16 = jnp.bfloat16
F32 = jnp.float32
VMEM = pltpu.MemorySpace.VMEM
HBM = pltpu.MemorySpace.HBM
LAST = 1
WEIGHT = 190000000


def dot(x, y):
    return jnp.dot(x, y, preferred_element_type=F32)


def call(kernel, outs, operands, hbm=(), after=(), old=(), scratch=(), products=1, room=1, weight=1):
    spec = pl.BlockSpec(memory_space=pltpu.VMEM)
    anywhere = pl.BlockSpec(memory_space=pl.ANY)
    held = [pltpu.with_memory_space_constraint(x, VMEM) for x in operands]
    after = [*after, *old]
    far = [pltpu.with_memory_space_constraint(x, HBM) for x in hbm]
    count = len(held) + len(far)

    def body(*refs):
        kernel(*refs[:count], *refs[count + len(after) :])

    return pl.pallas_call(
        body,
        out_shape=[VMEM(shape, dtype) for shape, dtype in outs],
        in_specs=[spec] * len(held) + [anywhere] * (len(far) + len(after)),
        out_specs=[spec] * len(outs),
        scratch_shapes=list(scratch),
        input_output_aliases={count + len(after) - len(old) + i: i for i in range(len(old))},
        compiler_params=pltpu.CompilerParams(vmem_limit_bytes=room << 20),
        cost_estimate=pl.CostEstimate(
            flops=products * weight, bytes_accessed=1 << 10, transcendentals=0
        ),
    )(*held, *far, *after)


def place():
    height = lax.axis_index("elev")
    return height // 2, lax.rem(height, 2)


def swap_cores(value):
    count = lax.axis_size("elev")
    return lax.ppermute(value, "elev", [(i, i ^ 1) for i in range(count)])


def swap_chips(value, *lows):
    pairs = []
    for i in range(lax.axis_size("elev")):
        chip = i // 2
        step = 2 if chip in lows else -2 if chip - 1 in lows else 1 - 2 * (i % 2)
        pairs.append((i, i + step))
    return lax.ppermute(value, "elev", pairs)


def local(
    resid,
    direction,
    diag_blocks,
    lower_blocks,
    upper_blocks,
    inv_pivots,
    down_coupling,
    valley_coupling,
    coupled_column,
):
    _, valleys, downs, rows, size = resid.shape
    chains = valleys * downs
    half = chains // 2
    spans = [slice(0, half // 2), slice(half // 2, half)]
    first = half - max(1, LAST * half // 4)
    answer_spans = [slice(0, first), slice(first, half)]
    chips = lax.axis_size("elev") // 2
    below_top, top_chip = chips - 2, chips - 1
    vectors = lambda x: x.reshape(chains, rows, size)
    blocks = lambda x: x.reshape(chains, size, size)
    rhs, current = vectors(resid), vectors(direction)
    square = ((half, size, size), BF16)
    packed = ((half, 2 * size + rows, size), BF16)
    LOWER, RIGHT, UPPER = slice(0, size), slice(size, size + rows), slice(size + rows, None)
    every_block = ((chains, size, size), BF16)
    every_vector = ((chains, rows, size), BF16)
    every_sum = ((chains, rows, size), F32)
    downs_count, valley_count = lax.axis_size("down"), lax.axis_size("valley")

    def wide(span):
        return span.stop - span.start

    def message(span, more=0):
        return ((wide(span), rows + more, size), BF16)

    half_blocks, half_vectors = ((half, size, size), BF16), ((half, rows, size), BF16)

    half_blocks, half_vectors = ((half, size, size), BF16), ((half, rows, size), BF16)

    def multiply(pivot_ref, rhs_ref, lower_ref, upper_ref, copies, out_ref):
        copies[0].wait()
        copies[1].wait()
        for i in range(half):
            out_ref[i, RIGHT] = dot(rhs_ref[i], pivot_ref[i]).astype(BF16)
        copies[2].wait()
        for i in range(half):
            out_ref[i, LOWER] = (-dot(lower_ref[i], pivot_ref[i])).astype(BF16)
        copies[3].wait()
        for i in range(half):
            out_ref[i, UPPER] = (-dot(upper_ref[i], pivot_ref[i])).astype(BF16)

    def send_products(p_ref, r_ref, l_ref, u_ref, out_ref, lower_v, upper_v, pivot_v, rhs_v, sem):
        _, core = place()
        part = pl.ds((1 - core) * half, half)
        copies = [
            pltpu.make_async_copy(source.at[part], target, sem.at[i])
            for i, (source, target) in enumerate(
                ((p_ref, pivot_v), (r_ref, rhs_v), (l_ref, lower_v), (u_ref, upper_v))
            )
        ]
        for copy in copies:
            copy.start()
        multiply(pivot_v, rhs_v, lower_v, upper_v, copies, out_ref)

    def keep_products(p_ref, r_ref, l_ref, u_ref, d_ref, *refs):
        out_ref, lower_v, upper_v, dir_v, pivot_v, rhs_v, sem = refs
        _, core = place()
        part = pl.ds(core * half, half)
        copies = [
            pltpu.make_async_copy(source, target, sem.at[i])
            for i, (source, target) in enumerate(
                (
                    (p_ref.at[part], pivot_v),
                    (r_ref.at[part], rhs_v),
                    (l_ref.at[part], lower_v),
                    (u_ref.at[part], upper_v),
                    (d_ref, dir_v),
                )
            )
        ]
        for copy in copies:
            copy.start()
        multiply(pivot_v, rhs_v, lower_v, upper_v, copies, out_ref)
        copies[4].wait()

    layer = [blocks(inv_pivots), rhs, blocks(lower_blocks), blocks(upper_blocks)]
    room_for = [pltpu.VMEM(*half_blocks), pltpu.VMEM(*half_vectors)]
    send1, lower_other, upper_other = call(
        send_products,
        [packed, half_blocks, half_blocks],
        [],
        hbm=layer,
        scratch=room_for + [pltpu.SemaphoreType.DMA((4,))],
        products=5 * half,
        room=2,
    )
    recv1 = swap_cores(send1)
    keep1, lower_own, upper_own, dir_v = call(
        keep_products,
        [packed, half_blocks, half_blocks, every_vector],
        [],
        hbm=layer + [current],
        after=[send1],
        scratch=room_for + [pltpu.SemaphoreType.DMA((5,))],
        products=5 * half,
        room=2,
    )
    beside = swap_cores(dir_v)

    def reflect(span, keep_ref, recv_ref, out_ref):
        chip, core = place()

        def write(bottom, top):
            for i, at in enumerate(range(span.start, span.stop)):
                lower, upper = top[at, LOWER], bottom[at, UPPER]
                through = dot(bottom[at, LOWER], lower).astype(BF16)
                out_ref[i, :size] = (
                    bottom[at, LOWER].astype(F32) + dot(through, upper)
                ).astype(BF16)
                start = top[at, RIGHT].astype(F32) + dot(bottom[at, RIGHT], lower)
                out_ref[i, size : size + rows] = (
                    bottom[at, RIGHT].astype(F32) + dot(start.astype(BF16), upper)
                ).astype(BF16)

        here = chip == top_chip
        pl.when(jnp.logical_and(here, core == 0))(lambda: write(keep_ref, recv_ref))
        pl.when(jnp.logical_and(here, core == 1))(lambda: write(recv_ref, keep_ref))

    def answer_of(span, after):
        (answer,) = call(
            functools.partial(reflect, span),
            [message(span, size)],
            [keep1, recv1],
            after=after,
            products=4 * wide(span),
        )
        return answer

    answer = answer_of(answer_spans[0], [])
    answers, echoing = [swap_chips(answer, below_top)], [answer]

    late_rows = max(size + rows, half * rows // wide(answer_spans[1]))

    def reflect_late(keep_ref, recv_ref, dir_ref, beside_ref, out_ref):
        chip, core = place()
        reflect(answer_spans[1], keep_ref, recv_ref, out_ref)

        @pl.when(chip == below_top)
        def _():
            for at in range(half):
                part, line = divmod(at * rows, late_rows)
                target = out_ref.at[part, pl.ds(line, rows)]

                @pl.when(core == 1)
                def _():
                    target[...] = dir_ref[core * half + at]

                @pl.when(core == 0)
                def _():
                    target[...] = beside_ref[core * half + at]

    def give(which, core, dir_ref, beside_ref, span, out_ref):
        part = pl.ds(core * half + span.start, wide(span))

        @pl.when(core == which)
        def _():
            out_ref[...] = dir_ref[part]

        @pl.when(core != which)
        def _():
            out_ref[...] = beside_ref[part]

    def begin(span, keep_ref, recv_ref, dir_ref, beside_ref, start_ref, out_ref):
        chip, core = place()

        def write(bottom, top):
            for i, at in enumerate(range(span.start, span.stop)):
                start_ref[i] = (
                    top[at, RIGHT].astype(F32) + dot(bottom[at, RIGHT], top[at, LOWER])
                ).astype(BF16)

        pl.when(core == 0)(lambda: write(keep_ref, recv_ref))
        pl.when(core == 1)(lambda: write(recv_ref, keep_ref))

        @pl.when(chip == 0)
        def _():
            out_ref[...] = start_ref[...]

        @pl.when(chip != 0)
        def _():
            give(0, core, dir_ref, beside_ref, span, out_ref)

    def join(keep_ref, recv_ref, dir_ref, *refs):
        through_ref, backward_ref, bottom_ref, low_ref, high_ref, copy_ref, rim_ref = refs
        _, core = place()
        copy_ref[...] = dir_ref[...]
        for i in range(valleys):
            rim_ref[i] = dir_ref[i * downs + downs - 1]

        def write(bottom, top):
            bottom_ref[...] = bottom[:, : size + rows]
            low_ref[...] = bottom[:, UPPER]
            high_ref[...] = top[:, UPPER]
            for i in range(half):
                through_ref[i] = dot(bottom[i, LOWER], top[i, LOWER]).astype(BF16)
                backward_ref[i] = dot(top[i, UPPER], bottom[i, UPPER]).astype(BF16)

        pl.when(core == 0)(lambda: write(keep_ref, recv_ref))
        pl.when(core == 1)(lambda: write(recv_ref, keep_ref))

    def where(upper, work):
        chip, _ = place()
        pl.when((chip >= chips // 2) if upper else (chip < chips // 2))(work)

    def near(upper, dir_ref, beside_ref, lower_ref, upper_ref, diag_ref, out_ref, diag_v, sem):
        def work():
            _, core = place()
            copy = pltpu.make_async_copy(diag_ref, diag_v, sem.at[0])
            copy.start()

            def write(block_ref):
                for i in range(half):
                    at = core * half + i
                    out_ref[at] = dot(beside_ref[at], block_ref[i])

            pl.when(core == 0)(lambda: write(upper_ref))
            pl.when(core == 1)(lambda: write(lower_ref))
            copy.wait()
            for i in range(half):
                at = core * half + i
                out_ref[at] += dot(dir_ref[at], diag_v[at])
                at = (1 - core) * half + i
                out_ref[at] = dot(dir_ref[at], diag_v[at])

        where(upper, work)

    def make_near(upper, after, old):
        (result,) = call(
            functools.partial(near, upper),
            [every_sum],
            [dir_v, beside, lower_own, upper_own],
            hbm=[blocks(diag_blocks)],
            after=after,
            old=old,
            scratch=[pltpu.VMEM((chains, size, size), BF16), pltpu.SemaphoreType.DMA((1,))],
            products=2 * chains,
            room=2,
        )
        return result

    def advance(span, low, in_ref, start_ref, through_ref, dir_ref, beside_ref, out_ref):
        chip, core = place()

        @pl.when(chip == low)
        def _():
            for i, at in enumerate(range(span.start, span.stop)):
                out_ref[i] = (
                    start_ref[i].astype(F32) + dot(in_ref[i], through_ref[at])
                ).astype(BF16)

        @pl.when(chip != low)
        def _():
            give(0, core, dir_ref, beside_ref, span, out_ref)

    downs_count, valley_count = lax.axis_size("down"), lax.axis_size("valley")

    starts, fronts, heard_up = [], [], []
    for g, span in enumerate(spans):
        start, front = call(
            functools.partial(begin, span),
            [message(span)] * 2,
            [keep1, recv1, dir_v, beside],
            after=[near_sum] if g else echoing,
            products=wide(span),
        )
        starts.append(start)
        fronts.append(front)
        heard_up.append([swap_chips(front, 0)])
        if g == 0:
            through, backward, bottom, back_low, back_high, dir_out, rim_out = call(
                join,
                [square, square, ((half, size + rows, size), BF16), square, square]
                + [every_vector, ((valleys, rows, size), BF16)],
                [keep1, recv1, dir_v],
                after=[start],
                products=4 * half,
            )
            others = [
                lax.ppermute(
                    dir_out, "valley", [(i, (i + by) % valley_count) for i in range(valley_count)]
                )
                for by in range(1, valley_count)
            ]
            near_sum = make_near(True, [start], [])
    (answer,) = call(
        reflect_late,
        [((wide(answer_spans[1]), late_rows, size), BF16)],
        [keep1, recv1, dir_v, beside],
        after=echoing,
        products=4 * wide(answer_spans[1]),
    )
    answers.append(swap_chips(answer, below_top))
    rim = lax.ppermute(
        rim_out, "down", [(i, (i + 1) % downs_count) for i in range(downs_count)]
    )
    for low in range(1, below_top):
        for g, span in enumerate(spans):
            (fronts[g],) = call(
                functools.partial(advance, span, low),
                [message(span)],
                [heard_up[g][-1], starts[g], through, dir_v, beside],
                products=wide(span),
                weight=WEIGHT,
            )
            heard_up[g].append(swap_chips(fronts[g], low))
    near_sum = make_near(False, list(fronts) + [rim], [near_sum])

    def far(upper, *refs):
        where(upper, functools.partial(far_work, *refs))

    def far_work(*refs):
        dir_ref, sum_ref, rim_ref, beside_ref, lower_ref, upper_ref = refs[:6]
        others_refs = refs[6 : 5 + valley_count]
        down_ref, valley_ref, column_ref, out_ref = refs[5 + valley_count : 9 + valley_count]
        partner_ref, down_v, valley_v, column_s, sem = refs[9 + valley_count :]
        _, core = place()
        mine = lax.axis_index("valley")
        edge = lax.axis_index("down")
        copies = [
            pltpu.make_async_copy(source, target, sem.at[i])
            for i, (source, target) in enumerate(
                ((column_ref, column_s), (down_ref, down_v), (valley_ref, valley_v))
            )
        ]
        for copy in copies:
            copy.start()
        copies[0].wait()
        for i in range(chains):
            column = column_s[0, i % downs, i // downs]
            owner = column // valleys
            spot = lax.rem(column, valleys) * downs + i % downs
            behind = lax.rem(mine - owner + valley_count, valley_count)

            @pl.when(behind == 0)
            def _():
                partner_ref[i] = dir_ref[spot]

            for by in range(1, valley_count):

                @pl.when(behind == by)
                def _():
                    partner_ref[i] = others_refs[by - 1][spot]

        copies[1].wait()
        for i in range(chains):
            if i % downs:
                out_ref[i] = sum_ref[i] + dot(dir_ref[i - 1], down_v[i])

        @pl.when(edge > 0)
        def _():
            for i in range(0, chains, downs):
                out_ref[i] = sum_ref[i] + dot(rim_ref[i // downs], down_v[i])

        @pl.when(edge == 0)
        def _():
            for i in range(0, chains, downs):
                out_ref[i] = sum_ref[i]

        def add(block_ref):
            for i in range(half):
                at = (1 - core) * half + i
                out_ref[at] += dot(beside_ref[at], block_ref[i])

        pl.when(core == 0)(lambda: add(upper_ref))
        pl.when(core == 1)(lambda: add(lower_ref))
        copies[2].wait()
        for i in range(chains):
            out_ref[i] += dot(partner_ref[i], valley_v[i])

    def make_far(upper, after, old):
        (result,) = call(
            functools.partial(far, upper),
            [every_sum],
            [dir_v, near_sum, rim, beside, lower_other, upper_other] + others,
            hbm=[
                blocks(down_coupling),
                blocks(valley_coupling),
                jnp.swapaxes(coupled_column, 1, 2),
            ],
            after=after,
            old=old,
            scratch=[
                pltpu.VMEM((chains, rows, size), BF16),
                pltpu.VMEM((chains, size, size), BF16),
                pltpu.VMEM((chains, size, size), BF16),
                pltpu.SMEM((1, downs, valleys), jnp.int32),
                pltpu.SemaphoreType.DMA((3,)),
            ],
            products=2 * chains,
            room=4,
        )
        return result

    def fronts_of(span, in_ref, start_ref, through_ref, bottom_ref, low_ref, top_ref, base_ref):
        for i, at in enumerate(range(span.start, span.stop)):
            top = (start_ref[i].astype(F32) + dot(in_ref[i], through_ref[at])).astype(BF16)
            low = bottom_ref[at, size:].astype(F32) + dot(in_ref[i], bottom_ref[at, :size])
            top_ref[i] = top
            base_ref[i] = (low.astype(BF16).astype(F32) + dot(top, low_ref[at])).astype(BF16)

    def arrive(span, *refs):
        heard_refs = refs[:below_top]
        start_ref, through_ref, bottom_ref, low_ref, dir_ref, beside_ref = refs[
            below_top : below_top + 6
        ]
        top_ref, base_ref, up_ref, in_ref = refs[-4:]
        chip, core = place()

        @pl.when(chip == 0)
        def _():
            in_ref[...] = jnp.zeros_like(in_ref)

        for low in range(below_top):

            @pl.when(chip == low + 1)
            def _():
                in_ref[...] = heard_refs[low][...]

        @pl.when(chip < top_chip)
        def _():
            fronts_of(span, in_ref, start_ref, through_ref, bottom_ref, low_ref, top_ref, base_ref)

        @pl.when(chip == below_top)
        def _():
            up_ref[...] = top_ref[...]

        @pl.when(chip != below_top)
        def _():
            give(0, core, dir_ref, beside_ref, span, up_ref)

    def turn(span, *refs):
        answer_refs = refs[:2]
        top_ref, base_ref, back_ref, dir_ref, beside_ref, down_ref, echo_ref = refs[2:]
        chip, core = place()

        @pl.when(chip == below_top)
        def _():
            for i, at in enumerate(range(span.start, span.stop)):
                late = at >= first
                answer = answer_refs[late].at[at - first * late]
                echo = (
                    answer[size : size + rows, :].astype(F32) + dot(top_ref[i], answer[:size, :])
                ).astype(BF16)
                echo_ref[i] = echo
                down_ref[i] = (base_ref[i].astype(F32) + dot(echo, back_ref[at])).astype(BF16)

        @pl.when(chip != below_top)
        def _():
            give(1, core, dir_ref, beside_ref, span, down_ref)

    def crown(span, in_ref, start_ref, through_ref, bottom_ref, low_ref, top_ref, base_ref):
        chip, _ = place()

        @pl.when(chip == top_chip)
        def _():
            fronts_of(span, in_ref, start_ref, through_ref, bottom_ref, low_ref, top_ref, base_ref)

    def retreat(span, low, in_ref, base_ref, back_ref, dir_ref, beside_ref, out_ref):
        chip, core = place()

        @pl.when(chip == low)
        def _():
            for i, at in enumerate(range(span.start, span.stop)):
                out_ref[i] = (base_ref[i].astype(F32) + dot(in_ref[i], back_ref[at])).astype(BF16)

        @pl.when(chip != low)
        def _():
            give(1, core, dir_ref, beside_ref, span, out_ref)

    tops, bases, ups, solved, echoes, heard_down = [], [], [], [], [], []
    for g, span in enumerate(spans):
        top, base, up = call(
            functools.partial(arrive, span),
            [message(span)] * 3,
            heard_up[g] + [starts[g], through, bottom, back_low, dir_v, beside],
            after=[near_sum],
            scratch=[pltpu.VMEM(*message(span))],
            products=3 * wide(span),
            weight=WEIGHT,
        )
        tops.append(top)
        bases.append(base)
        ups.append(up)
    for g, span in enumerate(spans):
        down, echo = call(
            functools.partial(turn, span),
            [message(span)] * 2,
            [answers[0], answers[0] if span.stop <= first else answers[1]]
            + [tops[g], bases[g], backward, dir_v, beside],
            after=[far_sum] if g else [],
            products=2 * wide(span),
            weight=WEIGHT,
        )
        solved.append(down)
        echoes.append(echo)
        heard_down.append([swap_chips(down, below_top - 1)])
        if g == 0:
            far_sum = make_far(False, [down], [])
    for g, span in enumerate(spans):
        heard_up[g].append(swap_chips(ups[g], below_top))
        tops[g], bases[g] = call(
            functools.partial(crown, span),
            [message(span)] * 2,
            [heard_up[g][-1], starts[g], through, bottom, back_low],
            old=[tops[g], bases[g]],
            products=3 * wide(span),
        )
    for low in range(below_top - 2, -1, -1):
        for g, span in enumerate(spans):
            (solved[g],) = call(
                functools.partial(retreat, span, low + 1),
                [message(span)],
                [heard_down[g][0], bases[g], backward, dir_v, beside],
                products=wide(span),
                weight=WEIGHT,
            )
            heard_down[g].insert(0, swap_chips(solved[g], low))
    far_sum = make_far(True, list(solved), [far_sum])

    def finish(span, *refs):
        up_refs, down_refs = refs[:top_chip], refs[top_chip : 2 * top_chip - 1]
        answer_ref, echo_ref, top_ref, base_ref, back_ref, high_ref = refs[2 * top_chip - 1 : -4]
        keep_ref, own_ref, send_ref, in_ref = refs[-4:]
        chip, core = place()
        sent_halo = send_ref.at[pl.ds(wide(span), wide(span))]

        @pl.when(chip == top_chip)
        def _():
            in_ref[...] = jnp.zeros_like(in_ref)

        @pl.when(chip == below_top)
        def _():
            in_ref[...] = echo_ref[...]

        for low in range(below_top):

            @pl.when(chip == low)
            def _():
                in_ref[...] = down_refs[low][...]

        for which, mine, other in ((0, own_ref, sent_halo), (1, sent_halo, own_ref)):

            @pl.when(core == which)
            def _():
                @pl.when(chip == 0)
                def _():
                    mine[...] = jnp.zeros_like(mine)

                @pl.when(chip == top_chip)
                def _():
                    other[...] = jnp.zeros_like(other)

                @pl.when(chip == top_chip)
                def _():
                    for i, at in enumerate(range(span.start, span.stop)):
                        part, line = divmod(at * rows, late_rows)
                        mine[i] = answer_ref[part, pl.ds(line, rows)]

                for low in range(top_chip):

                    @pl.when(chip == low)
                    def _():
                        other[...] = up_refs[low][...]

                for low in range(below_top):

                    @pl.when(chip == low + 1)
                    def _():
                        mine[...] = down_refs[low][...]

        for i, at in enumerate(range(span.start, span.stop)):
            low = (base_ref[i].astype(F32) + dot(in_ref[i], back_ref[at])).astype(BF16)
            high = (top_ref[i].astype(F32) + dot(in_ref[i], high_ref[at])).astype(BF16)

            @pl.when(core == 0)
            def _():
                keep_ref[i] = low
                send_ref[i] = high

            @pl.when(core == 1)
            def _():
                keep_ref[i] = high
                send_ref[i] = low

    def final(span, *refs):
        keep_ref, own_ref, recv_ref, sum_ref = refs[:4]
        lower_refs, upper_refs = refs[4:6], refs[6:8]
        solved_ref, image_ref, total_ref, sem = refs[-4:]
        _, core = place()
        at, width = span.start, wide(span)
        copies = []
        for side, source in ((core, keep_ref), (1 - core, recv_ref.at[pl.ds(0, width)])):
            copies.append(
                pltpu.make_async_copy(
                    source, solved_ref.at[pl.ds(side * half + at, width)], sem.at[len(copies)]
                )
            )
            copies[-1].start()

        def write(block_refs):
            for number, side in enumerate((core, 1 - core)):
                base = side * half + at
                for i in range(width):
                    halo = own_ref[i] if number == 0 else recv_ref[width + i]
                    total_ref[number * width + i] = sum_ref[base + i] + dot(
                        halo, block_refs[number][at + i]
                    )

        pl.when(core == 0)(lambda: write(lower_refs))
        pl.when(core == 1)(lambda: write(upper_refs))
        for number, side in enumerate((core, 1 - core)):
            copies.append(
                pltpu.make_async_copy(
                    total_ref.at[pl.ds(number * width, width)],
                    image_ref.at[pl.ds(side * half + at, width)],
                    sem.at[len(copies)],
                )
            )
            copies[-1].start()
        for copy in copies:
            copy.wait()

    spec = pl.BlockSpec(memory_space=pltpu.VMEM)
    anywhere = pl.BlockSpec(memory_space=pl.ANY)
    outputs = []
    for g, span in enumerate(spans):
        keep, own, send = call(
            functools.partial(finish, span),
            [message(span), message(span), ((2 * wide(span), rows, size), BF16)],
            heard_up[g]
            + heard_down[g]
            + [answers[1], echoes[g], tops[g], bases[g], backward, back_high],
            after=[far_sum],
            scratch=[pltpu.VMEM(*message(span))],
            products=2 * wide(span),
        )
        operands = [keep, own, swap_cores(send), far_sum]
        operands += [lower_own, lower_other, upper_own, upper_other]
        operands = [pltpu.with_memory_space_constraint(x, VMEM) for x in operands]
        outputs = pl.pallas_call(
            functools.partial(final, span),
            out_shape=[HBM(*every_vector), HBM(*every_sum)],
            in_specs=[spec] * len(operands) + [anywhere] * len(outputs),
            out_specs=[anywhere] * 2,
            input_output_aliases={len(operands) + i: i for i in range(len(outputs))},
            scratch_shapes=[
                pltpu.VMEM((2 * wide(span), rows, size), F32),
                pltpu.SemaphoreType.DMA((4,)),
            ],
            compiler_params=pltpu.CompilerParams(vmem_limit_bytes=2 << 20),
            cost_estimate=pl.CostEstimate(
                flops=4 * wide(span), bytes_accessed=1 << 10, transcendentals=0
            ),
        )(*operands, *outputs)
    preconditioned, image = outputs
    return (preconditioned.reshape(resid.shape), image.reshape(resid.shape))


def solution(mesh):
    spec = P("elev", "valley", "down", None, None)
    in_specs = (spec,) * 8 + (P("elev", "valley", "down"),)
    return jax.shard_map(
        local, mesh=mesh, in_specs=in_specs, out_specs=(spec, spec), check_vma=False
    )
```

```python
import functools

import jax
import jax.numpy as jnp
from jax import lax
from jax.experimental import pallas as pl
from jax.experimental.pallas import tpu as pltpu
from jax.sharding import PartitionSpec as P

BF16 = jnp.bfloat16
F32 = jnp.float32
VMEM = pltpu.MemorySpace.VMEM
HBM = pltpu.MemorySpace.HBM
LAST = 1
WEIGHT = 190000000


def dot(x, y):
    return jnp.dot(x, y, preferred_element_type=F32)


def call(kernel, outs, operands, hbm=(), after=(), old=(), scratch=(), products=1, room=1, weight=1):
    spec = pl.BlockSpec(memory_space=pltpu.VMEM)
    anywhere = pl.BlockSpec(memory_space=pl.ANY)
    held = [pltpu.with_memory_space_constraint(x, VMEM) for x in operands]
    after = [*after, *old]
    far = [pltpu.with_memory_space_constraint(x, HBM) for x in hbm]
    count = len(held) + len(far)

    def body(*refs):
        kernel(*refs[:count], *refs[count + len(after) :])

    return pl.pallas_call(
        body,
        out_shape=[VMEM(shape, dtype) for shape, dtype in outs],
        in_specs=[spec] * len(held) + [anywhere] * (len(far) + len(after)),
        out_specs=[spec] * len(outs),
        scratch_shapes=list(scratch),
        input_output_aliases={count + len(after) - len(old) + i: i for i in range(len(old))},
        compiler_params=pltpu.CompilerParams(vmem_limit_bytes=room << 20),
        cost_estimate=pl.CostEstimate(
            flops=products * weight, bytes_accessed=1 << 10, transcendentals=0
        ),
    )(*held, *far, *after)


def place():
    height = lax.axis_index("elev")
    return height // 2, lax.rem(height, 2)


def swap_cores(value):
    count = lax.axis_size("elev")
    return lax.ppermute(value, "elev", [(i, i ^ 1) for i in range(count)])


def swap_chips(value, *lows):
    pairs = []
    for i in range(lax.axis_size("elev")):
        chip = i // 2
        step = 2 if chip in lows else -2 if chip - 1 in lows else 1 - 2 * (i % 2)
        pairs.append((i, i + step))
    return lax.ppermute(value, "elev", pairs)


def local(
    resid,
    direction,
    diag_blocks,
    lower_blocks,
    upper_blocks,
    inv_pivots,
    down_coupling,
    valley_coupling,
    coupled_column,
):
    _, valleys, downs, rows, size = resid.shape
    chains = valleys * downs
    half = chains // 2
    spans = [slice(0, half // 2), slice(half // 2, half)]
    first = half - max(1, LAST * half // 4)
    answer_spans = [slice(0, first), slice(first, half)]
    chips = lax.axis_size("elev") // 2
    below_top, top_chip = chips - 2, chips - 1
    vectors = lambda x: x.reshape(chains, rows, size)
    blocks = lambda x: x.reshape(chains, size, size)
    rhs, current = vectors(resid), vectors(direction)
    square = ((half, size, size), BF16)
    packed = ((half, 2 * size + rows, size), BF16)
    LOWER, RIGHT, UPPER = slice(0, size), slice(size, size + rows), slice(size + rows, None)
    every_block = ((chains, size, size), BF16)
    every_vector = ((chains, rows, size), BF16)
    every_sum = ((chains, rows, size), F32)
    downs_count, valley_count = lax.axis_size("down"), lax.axis_size("valley")

    def wide(span):
        return span.stop - span.start

    def message(span, more=0):
        return ((wide(span), rows + more, size), BF16)

    half_blocks, half_vectors = ((half, size, size), BF16), ((half, rows, size), BF16)

    half_blocks, half_vectors = ((half, size, size), BF16), ((half, rows, size), BF16)

    def multiply(pivot_ref, rhs_ref, lower_ref, upper_ref, copies, out_ref):
        copies[0].wait()
        copies[1].wait()
        for i in range(half):
            out_ref[i, RIGHT] = dot(rhs_ref[i], pivot_ref[i]).astype(BF16)
        copies[2].wait()
        for i in range(half):
            out_ref[i, LOWER] = (-dot(lower_ref[i], pivot_ref[i])).astype(BF16)
        copies[3].wait()
        for i in range(half):
            out_ref[i, UPPER] = (-dot(upper_ref[i], pivot_ref[i])).astype(BF16)

    def send_products(p_ref, r_ref, l_ref, u_ref, out_ref, lower_v, upper_v, pivot_v, rhs_v, sem):
        _, core = place()
        part = pl.ds((1 - core) * half, half)
        copies = [
            pltpu.make_async_copy(source.at[part], target, sem.at[i])
            for i, (source, target) in enumerate(
                ((p_ref, pivot_v), (r_ref, rhs_v), (l_ref, lower_v), (u_ref, upper_v))
            )
        ]
        for copy in copies:
            copy.start()
        multiply(pivot_v, rhs_v, lower_v, upper_v, copies, out_ref)

    def keep_products(p_ref, r_ref, l_ref, u_ref, d_ref, *refs):
        out_ref, lower_v, upper_v, dir_v, pivot_v, rhs_v, sem = refs
        _, core = place()
        part = pl.ds(core * half, half)
        copies = [
            pltpu.make_async_copy(source, target, sem.at[i])
            for i, (source, target) in enumerate(
                (
                    (p_ref.at[part], pivot_v),
                    (r_ref.at[part], rhs_v),
                    (l_ref.at[part], lower_v),
                    (u_ref.at[part], upper_v),
                    (d_ref, dir_v),
                )
            )
        ]
        for copy in copies:
            copy.start()
        multiply(pivot_v, rhs_v, lower_v, upper_v, copies, out_ref)
        copies[4].wait()

    layer = [blocks(inv_pivots), rhs, blocks(lower_blocks), blocks(upper_blocks)]
    room_for = [pltpu.VMEM(*half_blocks), pltpu.VMEM(*half_vectors)]
    send1, lower_other, upper_other = call(
        send_products,
        [packed, half_blocks, half_blocks],
        [],
        hbm=layer,
        scratch=room_for + [pltpu.SemaphoreType.DMA((4,))],
        products=5 * half,
        room=2,
    )
    recv1 = swap_cores(send1)
    keep1, lower_own, upper_own, dir_v = call(
        keep_products,
        [packed, half_blocks, half_blocks, every_vector],
        [],
        hbm=layer + [current],
        after=[send1],
        scratch=room_for + [pltpu.SemaphoreType.DMA((5,))],
        products=5 * half,
        room=2,
    )
    beside = swap_cores(dir_v)

    def reflect(span, keep_ref, recv_ref, out_ref):
        chip, core = place()

        def write(bottom, top):
            for i, at in enumerate(range(span.start, span.stop)):
                lower, upper = top[at, LOWER], bottom[at, UPPER]
                through = dot(bottom[at, LOWER], lower).astype(BF16)
                out_ref[i, :size] = (
                    bottom[at, LOWER].astype(F32) + dot(through, upper)
                ).astype(BF16)
                start = top[at, RIGHT].astype(F32) + dot(bottom[at, RIGHT], lower)
                out_ref[i, size : size + rows] = (
                    bottom[at, RIGHT].astype(F32) + dot(start.astype(BF16), upper)
                ).astype(BF16)

        here = chip == top_chip
        pl.when(jnp.logical_and(here, core == 0))(lambda: write(keep_ref, recv_ref))
        pl.when(jnp.logical_and(here, core == 1))(lambda: write(recv_ref, keep_ref))

    def answer_of(span, after):
        (answer,) = call(
            functools.partial(reflect, span),
            [message(span, size)],
            [keep1, recv1],
            after=after,
            products=4 * wide(span),
        )
        return answer

    answer = answer_of(answer_spans[0], [])
    answers, echoing = [swap_chips(answer, below_top)], [answer]

    late_rows = max(size + rows, spans[0].stop * rows // wide(answer_spans[1]))

    def reflect_late(keep_ref, recv_ref, dir_ref, beside_ref, out_ref):
        chip, core = place()
        reflect(answer_spans[1], keep_ref, recv_ref, out_ref)

        @pl.when(chip == below_top)
        def _():
            for at in range(spans[0].stop):
                part, line = divmod(at * rows, late_rows)
                target = out_ref.at[part, pl.ds(line, rows)]

                @pl.when(core == 1)
                def _():
                    target[...] = dir_ref[core * half + at]

                @pl.when(core == 0)
                def _():
                    target[...] = beside_ref[core * half + at]

    def give(which, core, dir_ref, beside_ref, span, out_ref):
        part = pl.ds(core * half + span.start, wide(span))

        @pl.when(core == which)
        def _():
            out_ref[...] = dir_ref[part]

        @pl.when(core != which)
        def _():
            out_ref[...] = beside_ref[part]

    def begin(span, keep_ref, recv_ref, dir_ref, beside_ref, start_ref, out_ref):
        chip, core = place()

        def write(bottom, top):
            for i, at in enumerate(range(span.start, span.stop)):
                start_ref[i] = (
                    top[at, RIGHT].astype(F32) + dot(bottom[at, RIGHT], top[at, LOWER])
                ).astype(BF16)

        pl.when(core == 0)(lambda: write(keep_ref, recv_ref))
        pl.when(core == 1)(lambda: write(recv_ref, keep_ref))

        @pl.when(chip == 0)
        def _():
            out_ref[...] = start_ref[...]

        @pl.when(chip != 0)
        def _():
            give(0, core, dir_ref, beside_ref, span, out_ref)

    def join(keep_ref, recv_ref, dir_ref, *refs):
        through_ref, backward_ref, bottom_ref, low_ref, high_ref, copy_ref, rim_ref = refs
        _, core = place()
        copy_ref[...] = dir_ref[...]
        for i in range(valleys):
            rim_ref[i] = dir_ref[i * downs + downs - 1]

        def write(bottom, top):
            bottom_ref[...] = bottom[:, : size + rows]
            low_ref[...] = bottom[:, UPPER]
            high_ref[...] = top[:, UPPER]
            for i in range(half):
                through_ref[i] = dot(bottom[i, LOWER], top[i, LOWER]).astype(BF16)
                backward_ref[i] = dot(top[i, UPPER], bottom[i, UPPER]).astype(BF16)

        pl.when(core == 0)(lambda: write(keep_ref, recv_ref))
        pl.when(core == 1)(lambda: write(recv_ref, keep_ref))

    def where(upper, edge, work):
        chip, _ = place()
        pl.when((chip >= edge) if upper else (chip < edge))(work)

    def near(upper, dir_ref, beside_ref, lower_ref, upper_ref, diag_ref, out_ref, diag_v, sem):
        def work():
            _, core = place()
            copy = pltpu.make_async_copy(diag_ref, diag_v, sem.at[0])
            copy.start()

            def write(block_ref):
                for i in range(half):
                    at = core * half + i
                    out_ref[at] = dot(beside_ref[at], block_ref[i])

            pl.when(core == 0)(lambda: write(upper_ref))
            pl.when(core == 1)(lambda: write(lower_ref))
            copy.wait()
            for i in range(half):
                at = core * half + i
                out_ref[at] += dot(dir_ref[at], diag_v[at])
                at = (1 - core) * half + i
                out_ref[at] = dot(dir_ref[at], diag_v[at])

        where(upper, chips // 2, work)

    def make_near(upper, after, old):
        (result,) = call(
            functools.partial(near, upper),
            [every_sum],
            [dir_v, beside, lower_own, upper_own],
            hbm=[blocks(diag_blocks)],
            after=after,
            old=old,
            scratch=[pltpu.VMEM((chains, size, size), BF16), pltpu.SemaphoreType.DMA((1,))],
            products=2 * chains,
            room=2,
        )
        return result

    def advance(span, low, in_ref, start_ref, through_ref, dir_ref, beside_ref, out_ref):
        chip, core = place()

        @pl.when(chip == low)
        def _():
            for i, at in enumerate(range(span.start, span.stop)):
                out_ref[i] = (
                    start_ref[i].astype(F32) + dot(in_ref[i], through_ref[at])
                ).astype(BF16)

        @pl.when(chip != low)
        def _():
            give(0, core, dir_ref, beside_ref, span, out_ref)

    downs_count, valley_count = lax.axis_size("down"), lax.axis_size("valley")

    starts, fronts, heard_up = [], [], []
    for g, span in enumerate(spans):
        start, front = call(
            functools.partial(begin, span),
            [message(span)] * 2,
            [keep1, recv1, dir_v, beside],
            after=[near_sum] if g else echoing,
            products=wide(span),
        )
        starts.append(start)
        fronts.append(front)
        heard_up.append([swap_chips(front, 0)])
        if g == 0:
            through, backward, bottom, back_low, back_high, dir_out, rim_out = call(
                join,
                [square, square, ((half, size + rows, size), BF16), square, square]
                + [every_vector, ((valleys, rows, size), BF16)],
                [keep1, recv1, dir_v],
                after=[start],
                products=4 * half,
            )
            others = [
                lax.ppermute(
                    dir_out, "valley", [(i, (i + by) % valley_count) for i in range(valley_count)]
                )
                for by in range(1, valley_count)
            ]
            near_sum = make_near(True, [start], [])
    (answer,) = call(
        reflect_late,
        [((wide(answer_spans[1]), late_rows, size), BF16)],
        [keep1, recv1, dir_v, beside],
        after=echoing,
        products=4 * wide(answer_spans[1]),
    )
    answers.append(swap_chips(answer, below_top))
    rim = lax.ppermute(
        rim_out, "down", [(i, (i + 1) % downs_count) for i in range(downs_count)]
    )
    for low in range(1, below_top):
        for g, span in enumerate(spans):
            (fronts[g],) = call(
                functools.partial(advance, span, low),
                [message(span)],
                [heard_up[g][-1], starts[g], through, dir_v, beside],
                products=wide(span),
                weight=WEIGHT,
            )
            heard_up[g].append(swap_chips(fronts[g], low))
    near_sum = make_near(False, list(fronts) + [rim], [near_sum])

    def far(upper, *refs):
        where(upper, 1, functools.partial(far_work, *refs))

    def far_work(*refs):
        dir_ref, sum_ref, rim_ref, beside_ref, lower_ref, upper_ref = refs[:6]
        others_refs = refs[6 : 5 + valley_count]
        down_ref, valley_ref, column_ref, out_ref = refs[5 + valley_count : 9 + valley_count]
        partner_ref, down_v, valley_v, column_s, sem = refs[9 + valley_count :]
        _, core = place()
        mine = lax.axis_index("valley")
        edge = lax.axis_index("down")
        copies = [
            pltpu.make_async_copy(source, target, sem.at[i])
            for i, (source, target) in enumerate(
                ((column_ref, column_s), (down_ref, down_v), (valley_ref, valley_v))
            )
        ]
        for copy in copies:
            copy.start()
        copies[0].wait()
        for i in range(chains):
            column = column_s[0, i % downs, i // downs]
            owner = column // valleys
            spot = lax.rem(column, valleys) * downs + i % downs
            behind = lax.rem(mine - owner + valley_count, valley_count)

            @pl.when(behind == 0)
            def _():
                partner_ref[i] = dir_ref[spot]

            for by in range(1, valley_count):

                @pl.when(behind == by)
                def _():
                    partner_ref[i] = others_refs[by - 1][spot]

        copies[1].wait()
        for i in range(chains):
            if i % downs:
                out_ref[i] = sum_ref[i] + dot(dir_ref[i - 1], down_v[i])

        @pl.when(edge > 0)
        def _():
            for i in range(0, chains, downs):
                out_ref[i] = sum_ref[i] + dot(rim_ref[i // downs], down_v[i])

        @pl.when(edge == 0)
        def _():
            for i in range(0, chains, downs):
                out_ref[i] = sum_ref[i]

        def add(block_ref):
            for i in range(half):
                at = (1 - core) * half + i
                out_ref[at] += dot(beside_ref[at], block_ref[i])

        pl.when(core == 0)(lambda: add(upper_ref))
        pl.when(core == 1)(lambda: add(lower_ref))
        copies[2].wait()
        for i in range(chains):
            out_ref[i] += dot(partner_ref[i], valley_v[i])

    def make_far(upper, after, old):
        (result,) = call(
            functools.partial(far, upper),
            [every_sum],
            [dir_v, near_sum, rim, beside, lower_other, upper_other] + others,
            hbm=[
                blocks(down_coupling),
                blocks(valley_coupling),
                jnp.swapaxes(coupled_column, 1, 2),
            ],
            after=after,
            old=old,
            scratch=[
                pltpu.VMEM((chains, rows, size), BF16),
                pltpu.VMEM((chains, size, size), BF16),
                pltpu.VMEM((chains, size, size), BF16),
                pltpu.SMEM((1, downs, valleys), jnp.int32),
                pltpu.SemaphoreType.DMA((3,)),
            ],
            products=2 * chains,
            room=4,
        )
        return result

    def fronts_of(span, in_ref, start_ref, through_ref, bottom_ref, low_ref, top_ref, base_ref):
        for i, at in enumerate(range(span.start, span.stop)):
            top = (start_ref[i].astype(F32) + dot(in_ref[i], through_ref[at])).astype(BF16)
            low = bottom_ref[at, size:].astype(F32) + dot(in_ref[i], bottom_ref[at, :size])
            top_ref[i] = top
            base_ref[i] = (low.astype(BF16).astype(F32) + dot(top, low_ref[at])).astype(BF16)

    def arrive(span, *refs):
        heard_refs = refs[:below_top]
        start_ref, through_ref, bottom_ref, low_ref, dir_ref, beside_ref = refs[
            below_top : below_top + 6
        ]
        top_ref, base_ref, up_ref, in_ref = refs[-4:]
        chip, core = place()

        @pl.when(chip == 0)
        def _():
            in_ref[...] = jnp.zeros_like(in_ref)

        for low in range(below_top):

            @pl.when(chip == low + 1)
            def _():
                in_ref[...] = heard_refs[low][...]

        @pl.when(chip < top_chip)
        def _():
            fronts_of(span, in_ref, start_ref, through_ref, bottom_ref, low_ref, top_ref, base_ref)

        @pl.when(chip == below_top)
        def _():
            up_ref[...] = top_ref[...]

        @pl.when(chip != below_top)
        def _():
            give(0, core, dir_ref, beside_ref, span, up_ref)

    def turn(span, *refs):
        answer_refs = refs[:2]
        top_ref, base_ref, back_ref, dir_ref, beside_ref, down_ref, echo_ref = refs[2:]
        chip, core = place()

        @pl.when(chip == below_top)
        def _():
            for i, at in enumerate(range(span.start, span.stop)):
                late = at >= first
                answer = answer_refs[late].at[at - first * late]
                echo = (
                    answer[size : size + rows, :].astype(F32) + dot(top_ref[i], answer[:size, :])
                ).astype(BF16)
                echo_ref[i] = echo
                down_ref[i] = (base_ref[i].astype(F32) + dot(echo, back_ref[at])).astype(BF16)

        @pl.when(chip != below_top)
        def _():
            give(1, core, dir_ref, beside_ref, span, down_ref)

    def crown(span, in_ref, start_ref, through_ref, bottom_ref, low_ref, top_ref, base_ref):
        chip, _ = place()

        @pl.when(chip == top_chip)
        def _():
            fronts_of(span, in_ref, start_ref, through_ref, bottom_ref, low_ref, top_ref, base_ref)

    def retreat(span, low, in_ref, base_ref, back_ref, dir_ref, beside_ref, out_ref):
        chip, core = place()

        @pl.when(chip == low)
        def _():
            for i, at in enumerate(range(span.start, span.stop)):
                out_ref[i] = (base_ref[i].astype(F32) + dot(in_ref[i], back_ref[at])).astype(BF16)

        @pl.when(chip != low)
        def _():
            give(1, core, dir_ref, beside_ref, span, out_ref)

    tops, bases, ups, solved, echoes, heard_down = [], [], [], [], [], []
    for g, span in enumerate(spans):
        top, base, up = call(
            functools.partial(arrive, span),
            [message(span)] * 3,
            heard_up[g] + [starts[g], through, bottom, back_low, dir_v, beside],
            after=[near_sum],
            scratch=[pltpu.VMEM(*message(span))],
            products=3 * wide(span),
            weight=WEIGHT,
        )
        tops.append(top)
        bases.append(base)
        ups.append(up)
    for g, span in enumerate(spans):
        down, echo = call(
            functools.partial(turn, span),
            [message(span)] * 2,
            [answers[0], answers[0] if span.stop <= first else answers[1]]
            + [tops[g], bases[g], backward, dir_v, beside],
            after=[far_sum] if g else [],
            products=2 * wide(span),
            weight=WEIGHT,
        )
        solved.append(down)
        echoes.append(echo)
        heard_down.append([swap_chips(down, below_top - 1)])
        if g == 0:
            far_sum = make_far(False, [down], [])
    for g, span in enumerate(spans):
        heard_up[g].append(swap_chips(ups[g], below_top))
        tops[g], bases[g] = call(
            functools.partial(crown, span),
            [message(span)] * 2,
            [heard_up[g][-1], starts[g], through, bottom, back_low],
            old=[tops[g], bases[g]],
            products=3 * wide(span),
        )
    for low in range(below_top - 2, -1, -1):
        for g, span in enumerate(spans):
            (solved[g],) = call(
                functools.partial(retreat, span, low + 1),
                [message(span)],
                [heard_down[g][0], bases[g], backward, dir_v, beside],
                products=wide(span),
                weight=WEIGHT,
            )
            lows = (low, below_top) if g and low == 0 else (low,)
            heard_down[g].insert(0, swap_chips(solved[g], *lows))
    far_sum = make_far(True, list(solved), [far_sum])

    def finish(span, *refs):
        up_refs, down_refs = refs[:top_chip], refs[top_chip : 2 * top_chip - 1]
        answer_ref, echo_ref, top_ref, base_ref, back_ref, high_ref = refs[2 * top_chip - 1 : -4]
        keep_ref, own_ref, send_ref, in_ref = refs[-4:]
        chip, core = place()
        sent_halo = send_ref.at[pl.ds(wide(span), wide(span))]

        @pl.when(chip == top_chip)
        def _():
            in_ref[...] = jnp.zeros_like(in_ref)

        @pl.when(chip == below_top)
        def _():
            in_ref[...] = echo_ref[...]

        for low in range(below_top):

            @pl.when(chip == low)
            def _():
                in_ref[...] = down_refs[low][...]

        for which, mine, other in ((0, own_ref, sent_halo), (1, sent_halo, own_ref)):

            @pl.when(core == which)
            def _():
                @pl.when(chip == 0)
                def _():
                    mine[...] = jnp.zeros_like(mine)

                @pl.when(chip == top_chip)
                def _():
                    other[...] = jnp.zeros_like(other)

                @pl.when(chip == top_chip)
                def _():
                    if span.start:
                        mine[...] = down_refs[0][...]
                    else:
                        for at in range(span.stop):
                            part, line = divmod(at * rows, late_rows)
                            mine[at] = answer_ref[part, pl.ds(line, rows)]

                for low in range(top_chip):

                    @pl.when(chip == low)
                    def _():
                        other[...] = up_refs[low][...]

                for low in range(below_top):

                    @pl.when(chip == low + 1)
                    def _():
                        mine[...] = down_refs[low][...]

        for i, at in enumerate(range(span.start, span.stop)):
            low = (base_ref[i].astype(F32) + dot(in_ref[i], back_ref[at])).astype(BF16)
            high = (top_ref[i].astype(F32) + dot(in_ref[i], high_ref[at])).astype(BF16)

            @pl.when(core == 0)
            def _():
                keep_ref[i] = low
                send_ref[i] = high

            @pl.when(core == 1)
            def _():
                keep_ref[i] = high
                send_ref[i] = low

    def final(span, *refs):
        keep_ref, own_ref, recv_ref, sum_ref = refs[:4]
        lower_refs, upper_refs = refs[4:6], refs[6:8]
        solved_ref, image_ref, total_ref, sem = refs[-4:]
        _, core = place()
        at, width = span.start, wide(span)
        copies = []
        for side, source in ((core, keep_ref), (1 - core, recv_ref.at[pl.ds(0, width)])):
            copies.append(
                pltpu.make_async_copy(
                    source, solved_ref.at[pl.ds(side * half + at, width)], sem.at[len(copies)]
                )
            )
            copies[-1].start()

        def write(block_refs):
            for number, side in enumerate((core, 1 - core)):
                base = side * half + at
                for i in range(width):
                    halo = own_ref[i] if number == 0 else recv_ref[width + i]
                    total_ref[number * width + i] = sum_ref[base + i] + dot(
                        halo, block_refs[number][at + i]
                    )

        pl.when(core == 0)(lambda: write(lower_refs))
        pl.when(core == 1)(lambda: write(upper_refs))
        for number, side in enumerate((core, 1 - core)):
            copies.append(
                pltpu.make_async_copy(
                    total_ref.at[pl.ds(number * width, width)],
                    image_ref.at[pl.ds(side * half + at, width)],
                    sem.at[len(copies)],
                )
            )
            copies[-1].start()
        for copy in copies:
            copy.wait()

    spec = pl.BlockSpec(memory_space=pltpu.VMEM)
    anywhere = pl.BlockSpec(memory_space=pl.ANY)
    outputs = []
    for g, span in enumerate(spans):
        keep, own, send = call(
            functools.partial(finish, span),
            [message(span), message(span), ((2 * wide(span), rows, size), BF16)],
            heard_up[g]
            + heard_down[g]
            + [answers[1], echoes[g], tops[g], bases[g], backward, back_high],
            after=[far_sum],
            scratch=[pltpu.VMEM(*message(span))],
            products=2 * wide(span),
        )
        operands = [keep, own, swap_cores(send), far_sum]
        operands += [lower_own, lower_other, upper_own, upper_other]
        operands = [pltpu.with_memory_space_constraint(x, VMEM) for x in operands]
        outputs = pl.pallas_call(
            functools.partial(final, span),
            out_shape=[HBM(*every_vector), HBM(*every_sum)],
            in_specs=[spec] * len(operands) + [anywhere] * len(outputs),
            out_specs=[anywhere] * 2,
            input_output_aliases={len(operands) + i: i for i in range(len(outputs))},
            scratch_shapes=[
                pltpu.VMEM((2 * wide(span), rows, size), F32),
                pltpu.SemaphoreType.DMA((4,)),
            ],
            compiler_params=pltpu.CompilerParams(vmem_limit_bytes=2 << 20),
            cost_estimate=pl.CostEstimate(
                flops=4 * wide(span), bytes_accessed=1 << 10, transcendentals=0
            ),
        )(*operands, *outputs)
    preconditioned, image = outputs
    return (preconditioned.reshape(resid.shape), image.reshape(resid.shape))


def solution(mesh):
    spec = P("elev", "valley", "down", None, None)
    in_specs = (spec,) * 8 + (P("elev", "valley", "down"),)
    return jax.shard_map(
        local, mesh=mesh, in_specs=in_specs, out_specs=(spec, spec), check_vma=False
    )
```

```python
import functools

import jax
import jax.numpy as jnp
from jax import lax
from jax.experimental import pallas as pl
from jax.experimental.pallas import tpu as pltpu
from jax.sharding import PartitionSpec as P

BF16 = jnp.bfloat16
F32 = jnp.float32
VMEM = pltpu.MemorySpace.VMEM
HBM = pltpu.MemorySpace.HBM
LAST = 1
WEIGHT = 190000000


def dot(x, y):
    return jnp.dot(x, y, preferred_element_type=F32)


def call(kernel, outs, operands, hbm=(), after=(), old=(), scratch=(), products=1, room=1, weight=1):
    spec = pl.BlockSpec(memory_space=pltpu.VMEM)
    anywhere = pl.BlockSpec(memory_space=pl.ANY)
    held = [pltpu.with_memory_space_constraint(x, VMEM) for x in operands]
    after = [*after, *old]
    far = [pltpu.with_memory_space_constraint(x, HBM) for x in hbm]
    count = len(held) + len(far)

    def body(*refs):
        kernel(*refs[:count], *refs[count + len(after) :])

    return pl.pallas_call(
        body,
        out_shape=[VMEM(shape, dtype) for shape, dtype in outs],
        in_specs=[spec] * len(held) + [anywhere] * (len(far) + len(after)),
        out_specs=[spec] * len(outs),
        scratch_shapes=list(scratch),
        input_output_aliases={count + len(after) - len(old) + i: i for i in range(len(old))},
        compiler_params=pltpu.CompilerParams(vmem_limit_bytes=room << 20),
        cost_estimate=pl.CostEstimate(
            flops=products * weight, bytes_accessed=1 << 10, transcendentals=0
        ),
    )(*held, *far, *after)


def place():
    height = lax.axis_index("elev")
    return height // 2, lax.rem(height, 2)


def swap_cores(value):
    count = lax.axis_size("elev")
    return lax.ppermute(value, "elev", [(i, i ^ 1) for i in range(count)])


def swap_chips(value, *lows):
    pairs = []
    for i in range(lax.axis_size("elev")):
        chip = i // 2
        step = 2 if chip in lows else -2 if chip - 1 in lows else 1 - 2 * (i % 2)
        pairs.append((i, i + step))
    return lax.ppermute(value, "elev", pairs)


def local(
    resid,
    direction,
    diag_blocks,
    lower_blocks,
    upper_blocks,
    inv_pivots,
    down_coupling,
    valley_coupling,
    coupled_column,
):
    _, valleys, downs, rows, size = resid.shape
    chains = valleys * downs
    half = chains // 2
    spans = [slice(0, half // 2), slice(half // 2, half)]
    first = half - max(1, LAST * half // 4)
    answer_spans = [slice(0, first), slice(first, half)]
    chips = lax.axis_size("elev") // 2
    below_top, top_chip = chips - 2, chips - 1
    vectors = lambda x: x.reshape(chains, rows, size)
    blocks = lambda x: x.reshape(chains, size, size)
    rhs, current = vectors(resid), vectors(direction)
    square = ((half, size, size), BF16)
    packed = ((half, 2 * size + rows, size), BF16)
    LOWER, RIGHT, UPPER = slice(0, size), slice(size, size + rows), slice(size + rows, None)
    every_block = ((chains, size, size), BF16)
    every_vector = ((chains, rows, size), BF16)
    every_sum = ((chains, rows, size), F32)
    downs_count, valley_count = lax.axis_size("down"), lax.axis_size("valley")

    def wide(span):
        return span.stop - span.start

    def message(span, more=0):
        return ((wide(span), rows + more, size), BF16)

    half_blocks, half_vectors = ((half, size, size), BF16), ((half, rows, size), BF16)

    half_blocks, half_vectors = ((half, size, size), BF16), ((half, rows, size), BF16)

    def multiply(pivot_ref, rhs_ref, lower_ref, upper_ref, copies, out_ref):
        copies[0].wait()
        copies[1].wait()
        for i in range(half):
            out_ref[i, RIGHT] = dot(rhs_ref[i], pivot_ref[i]).astype(BF16)
        copies[2].wait()
        for i in range(half):
            out_ref[i, LOWER] = (-dot(lower_ref[i], pivot_ref[i])).astype(BF16)
        copies[3].wait()
        for i in range(half):
            out_ref[i, UPPER] = (-dot(upper_ref[i], pivot_ref[i])).astype(BF16)

    def send_products(p_ref, r_ref, l_ref, u_ref, out_ref, lower_v, upper_v, pivot_v, rhs_v, sem):
        _, core = place()
        part = pl.ds((1 - core) * half, half)
        copies = [
            pltpu.make_async_copy(source.at[part], target, sem.at[i])
            for i, (source, target) in enumerate(
                ((p_ref, pivot_v), (r_ref, rhs_v), (l_ref, lower_v), (u_ref, upper_v))
            )
        ]
        for copy in copies:
            copy.start()
        multiply(pivot_v, rhs_v, lower_v, upper_v, copies, out_ref)

    def keep_products(p_ref, r_ref, l_ref, u_ref, d_ref, *refs):
        out_ref, lower_v, upper_v, dir_v, pivot_v, rhs_v, sem = refs
        _, core = place()
        part = pl.ds(core * half, half)
        copies = [
            pltpu.make_async_copy(source, target, sem.at[i])
            for i, (source, target) in enumerate(
                (
                    (p_ref.at[part], pivot_v),
                    (r_ref.at[part], rhs_v),
                    (l_ref.at[part], lower_v),
                    (u_ref.at[part], upper_v),
                    (d_ref, dir_v),
                )
            )
        ]
        for copy in copies:
            copy.start()
        multiply(pivot_v, rhs_v, lower_v, upper_v, copies, out_ref)
        copies[4].wait()

    layer = [blocks(inv_pivots), rhs, blocks(lower_blocks), blocks(upper_blocks)]
    room_for = [pltpu.VMEM(*half_blocks), pltpu.VMEM(*half_vectors)]
    send1, lower_other, upper_other = call(
        send_products,
        [packed, half_blocks, half_blocks],
        [],
        hbm=layer,
        scratch=room_for + [pltpu.SemaphoreType.DMA((4,))],
        products=5 * half,
        room=2,
    )
    recv1 = swap_cores(send1)
    keep1, lower_own, upper_own, dir_v = call(
        keep_products,
        [packed, half_blocks, half_blocks, every_vector],
        [],
        hbm=layer + [current],
        after=[send1],
        scratch=room_for + [pltpu.SemaphoreType.DMA((5,))],
        products=5 * half,
        room=2,
    )
    beside = swap_cores(dir_v)

    def reflect(span, keep_ref, recv_ref, out_ref):
        chip, core = place()

        def write(bottom, top):
            for i, at in enumerate(range(span.start, span.stop)):
                lower, upper = top[at, LOWER], bottom[at, UPPER]
                through = dot(bottom[at, LOWER], lower).astype(BF16)
                out_ref[i, :size] = (
                    bottom[at, LOWER].astype(F32) + dot(through, upper)
                ).astype(BF16)
                start = top[at, RIGHT].astype(F32) + dot(bottom[at, RIGHT], lower)
                out_ref[i, size : size + rows] = (
                    bottom[at, RIGHT].astype(F32) + dot(start.astype(BF16), upper)
                ).astype(BF16)

        here = chip == top_chip
        pl.when(jnp.logical_and(here, core == 0))(lambda: write(keep_ref, recv_ref))
        pl.when(jnp.logical_and(here, core == 1))(lambda: write(recv_ref, keep_ref))

    def answer_of(span, after):
        (answer,) = call(
            functools.partial(reflect, span),
            [message(span, size)],
            [keep1, recv1],
            after=after,
            products=4 * wide(span),
        )
        return answer

    answer = answer_of(answer_spans[0], [])
    answers, echoing = [swap_chips(answer, below_top)], [answer]

    late_rows = max(size + rows, spans[0].stop * rows // wide(answer_spans[1]))

    def reflect_late(keep_ref, recv_ref, dir_ref, beside_ref, out_ref):
        chip, core = place()
        reflect(answer_spans[1], keep_ref, recv_ref, out_ref)

        @pl.when(chip == below_top)
        def _():
            for at in range(spans[0].stop):
                part, line = divmod(at * rows, late_rows)
                target = out_ref.at[part, pl.ds(line, rows)]

                @pl.when(core == 1)
                def _():
                    target[...] = dir_ref[core * half + at]

                @pl.when(core == 0)
                def _():
                    target[...] = beside_ref[core * half + at]

    def give(which, core, dir_ref, beside_ref, span, out_ref):
        part = pl.ds(core * half + span.start, wide(span))

        @pl.when(core == which)
        def _():
            out_ref[...] = dir_ref[part]

        @pl.when(core != which)
        def _():
            out_ref[...] = beside_ref[part]

    def begin(span, keep_ref, recv_ref, dir_ref, beside_ref, start_ref, out_ref):
        chip, core = place()

        def write(bottom, top):
            for i, at in enumerate(range(span.start, span.stop)):
                start_ref[i] = (
                    top[at, RIGHT].astype(F32) + dot(bottom[at, RIGHT], top[at, LOWER])
                ).astype(BF16)

        pl.when(core == 0)(lambda: write(keep_ref, recv_ref))
        pl.when(core == 1)(lambda: write(recv_ref, keep_ref))

        @pl.when(chip == 0)
        def _():
            out_ref[...] = start_ref[...]

        @pl.when(chip != 0)
        def _():
            give(0, core, dir_ref, beside_ref, span, out_ref)

    def join(keep_ref, recv_ref, dir_ref, *refs):
        through_ref, backward_ref, bottom_ref, low_ref, high_ref, copy_ref, rim_ref = refs
        _, core = place()
        copy_ref[...] = dir_ref[...]
        for i in range(valleys):
            rim_ref[i] = dir_ref[i * downs + downs - 1]

        def write(bottom, top):
            bottom_ref[...] = bottom[:, : size + rows]
            low_ref[...] = bottom[:, UPPER]
            high_ref[...] = top[:, UPPER]
            for i in range(half):
                through_ref[i] = dot(bottom[i, LOWER], top[i, LOWER]).astype(BF16)
                backward_ref[i] = dot(top[i, UPPER], bottom[i, UPPER]).astype(BF16)

        pl.when(core == 0)(lambda: write(keep_ref, recv_ref))
        pl.when(core == 1)(lambda: write(recv_ref, keep_ref))

    def where(upper, edge, work):
        chip, _ = place()
        pl.when((chip >= edge) if upper else (chip < edge))(work)

    def near(upper, dir_ref, beside_ref, lower_ref, upper_ref, diag_ref, out_ref, diag_v, sem):
        def work():
            _, core = place()
            copy = pltpu.make_async_copy(diag_ref, diag_v, sem.at[0])
            copy.start()

            def write(block_ref):
                for i in range(half):
                    at = core * half + i
                    out_ref[at] = dot(beside_ref[at], block_ref[i])

            pl.when(core == 0)(lambda: write(upper_ref))
            pl.when(core == 1)(lambda: write(lower_ref))
            copy.wait()
            for i in range(half):
                at = core * half + i
                out_ref[at] += dot(dir_ref[at], diag_v[at])
                at = (1 - core) * half + i
                out_ref[at] = dot(dir_ref[at], diag_v[at])

        where(upper, chips // 2, work)

    def make_near(upper, after, old):
        (result,) = call(
            functools.partial(near, upper),
            [every_sum],
            [dir_v, beside, lower_own, upper_own],
            hbm=[blocks(diag_blocks)],
            after=after,
            old=old,
            scratch=[pltpu.VMEM((chains, size, size), BF16), pltpu.SemaphoreType.DMA((1,))],
            products=2 * chains,
            room=2,
        )
        return result

    def advance(span, low, in_ref, start_ref, through_ref, dir_ref, beside_ref, out_ref):
        chip, core = place()

        @pl.when(chip == low)
        def _():
            for i, at in enumerate(range(span.start, span.stop)):
                out_ref[i] = (
                    start_ref[i].astype(F32) + dot(in_ref[i], through_ref[at])
                ).astype(BF16)

        @pl.when(chip != low)
        def _():
            give(0, core, dir_ref, beside_ref, span, out_ref)

    downs_count, valley_count = lax.axis_size("down"), lax.axis_size("valley")

    starts, fronts, heard_up = [], [], []
    for g, span in enumerate(spans):
        start, front = call(
            functools.partial(begin, span),
            [message(span)] * 2,
            [keep1, recv1, dir_v, beside],
            after=[near_sum] if g else echoing,
            products=wide(span),
        )
        starts.append(start)
        fronts.append(front)
        heard_up.append([swap_chips(front, 0)])
        if g == 0:
            through, backward, bottom, back_low, back_high, dir_out, rim_out = call(
                join,
                [square, square, ((half, size + rows, size), BF16), square, square]
                + [every_vector, ((valleys, rows, size), BF16)],
                [keep1, recv1, dir_v],
                after=[start],
                products=4 * half,
            )
            others = [
                lax.ppermute(
                    dir_out, "valley", [(i, (i + by) % valley_count) for i in range(valley_count)]
                )
                for by in range(1, valley_count)
            ]
            near_sum = make_near(True, [start], [])
    (answer,) = call(
        reflect_late,
        [((wide(answer_spans[1]), late_rows, size), BF16)],
        [keep1, recv1, dir_v, beside],
        after=echoing,
        products=4 * wide(answer_spans[1]),
    )
    answers.append(swap_chips(answer, below_top))
    rim = lax.ppermute(
        rim_out, "down", [(i, (i + 1) % downs_count) for i in range(downs_count)]
    )
    for low in range(1, below_top):
        for g, span in enumerate(spans):
            (fronts[g],) = call(
                functools.partial(advance, span, low),
                [message(span)],
                [heard_up[g][-1], starts[g], through, dir_v, beside],
                products=wide(span),
                weight=WEIGHT,
            )
            heard_up[g].append(swap_chips(fronts[g], low))
    near_sum = make_near(False, list(fronts) + [rim], [near_sum])

    def far(upper, *refs):
        where(upper, chips // 2, functools.partial(far_work, *refs))

    def far_work(*refs):
        dir_ref, sum_ref, rim_ref, beside_ref, lower_ref, upper_ref = refs[:6]
        others_refs = refs[6 : 5 + valley_count]
        down_ref, valley_ref, column_ref, out_ref = refs[5 + valley_count : 9 + valley_count]
        partner_ref, down_v, valley_v, column_s, sem = refs[9 + valley_count :]
        _, core = place()
        mine = lax.axis_index("valley")
        edge = lax.axis_index("down")
        copies = [
            pltpu.make_async_copy(source, target, sem.at[i])
            for i, (source, target) in enumerate(
                ((column_ref, column_s), (down_ref, down_v), (valley_ref, valley_v))
            )
        ]
        for copy in copies:
            copy.start()
        copies[0].wait()
        for i in range(chains):
            column = column_s[0, i % downs, i // downs]
            owner = column // valleys
            spot = lax.rem(column, valleys) * downs + i % downs
            behind = lax.rem(mine - owner + valley_count, valley_count)

            @pl.when(behind == 0)
            def _():
                partner_ref[i] = dir_ref[spot]

            for by in range(1, valley_count):

                @pl.when(behind == by)
                def _():
                    partner_ref[i] = others_refs[by - 1][spot]

        copies[1].wait()
        for i in range(chains):
            if i % downs:
                out_ref[i] = sum_ref[i] + dot(dir_ref[i - 1], down_v[i])

        @pl.when(edge > 0)
        def _():
            for i in range(0, chains, downs):
                out_ref[i] = sum_ref[i] + dot(rim_ref[i // downs], down_v[i])

        @pl.when(edge == 0)
        def _():
            for i in range(0, chains, downs):
                out_ref[i] = sum_ref[i]

        def add(block_ref):
            for i in range(half):
                at = (1 - core) * half + i
                out_ref[at] += dot(beside_ref[at], block_ref[i])

        pl.when(core == 0)(lambda: add(upper_ref))
        pl.when(core == 1)(lambda: add(lower_ref))
        copies[2].wait()
        for i in range(chains):
            out_ref[i] += dot(partner_ref[i], valley_v[i])

    def make_far(upper, after, old):
        (result,) = call(
            functools.partial(far, upper),
            [every_sum],
            [dir_v, near_sum, rim, beside, lower_other, upper_other] + others,
            hbm=[
                blocks(down_coupling),
                blocks(valley_coupling),
                jnp.swapaxes(coupled_column, 1, 2),
            ],
            after=after,
            old=old,
            scratch=[
                pltpu.VMEM((chains, rows, size), BF16),
                pltpu.VMEM((chains, size, size), BF16),
                pltpu.VMEM((chains, size, size), BF16),
                pltpu.SMEM((1, downs, valleys), jnp.int32),
                pltpu.SemaphoreType.DMA((3,)),
            ],
            products=2 * chains,
            room=4,
        )
        return result

    def fronts_of(span, in_ref, start_ref, through_ref, bottom_ref, low_ref, top_ref, base_ref):
        for i, at in enumerate(range(span.start, span.stop)):
            top = (start_ref[i].astype(F32) + dot(in_ref[i], through_ref[at])).astype(BF16)
            low = bottom_ref[at, size:].astype(F32) + dot(in_ref[i], bottom_ref[at, :size])
            top_ref[i] = top
            base_ref[i] = (low.astype(BF16).astype(F32) + dot(top, low_ref[at])).astype(BF16)

    def arrive(span, *refs):
        heard_refs = refs[:below_top]
        start_ref, through_ref, bottom_ref, low_ref, dir_ref, beside_ref = refs[
            below_top : below_top + 6
        ]
        top_ref, base_ref, up_ref, in_ref = refs[-4:]
        chip, core = place()

        @pl.when(chip == 0)
        def _():
            in_ref[...] = jnp.zeros_like(in_ref)

        for low in range(below_top):

            @pl.when(chip == low + 1)
            def _():
                in_ref[...] = heard_refs[low][...]

        @pl.when(chip < top_chip)
        def _():
            fronts_of(span, in_ref, start_ref, through_ref, bottom_ref, low_ref, top_ref, base_ref)

        @pl.when(chip == below_top)
        def _():
            up_ref[...] = top_ref[...]

        @pl.when(chip != below_top)
        def _():
            give(0, core, dir_ref, beside_ref, span, up_ref)

    def turn(span, *refs):
        answer_refs = refs[:2]
        top_ref, base_ref, back_ref, dir_ref, beside_ref, down_ref, echo_ref = refs[2:]
        chip, core = place()

        @pl.when(chip == below_top)
        def _():
            for i, at in enumerate(range(span.start, span.stop)):
                late = at >= first
                answer = answer_refs[late].at[at - first * late]
                echo = (
                    answer[size : size + rows, :].astype(F32) + dot(top_ref[i], answer[:size, :])
                ).astype(BF16)
                echo_ref[i] = echo
                down_ref[i] = (base_ref[i].astype(F32) + dot(echo, back_ref[at])).astype(BF16)

        @pl.when(chip != below_top)
        def _():
            give(1, core, dir_ref, beside_ref, span, down_ref)

    def crown(span, in_ref, start_ref, through_ref, bottom_ref, low_ref, top_ref, base_ref):
        chip, _ = place()

        @pl.when(chip == top_chip)
        def _():
            fronts_of(span, in_ref, start_ref, through_ref, bottom_ref, low_ref, top_ref, base_ref)

    def retreat(span, low, in_ref, base_ref, back_ref, dir_ref, beside_ref, out_ref):
        chip, core = place()

        @pl.when(chip == low)
        def _():
            for i, at in enumerate(range(span.start, span.stop)):
                out_ref[i] = (base_ref[i].astype(F32) + dot(in_ref[i], back_ref[at])).astype(BF16)

        @pl.when(chip != low)
        def _():
            give(1, core, dir_ref, beside_ref, span, out_ref)

    tops, bases, ups, solved, echoes, heard_down = [], [], [], [], [], []
    for g, span in enumerate(spans):
        top, base, up = call(
            functools.partial(arrive, span),
            [message(span)] * 3,
            heard_up[g] + [starts[g], through, bottom, back_low, dir_v, beside],
            after=[near_sum],
            scratch=[pltpu.VMEM(*message(span))],
            products=3 * wide(span),
            weight=WEIGHT,
        )
        tops.append(top)
        bases.append(base)
        ups.append(up)
    for g, span in enumerate(spans):
        down, echo = call(
            functools.partial(turn, span),
            [message(span)] * 2,
            [answers[0], answers[0] if span.stop <= first else answers[1]]
            + [tops[g], bases[g], backward, dir_v, beside],
            after=[far_sum] if g else [],
            products=2 * wide(span),
            weight=WEIGHT,
        )
        solved.append(down)
        echoes.append(echo)
        heard_down.append([swap_chips(down, below_top - 1)])
        if g == 0:
            far_sum = make_far(False, [down], [])
    def take_in(g, span):
        heard_up[g].append(swap_chips(ups[g], below_top))
        tops[g], bases[g] = call(
            functools.partial(crown, span),
            [message(span)] * 2,
            [heard_up[g][-1], starts[g], through, bottom, back_low],
            old=[tops[g], bases[g]],
            products=3 * wide(span),
        )

    take_in(0, spans[0])
    for low in range(below_top - 2, -1, -1):
        for g, span in enumerate(spans):
            (solved[g],) = call(
                functools.partial(retreat, span, low + 1),
                [message(span)],
                [heard_down[g][0], bases[g], backward, dir_v, beside],
                products=wide(span),
                weight=WEIGHT,
            )
            lows = (low, below_top) if g and low == 0 else (low,)
            heard_down[g].insert(0, swap_chips(solved[g], *lows))
    take_in(1, spans[1])
    far_sum = make_far(True, list(solved), [far_sum])

    def finish(span, *refs):
        up_refs, down_refs = refs[:top_chip], refs[top_chip : 2 * top_chip - 1]
        answer_ref, echo_ref, top_ref, base_ref, back_ref, high_ref = refs[2 * top_chip - 1 : -4]
        keep_ref, own_ref, send_ref, in_ref = refs[-4:]
        chip, core = place()
        sent_halo = send_ref.at[pl.ds(wide(span), wide(span))]

        @pl.when(chip == top_chip)
        def _():
            in_ref[...] = jnp.zeros_like(in_ref)

        @pl.when(chip == below_top)
        def _():
            in_ref[...] = echo_ref[...]

        for low in range(below_top):

            @pl.when(chip == low)
            def _():
                in_ref[...] = down_refs[low][...]

        for which, mine, other in ((0, own_ref, sent_halo), (1, sent_halo, own_ref)):

            @pl.when(core == which)
            def _():
                @pl.when(chip == 0)
                def _():
                    mine[...] = jnp.zeros_like(mine)

                @pl.when(chip == top_chip)
                def _():
                    other[...] = jnp.zeros_like(other)

                @pl.when(chip == top_chip)
                def _():
                    if span.start:
                        mine[...] = down_refs[0][...]
                    else:
                        for at in range(span.stop):
                            part, line = divmod(at * rows, late_rows)
                            mine[at] = answer_ref[part, pl.ds(line, rows)]

                for low in range(top_chip):

                    @pl.when(chip == low)
                    def _():
                        other[...] = up_refs[low][...]

                for low in range(below_top):

                    @pl.when(chip == low + 1)
                    def _():
                        mine[...] = down_refs[low][...]

        for i, at in enumerate(range(span.start, span.stop)):
            low = (base_ref[i].astype(F32) + dot(in_ref[i], back_ref[at])).astype(BF16)
            high = (top_ref[i].astype(F32) + dot(in_ref[i], high_ref[at])).astype(BF16)

            @pl.when(core == 0)
            def _():
                keep_ref[i] = low
                send_ref[i] = high

            @pl.when(core == 1)
            def _():
                keep_ref[i] = high
                send_ref[i] = low

    def final(span, *refs):
        keep_ref, own_ref, recv_ref, sum_ref = refs[:4]
        lower_refs, upper_refs = refs[4:6], refs[6:8]
        solved_ref, image_ref, total_ref, sem = refs[-4:]
        _, core = place()
        at, width = span.start, wide(span)
        copies = []
        for side, source in ((core, keep_ref), (1 - core, recv_ref.at[pl.ds(0, width)])):
            copies.append(
                pltpu.make_async_copy(
                    source, solved_ref.at[pl.ds(side * half + at, width)], sem.at[len(copies)]
                )
            )
            copies[-1].start()

        def write(block_refs):
            for number, side in enumerate((core, 1 - core)):
                base = side * half + at
                for i in range(width):
                    halo = own_ref[i] if number == 0 else recv_ref[width + i]
                    total_ref[number * width + i] = sum_ref[base + i] + dot(
                        halo, block_refs[number][at + i]
                    )

        pl.when(core == 0)(lambda: write(lower_refs))
        pl.when(core == 1)(lambda: write(upper_refs))
        for number, side in enumerate((core, 1 - core)):
            copies.append(
                pltpu.make_async_copy(
                    total_ref.at[pl.ds(number * width, width)],
                    image_ref.at[pl.ds(side * half + at, width)],
                    sem.at[len(copies)],
                )
            )
            copies[-1].start()
        for copy in copies:
            copy.wait()

    spec = pl.BlockSpec(memory_space=pltpu.VMEM)
    anywhere = pl.BlockSpec(memory_space=pl.ANY)
    outputs = []
    for g, span in enumerate(spans):
        keep, own, send = call(
            functools.partial(finish, span),
            [message(span), message(span), ((2 * wide(span), rows, size), BF16)],
            heard_up[g]
            + heard_down[g]
            + [answers[1], echoes[g], tops[g], bases[g], backward, back_high],
            after=[far_sum],
            scratch=[pltpu.VMEM(*message(span))],
            products=2 * wide(span),
        )
        operands = [keep, own, swap_cores(send), far_sum]
        operands += [lower_own, lower_other, upper_own, upper_other]
        operands = [pltpu.with_memory_space_constraint(x, VMEM) for x in operands]
        outputs = pl.pallas_call(
            functools.partial(final, span),
            out_shape=[HBM(*every_vector), HBM(*every_sum)],
            in_specs=[spec] * len(operands) + [anywhere] * len(outputs),
            out_specs=[anywhere] * 2,
            input_output_aliases={len(operands) + i: i for i in range(len(outputs))},
            scratch_shapes=[
                pltpu.VMEM((2 * wide(span), rows, size), F32),
                pltpu.SemaphoreType.DMA((4,)),
            ],
            compiler_params=pltpu.CompilerParams(vmem_limit_bytes=2 << 20),
            cost_estimate=pl.CostEstimate(
                flops=4 * wide(span), bytes_accessed=1 << 10, transcendentals=0
            ),
        )(*operands, *outputs)
    preconditioned, image = outputs
    return (preconditioned.reshape(resid.shape), image.reshape(resid.shape))


def solution(mesh):
    spec = P("elev", "valley", "down", None, None)
    in_specs = (spec,) * 8 + (P("elev", "valley", "down"),)
    return jax.shard_map(
        local, mesh=mesh, in_specs=in_specs, out_specs=(spec, spec), check_vma=False
    )
```

```python
import functools

import jax
import jax.numpy as jnp
from jax import lax
from jax.experimental import pallas as pl
from jax.experimental.pallas import tpu as pltpu
from jax.sharding import PartitionSpec as P

BF16 = jnp.bfloat16
F32 = jnp.float32
VMEM = pltpu.MemorySpace.VMEM
HBM = pltpu.MemorySpace.HBM
LAST = 1
WEIGHT = 190000000


def dot(x, y):
    return jnp.dot(x, y, preferred_element_type=F32)


def call(kernel, outs, operands, hbm=(), after=(), old=(), scratch=(), products=1, room=1, weight=1):
    spec = pl.BlockSpec(memory_space=pltpu.VMEM)
    anywhere = pl.BlockSpec(memory_space=pl.ANY)
    held = [pltpu.with_memory_space_constraint(x, VMEM) for x in operands]
    after = [*after, *old]
    far = [pltpu.with_memory_space_constraint(x, HBM) for x in hbm]
    count = len(held) + len(far)

    def body(*refs):
        kernel(*refs[:count], *refs[count + len(after) :])

    return pl.pallas_call(
        body,
        out_shape=[VMEM(shape, dtype) for shape, dtype in outs],
        in_specs=[spec] * len(held) + [anywhere] * (len(far) + len(after)),
        out_specs=[spec] * len(outs),
        scratch_shapes=list(scratch),
        input_output_aliases={count + len(after) - len(old) + i: i for i in range(len(old))},
        compiler_params=pltpu.CompilerParams(vmem_limit_bytes=room << 20),
        cost_estimate=pl.CostEstimate(
            flops=products * weight, bytes_accessed=1 << 10, transcendentals=0
        ),
    )(*held, *far, *after)


def place():
    height = lax.axis_index("elev")
    return height // 2, lax.rem(height, 2)


def swap_cores(value):
    count = lax.axis_size("elev")
    return lax.ppermute(value, "elev", [(i, i ^ 1) for i in range(count)])


def swap_chips(value, *lows):
    pairs = []
    for i in range(lax.axis_size("elev")):
        chip = i // 2
        step = 2 if chip in lows else -2 if chip - 1 in lows else 1 - 2 * (i % 2)
        pairs.append((i, i + step))
    return lax.ppermute(value, "elev", pairs)


def local(
    resid,
    direction,
    diag_blocks,
    lower_blocks,
    upper_blocks,
    inv_pivots,
    down_coupling,
    valley_coupling,
    coupled_column,
):
    _, valleys, downs, rows, size = resid.shape
    chains = valleys * downs
    half = chains // 2
    spans = [slice(0, half // 2), slice(half // 2, half)]
    first = half - max(1, LAST * half // 4)
    answer_spans = [slice(0, first), slice(first, half)]
    chips = lax.axis_size("elev") // 2
    below_top, top_chip = chips - 2, chips - 1
    vectors = lambda x: x.reshape(chains, rows, size)
    blocks = lambda x: x.reshape(chains, size, size)
    rhs, current = vectors(resid), vectors(direction)
    square = ((half, size, size), BF16)
    packed = ((half, 2 * size + rows, size), BF16)
    LOWER, RIGHT, UPPER = slice(0, size), slice(size, size + rows), slice(size + rows, None)
    every_block = ((chains, size, size), BF16)
    every_vector = ((chains, rows, size), BF16)
    every_sum = ((chains, rows, size), F32)
    downs_count, valley_count = lax.axis_size("down"), lax.axis_size("valley")

    def wide(span):
        return span.stop - span.start

    def message(span, more=0):
        return ((wide(span), rows + more, size), BF16)

    half_blocks, half_vectors = ((half, size, size), BF16), ((half, rows, size), BF16)

    half_blocks, half_vectors = ((half, size, size), BF16), ((half, rows, size), BF16)

    def multiply(pivot_ref, rhs_ref, lower_ref, upper_ref, copies, out_ref):
        copies[0].wait()
        copies[1].wait()
        for i in range(half):
            out_ref[i, RIGHT] = dot(rhs_ref[i], pivot_ref[i]).astype(BF16)
        copies[2].wait()
        for i in range(half):
            out_ref[i, LOWER] = (-dot(lower_ref[i], pivot_ref[i])).astype(BF16)
        copies[3].wait()
        for i in range(half):
            out_ref[i, UPPER] = (-dot(upper_ref[i], pivot_ref[i])).astype(BF16)

    def send_products(p_ref, r_ref, l_ref, u_ref, out_ref, lower_v, upper_v, pivot_v, rhs_v, sem):
        _, core = place()
        part = pl.ds((1 - core) * half, half)
        copies = [
            pltpu.make_async_copy(source.at[part], target, sem.at[i])
            for i, (source, target) in enumerate(
                ((p_ref, pivot_v), (r_ref, rhs_v), (l_ref, lower_v), (u_ref, upper_v))
            )
        ]
        for copy in copies:
            copy.start()
        multiply(pivot_v, rhs_v, lower_v, upper_v, copies, out_ref)

    def keep_products(p_ref, r_ref, l_ref, u_ref, d_ref, *refs):
        out_ref, lower_v, upper_v, dir_v, pivot_v, rhs_v, sem = refs
        _, core = place()
        part = pl.ds(core * half, half)
        copies = [
            pltpu.make_async_copy(source, target, sem.at[i])
            for i, (source, target) in enumerate(
                (
                    (p_ref.at[part], pivot_v),
                    (r_ref.at[part], rhs_v),
                    (l_ref.at[part], lower_v),
                    (u_ref.at[part], upper_v),
                    (d_ref, dir_v),
                )
            )
        ]
        for copy in copies:
            copy.start()
        multiply(pivot_v, rhs_v, lower_v, upper_v, copies, out_ref)
        copies[4].wait()

    layer = [blocks(inv_pivots), rhs, blocks(lower_blocks), blocks(upper_blocks)]
    room_for = [pltpu.VMEM(*half_blocks), pltpu.VMEM(*half_vectors)]
    send1, lower_other, upper_other = call(
        send_products,
        [packed, half_blocks, half_blocks],
        [],
        hbm=layer,
        scratch=room_for + [pltpu.SemaphoreType.DMA((4,))],
        products=5 * half,
        room=2,
    )
    recv1 = swap_cores(send1)
    keep1, lower_own, upper_own, dir_v = call(
        keep_products,
        [packed, half_blocks, half_blocks, every_vector],
        [],
        hbm=layer + [current],
        after=[send1],
        scratch=room_for + [pltpu.SemaphoreType.DMA((5,))],
        products=5 * half,
        room=2,
    )
    beside = swap_cores(dir_v)

    def reflect(span, keep_ref, recv_ref, out_ref):
        chip, core = place()

        def write(bottom, top):
            for i, at in enumerate(range(span.start, span.stop)):
                lower, upper = top[at, LOWER], bottom[at, UPPER]
                through = dot(bottom[at, LOWER], lower).astype(BF16)
                out_ref[i, :size] = (
                    bottom[at, LOWER].astype(F32) + dot(through, upper)
                ).astype(BF16)
                start = top[at, RIGHT].astype(F32) + dot(bottom[at, RIGHT], lower)
                out_ref[i, size : size + rows] = (
                    bottom[at, RIGHT].astype(F32) + dot(start.astype(BF16), upper)
                ).astype(BF16)

        here = chip == top_chip
        pl.when(jnp.logical_and(here, core == 0))(lambda: write(keep_ref, recv_ref))
        pl.when(jnp.logical_and(here, core == 1))(lambda: write(recv_ref, keep_ref))

    def answer_of(span, after):
        (answer,) = call(
            functools.partial(reflect, span),
            [message(span, size)],
            [keep1, recv1],
            after=after,
            products=4 * wide(span),
        )
        return answer

    answer = answer_of(answer_spans[0], [])
    answers, echoing = [swap_chips(answer, below_top)], [answer]

    late_rows = max(size + rows, spans[0].stop * rows // wide(answer_spans[1]))

    def reflect_late(keep_ref, recv_ref, dir_ref, beside_ref, out_ref):
        chip, core = place()
        reflect(answer_spans[1], keep_ref, recv_ref, out_ref)

        @pl.when(chip == below_top)
        def _():
            for at in range(spans[0].stop):
                part, line = divmod(at * rows, late_rows)
                target = out_ref.at[part, pl.ds(line, rows)]

                @pl.when(core == 1)
                def _():
                    target[...] = dir_ref[core * half + at]

                @pl.when(core == 0)
                def _():
                    target[...] = beside_ref[core * half + at]

    def give(which, core, dir_ref, beside_ref, span, out_ref):
        part = pl.ds(core * half + span.start, wide(span))

        @pl.when(core == which)
        def _():
            out_ref[...] = dir_ref[part]

        @pl.when(core != which)
        def _():
            out_ref[...] = beside_ref[part]

    def begin(span, keep_ref, recv_ref, dir_ref, beside_ref, start_ref, out_ref):
        chip, core = place()

        def write(bottom, top):
            for i, at in enumerate(range(span.start, span.stop)):
                start_ref[i] = (
                    top[at, RIGHT].astype(F32) + dot(bottom[at, RIGHT], top[at, LOWER])
                ).astype(BF16)

        pl.when(core == 0)(lambda: write(keep_ref, recv_ref))
        pl.when(core == 1)(lambda: write(recv_ref, keep_ref))

        @pl.when(chip == 0)
        def _():
            out_ref[...] = start_ref[...]

        @pl.when(chip != 0)
        def _():
            give(0, core, dir_ref, beside_ref, span, out_ref)

    def join(keep_ref, recv_ref, dir_ref, *refs):
        through_ref, backward_ref, bottom_ref, low_ref, high_ref, copy_ref, rim_ref = refs
        _, core = place()
        copy_ref[...] = dir_ref[...]
        for i in range(valleys):
            rim_ref[i] = dir_ref[i * downs + downs - 1]

        def write(bottom, top):
            bottom_ref[...] = bottom[:, : size + rows]
            low_ref[...] = bottom[:, UPPER]
            high_ref[...] = top[:, UPPER]
            for i in range(half):
                through_ref[i] = dot(bottom[i, LOWER], top[i, LOWER]).astype(BF16)
                backward_ref[i] = dot(top[i, UPPER], bottom[i, UPPER]).astype(BF16)

        pl.when(core == 0)(lambda: write(keep_ref, recv_ref))
        pl.when(core == 1)(lambda: write(recv_ref, keep_ref))

    def where(upper, edge, work):
        chip, _ = place()
        pl.when((chip >= edge) if upper else (chip < edge))(work)

    def near(upper, dir_ref, beside_ref, lower_ref, upper_ref, diag_ref, out_ref, diag_v, sem):
        def work():
            _, core = place()
            copy = pltpu.make_async_copy(diag_ref, diag_v, sem.at[0])
            copy.start()

            def write(block_ref):
                for i in range(half):
                    at = core * half + i
                    out_ref[at] = dot(beside_ref[at], block_ref[i])

            pl.when(core == 0)(lambda: write(upper_ref))
            pl.when(core == 1)(lambda: write(lower_ref))
            copy.wait()
            for i in range(half):
                at = core * half + i
                out_ref[at] += dot(dir_ref[at], diag_v[at])
                at = (1 - core) * half + i
                out_ref[at] = dot(dir_ref[at], diag_v[at])

        where(upper, chips // 2, work)

    def make_near(upper, after, old):
        (result,) = call(
            functools.partial(near, upper),
            [every_sum],
            [dir_v, beside, lower_own, upper_own],
            hbm=[blocks(diag_blocks)],
            after=after,
            old=old,
            scratch=[pltpu.VMEM((chains, size, size), BF16), pltpu.SemaphoreType.DMA((1,))],
            products=2 * chains,
            room=2,
        )
        return result

    def advance(span, low, in_ref, start_ref, through_ref, dir_ref, beside_ref, out_ref):
        chip, core = place()

        @pl.when(chip == low)
        def _():
            for i, at in enumerate(range(span.start, span.stop)):
                out_ref[i] = (
                    start_ref[i].astype(F32) + dot(in_ref[i], through_ref[at])
                ).astype(BF16)

        @pl.when(chip != low)
        def _():
            give(0, core, dir_ref, beside_ref, span, out_ref)

    downs_count, valley_count = lax.axis_size("down"), lax.axis_size("valley")

    starts, fronts, heard_up = [], [], []
    for g, span in enumerate(spans):
        start, front = call(
            functools.partial(begin, span),
            [message(span)] * 2,
            [keep1, recv1, dir_v, beside],
            after=[near_sum] if g else echoing,
            products=wide(span),
        )
        starts.append(start)
        fronts.append(front)
        heard_up.append([swap_chips(front, 0)])
        if g == 0:
            through, backward, bottom, back_low, back_high, dir_out, rim_out = call(
                join,
                [square, square, ((half, size + rows, size), BF16), square, square]
                + [every_vector, ((valleys, rows, size), BF16)],
                [keep1, recv1, dir_v],
                after=[start],
                products=4 * half,
            )
            others = [
                lax.ppermute(
                    dir_out, "valley", [(i, (i + by) % valley_count) for i in range(valley_count)]
                )
                for by in range(1, valley_count)
            ]
            near_sum = make_near(True, [start], [])
    (answer,) = call(
        reflect_late,
        [((wide(answer_spans[1]), late_rows, size), BF16)],
        [keep1, recv1, dir_v, beside],
        after=echoing,
        products=4 * wide(answer_spans[1]),
    )
    answers.append(swap_chips(answer, below_top))
    rim = lax.ppermute(
        rim_out, "down", [(i, (i + 1) % downs_count) for i in range(downs_count)]
    )
    for low in range(1, below_top):
        for g, span in enumerate(spans):
            (fronts[g],) = call(
                functools.partial(advance, span, low),
                [message(span)],
                [heard_up[g][-1], starts[g], through, dir_v, beside],
                products=wide(span),
                weight=WEIGHT,
            )
            heard_up[g].append(swap_chips(fronts[g], low))
    near_sum = make_near(False, list(fronts) + [rim], [near_sum])

    def far(upper, *refs):
        where(upper, 1, functools.partial(far_work, *refs))

    def far_work(*refs):
        dir_ref, sum_ref, rim_ref, beside_ref, lower_ref, upper_ref = refs[:6]
        others_refs = refs[6 : 5 + valley_count]
        down_ref, valley_ref, column_ref, out_ref = refs[5 + valley_count : 9 + valley_count]
        partner_ref, down_v, valley_v, column_s, sem = refs[9 + valley_count :]
        _, core = place()
        mine = lax.axis_index("valley")
        edge = lax.axis_index("down")
        copies = [
            pltpu.make_async_copy(source, target, sem.at[i])
            for i, (source, target) in enumerate(
                ((column_ref, column_s), (down_ref, down_v), (valley_ref, valley_v))
            )
        ]
        for copy in copies:
            copy.start()
        copies[0].wait()
        for i in range(chains):
            column = column_s[0, i % downs, i // downs]
            owner = column // valleys
            spot = lax.rem(column, valleys) * downs + i % downs
            behind = lax.rem(mine - owner + valley_count, valley_count)

            @pl.when(behind == 0)
            def _():
                partner_ref[i] = dir_ref[spot]

            for by in range(1, valley_count):

                @pl.when(behind == by)
                def _():
                    partner_ref[i] = others_refs[by - 1][spot]

        copies[1].wait()
        for i in range(chains):
            if i % downs:
                out_ref[i] = sum_ref[i] + dot(dir_ref[i - 1], down_v[i])

        @pl.when(edge > 0)
        def _():
            for i in range(0, chains, downs):
                out_ref[i] = sum_ref[i] + dot(rim_ref[i // downs], down_v[i])

        @pl.when(edge == 0)
        def _():
            for i in range(0, chains, downs):
                out_ref[i] = sum_ref[i]

        def add(block_ref):
            for i in range(half):
                at = (1 - core) * half + i
                out_ref[at] += dot(beside_ref[at], block_ref[i])

        pl.when(core == 0)(lambda: add(upper_ref))
        pl.when(core == 1)(lambda: add(lower_ref))
        copies[2].wait()
        for i in range(chains):
            out_ref[i] += dot(partner_ref[i], valley_v[i])

    def make_far(upper, after, old):
        (result,) = call(
            functools.partial(far, upper),
            [every_sum],
            [dir_v, near_sum, rim, beside, lower_other, upper_other] + others,
            hbm=[
                blocks(down_coupling),
                blocks(valley_coupling),
                jnp.swapaxes(coupled_column, 1, 2),
            ],
            after=after,
            old=old,
            scratch=[
                pltpu.VMEM((chains, rows, size), BF16),
                pltpu.VMEM((chains, size, size), BF16),
                pltpu.VMEM((chains, size, size), BF16),
                pltpu.SMEM((1, downs, valleys), jnp.int32),
                pltpu.SemaphoreType.DMA((3,)),
            ],
            products=2 * chains,
            room=4,
        )
        return result

    def fronts_of(span, in_ref, start_ref, through_ref, bottom_ref, low_ref, top_ref, base_ref):
        for i, at in enumerate(range(span.start, span.stop)):
            top = (start_ref[i].astype(F32) + dot(in_ref[i], through_ref[at])).astype(BF16)
            low = bottom_ref[at, size:].astype(F32) + dot(in_ref[i], bottom_ref[at, :size])
            top_ref[i] = top
            base_ref[i] = (low.astype(BF16).astype(F32) + dot(top, low_ref[at])).astype(BF16)

    def arrive(span, *refs):
        heard_refs = refs[:below_top]
        start_ref, through_ref, bottom_ref, low_ref, dir_ref, beside_ref = refs[
            below_top : below_top + 6
        ]
        top_ref, base_ref, up_ref, in_ref = refs[-4:]
        chip, core = place()

        @pl.when(chip == 0)
        def _():
            in_ref[...] = jnp.zeros_like(in_ref)

        for low in range(below_top):

            @pl.when(chip == low + 1)
            def _():
                in_ref[...] = heard_refs[low][...]

        @pl.when(chip < top_chip)
        def _():
            fronts_of(span, in_ref, start_ref, through_ref, bottom_ref, low_ref, top_ref, base_ref)

        @pl.when(chip == below_top)
        def _():
            up_ref[...] = top_ref[...]

        @pl.when(chip != below_top)
        def _():
            give(0, core, dir_ref, beside_ref, span, up_ref)

    def turn(span, *refs):
        answer_refs = refs[:2]
        top_ref, base_ref, back_ref, dir_ref, beside_ref, down_ref, echo_ref = refs[2:]
        chip, core = place()

        @pl.when(chip == below_top)
        def _():
            for i, at in enumerate(range(span.start, span.stop)):
                late = at >= first
                answer = answer_refs[late].at[at - first * late]
                echo = (
                    answer[size : size + rows, :].astype(F32) + dot(top_ref[i], answer[:size, :])
                ).astype(BF16)
                echo_ref[i] = echo
                down_ref[i] = (base_ref[i].astype(F32) + dot(echo, back_ref[at])).astype(BF16)

        @pl.when(chip != below_top)
        def _():
            give(1, core, dir_ref, beside_ref, span, down_ref)

    def crown(span, in_ref, start_ref, through_ref, bottom_ref, low_ref, top_ref, base_ref):
        chip, _ = place()

        @pl.when(chip == top_chip)
        def _():
            fronts_of(span, in_ref, start_ref, through_ref, bottom_ref, low_ref, top_ref, base_ref)

    def retreat(span, low, in_ref, base_ref, back_ref, dir_ref, beside_ref, out_ref):
        chip, core = place()

        @pl.when(chip == low)
        def _():
            for i, at in enumerate(range(span.start, span.stop)):
                out_ref[i] = (base_ref[i].astype(F32) + dot(in_ref[i], back_ref[at])).astype(BF16)

        @pl.when(chip != low)
        def _():
            give(1, core, dir_ref, beside_ref, span, out_ref)

    tops, bases, ups, solved, echoes, heard_down = [], [], [], [], [], []
    for g, span in enumerate(spans):
        top, base, up = call(
            functools.partial(arrive, span),
            [message(span)] * 3,
            heard_up[g] + [starts[g], through, bottom, back_low, dir_v, beside],
            after=[near_sum],
            scratch=[pltpu.VMEM(*message(span))],
            products=3 * wide(span),
            weight=WEIGHT,
        )
        tops.append(top)
        bases.append(base)
        ups.append(up)
    for g, span in enumerate(spans):
        down, echo = call(
            functools.partial(turn, span),
            [message(span)] * 2,
            [answers[0], answers[0] if span.stop <= first else answers[1]]
            + [tops[g], bases[g], backward, dir_v, beside],
            after=[far_sum] if g else [],
            products=2 * wide(span),
            weight=WEIGHT,
        )
        solved.append(down)
        echoes.append(echo)
        heard_down.append([swap_chips(down, below_top - 1)])
        if g == 0:
            far_sum = make_far(False, [down], [])
    def take_in(g, span):
        heard_up[g].append(swap_chips(ups[g], below_top))
        tops[g], bases[g] = call(
            functools.partial(crown, span),
            [message(span)] * 2,
            [heard_up[g][-1], starts[g], through, bottom, back_low],
            old=[tops[g], bases[g]],
            products=3 * wide(span),
        )

    take_in(0, spans[0])
    for low in range(below_top - 2, -1, -1):
        for g, span in enumerate(spans):
            (solved[g],) = call(
                functools.partial(retreat, span, low + 1),
                [message(span)],
                [heard_down[g][0], bases[g], backward, dir_v, beside],
                products=wide(span),
                weight=WEIGHT,
            )
            lows = (low, below_top) if g and low == 0 else (low,)
            heard_down[g].insert(0, swap_chips(solved[g], *lows))
    take_in(1, spans[1])
    far_sum = make_far(True, list(solved), [far_sum])

    def finish(span, *refs):
        up_refs, down_refs = refs[:top_chip], refs[top_chip : 2 * top_chip - 1]
        answer_ref, echo_ref, top_ref, base_ref, back_ref, high_ref = refs[2 * top_chip - 1 : -4]
        keep_ref, own_ref, send_ref, in_ref = refs[-4:]
        chip, core = place()
        sent_halo = send_ref.at[pl.ds(wide(span), wide(span))]

        @pl.when(chip == top_chip)
        def _():
            in_ref[...] = jnp.zeros_like(in_ref)

        @pl.when(chip == below_top)
        def _():
            in_ref[...] = echo_ref[...]

        for low in range(below_top):

            @pl.when(chip == low)
            def _():
                in_ref[...] = down_refs[low][...]

        for which, mine, other in ((0, own_ref, sent_halo), (1, sent_halo, own_ref)):

            @pl.when(core == which)
            def _():
                @pl.when(chip == 0)
                def _():
                    mine[...] = jnp.zeros_like(mine)

                @pl.when(chip == top_chip)
                def _():
                    other[...] = jnp.zeros_like(other)

                @pl.when(chip == top_chip)
                def _():
                    if span.start:
                        mine[...] = down_refs[0][...]
                    else:
                        for at in range(span.stop):
                            part, line = divmod(at * rows, late_rows)
                            mine[at] = answer_ref[part, pl.ds(line, rows)]

                for low in range(top_chip):

                    @pl.when(chip == low)
                    def _():
                        other[...] = up_refs[low][...]

                for low in range(below_top):

                    @pl.when(chip == low + 1)
                    def _():
                        mine[...] = down_refs[low][...]

        for i, at in enumerate(range(span.start, span.stop)):
            low = (base_ref[i].astype(F32) + dot(in_ref[i], back_ref[at])).astype(BF16)
            high = (top_ref[i].astype(F32) + dot(in_ref[i], high_ref[at])).astype(BF16)

            @pl.when(core == 0)
            def _():
                keep_ref[i] = low
                send_ref[i] = high

            @pl.when(core == 1)
            def _():
                keep_ref[i] = high
                send_ref[i] = low

    def final(span, *refs):
        keep_ref, own_ref, recv_ref, sum_ref = refs[:4]
        lower_refs, upper_refs = refs[4:6], refs[6:8]
        solved_ref, image_ref, total_ref, sem = refs[-4:]
        _, core = place()
        at, width = span.start, wide(span)
        copies = []
        for side, source in ((core, keep_ref), (1 - core, recv_ref.at[pl.ds(0, width)])):
            copies.append(
                pltpu.make_async_copy(
                    source, solved_ref.at[pl.ds(side * half + at, width)], sem.at[len(copies)]
                )
            )
            copies[-1].start()

        def write(block_refs):
            for number, side in enumerate((core, 1 - core)):
                base = side * half + at
                for i in range(width):
                    halo = own_ref[i] if number == 0 else recv_ref[width + i]
                    total_ref[number * width + i] = sum_ref[base + i] + dot(
                        halo, block_refs[number][at + i]
                    )

        pl.when(core == 0)(lambda: write(lower_refs))
        pl.when(core == 1)(lambda: write(upper_refs))
        for number, side in enumerate((core, 1 - core)):
            copies.append(
                pltpu.make_async_copy(
                    total_ref.at[pl.ds(number * width, width)],
                    image_ref.at[pl.ds(side * half + at, width)],
                    sem.at[len(copies)],
                )
            )
            copies[-1].start()
        for copy in copies:
            copy.wait()

    spec = pl.BlockSpec(memory_space=pltpu.VMEM)
    anywhere = pl.BlockSpec(memory_space=pl.ANY)
    outputs = []
    for g, span in enumerate(spans):
        keep, own, send = call(
            functools.partial(finish, span),
            [message(span), message(span), ((2 * wide(span), rows, size), BF16)],
            heard_up[g]
            + heard_down[g]
            + [answers[1], echoes[g], tops[g], bases[g], backward, back_high],
            after=[far_sum],
            scratch=[pltpu.VMEM(*message(span))],
            products=2 * wide(span),
        )
        operands = [keep, own, swap_cores(send), far_sum]
        operands += [lower_own, lower_other, upper_own, upper_other]
        operands = [pltpu.with_memory_space_constraint(x, VMEM) for x in operands]
        outputs = pl.pallas_call(
            functools.partial(final, span),
            out_shape=[HBM(*every_vector), HBM(*every_sum)],
            in_specs=[spec] * len(operands) + [anywhere] * len(outputs),
            out_specs=[anywhere] * 2,
            input_output_aliases={len(operands) + i: i for i in range(len(outputs))},
            scratch_shapes=[
                pltpu.VMEM((2 * wide(span), rows, size), F32),
                pltpu.SemaphoreType.DMA((4,)),
            ],
            compiler_params=pltpu.CompilerParams(vmem_limit_bytes=2 << 20),
            cost_estimate=pl.CostEstimate(
                flops=4 * wide(span), bytes_accessed=1 << 10, transcendentals=0
            ),
        )(*operands, *outputs)
    preconditioned, image = outputs
    return (preconditioned.reshape(resid.shape), image.reshape(resid.shape))


def solution(mesh):
    spec = P("elev", "valley", "down", None, None)
    in_specs = (spec,) * 8 + (P("elev", "valley", "down"),)
    return jax.shard_map(
        local, mesh=mesh, in_specs=in_specs, out_specs=(spec, spec), check_vma=False
    )
```
